32 devices in a mesh: dp: 4 (over y, core), tensor: 8 (over z, x).
Axes of the slice: x: 2, y: 2, z: 4, core: 2. Of those that a mesh axis runs over, the one named last changes fastest.
Arguments:
- inputs: bfloat16 [8, 256, 1152], P('dp'), may hold values from -32 to 32
- out_grad: bfloat16 [8, 256, 1152], P('dp'), may hold values from -6 to 6
- bucket: int32 [4], P('dp'), may hold values from 0 to 7
- counts: int32 [4], replicated, may hold values from 1 to 8
- images_held: int32 [4], P('dp'), may hold values from 1 to 2, as said below
- owners: int32 [120], replicated, may hold values from 0 to 3, as said below
- master_weight: float32 [360, 192, 1152], P('dp', 'tensor'), may hold values from -0.23570226 to 0.23570226
- first_moment: float32 [360, 192, 1152], P('dp', 'tensor'), may hold values from -85.85453 to 85.85453
- second_moment: float32 [360, 192, 1152], P('dp', 'tensor'), may hold values from 81.9 to 7371
Outputs:
- block_output: bfloat16 [8, 256, 1152], P('dp')
- input_grad: float32 [8, 256, 1152], P('dp')
- new_first: float32 [360, 192, 1152], P('dp', 'tensor')
- new_second: float32 [360, 192, 1152], P('dp', 'tensor')
- new_master: float32 [360, 192, 1152], P('dp', 'tensor')
The draws below stay inside these ranges and needn't reach their ends.
Inputs may be any that keep to these rules, and one draw needn't show every extreme that they name: Slots 0 to images_held - 1 of a dp index hold its images, the others are empty; one dp index holds 2. `owners`: no dp index owns more than 90 blocks; one owns exactly 90.
All inputs are finite; a program needn't handle non-finite values.
Results may differ from the reference program's by a relative error of at most 0.022.
Values may be sent and summed in bfloat16 or wider, within the bound.
A program may use at most 256 MiB of HBM per device.

```python
import math
import jax
import jax.numpy as jnp
from jax import lax

D = 1152
HEADS = 16
HEAD_DIM = 72
FF = 4608
SEQ = 256
CAP = 2
NBUCKET = 8
STEP = 10
BR = 24
IMAGES = 8
ROWS_T = 2880
NBLK = 120
OWN_CAP = 90
N_DP = 4
N_TENSOR = 8


def owner_list(key):
    key = jax.random.fold_in(key, 7001)
    first, second, third = jax.random.split(key, 3)
    heavy = jax.random.randint(first, (), 0, N_DP)
    spare = jax.random.permutation(second, (N_DP - 1) * OWN_CAP)[:NBLK - OWN_CAP]
    relative = jnp.concatenate([jnp.zeros((OWN_CAP,), jnp.int32), 1 + (spare // OWN_CAP).astype(jnp.int32)])
    owners = (relative + heavy) % N_DP
    return owners[jax.random.permutation(third, NBLK)].astype(jnp.int32)


def kind_table(key, levels):
    owners = owner_list(key)
    block_ids = jnp.arange(NBLK, dtype=jnp.int32)
    earlier = (owners[None, :] == owners[:, None]) & (block_ids[None, :] < block_ids[:, None])
    slot_of = owners * OWN_CAP + jnp.sum(earlier.astype(jnp.int32), axis=1)
    owned = jnp.zeros((N_DP * OWN_CAP,), jnp.int32).at[slot_of].set(block_ids)
    inner = jnp.arange(N_TENSOR * BR, dtype=jnp.int32) % BR
    rows = owned[:, None] * BR + inner[None, :]
    head_cols = D // N_TENSOR
    ffn_cols = FF // N_TENSOR
    edges = [6 * head_cols, 9 * head_cols, 10 * head_cols, 11 * head_cols, 12 * head_cols, 12 * head_cols + ffn_cols]
    table = jnp.full(rows.shape, levels[0], jnp.float32)
    for edge, lower, upper in zip(edges, levels[:-1], levels[1:]):
        table = table + (upper - lower) * (rows >= edge).astype(jnp.float32)
    return table[:, :, None]


def grad_levels():
    typical = float(N_DP * CAP * SEQ * 2 // 5) ** 0.5
    return [0.8 * typical, 1.5 * typical, 0.5 * typical, 0.9 * typical, 0.55 * typical, 0.37 * typical, 0.8 * typical]


def draw_inputs(key, part):
    key = jax.random.fold_in(key, 31)
    first, second, third = jax.random.split(key, 3)
    base = jax.random.truncated_normal(first, -4.0, 4.0, (IMAGES, SEQ, D), jnp.float32)
    rows = jnp.exp(jax.random.uniform(second, (IMAGES, SEQ, 1), jnp.float32, math.log(0.5), math.log(2.0)))
    cols = jnp.exp(jax.random.uniform(third, (1, 1, D), jnp.float32, math.log(0.4), math.log(4.0)))
    return (base * rows * cols).astype(jnp.bfloat16)


def draw_images_held(key, part):
    key = jax.random.fold_in(key, 43)
    first, second = jax.random.split(key)
    heavy = jax.random.randint(first, (), 0, N_DP)
    held = jax.random.randint(second, (N_DP,), 1, CAP + 1)
    return jnp.where(jnp.arange(N_DP) == heavy, CAP, held).astype(jnp.int32)


def draw_owners(key, part):
    return owner_list(key)


def draw_master_weight(key, part):
    spread = kind_table(key, [2.0 / D ** 0.5, 1.0 / D ** 0.5, 1.0 / D ** 0.5, 1.0 / D ** 0.5, 2.0 / D ** 0.5, 1.0 / D ** 0.5, 1.0 / FF ** 0.5])
    key = jax.random.fold_in(key, 53)
    shape = (N_DP * OWN_CAP, N_TENSOR * BR, D)
    base = jax.random.truncated_normal(key, -4.0, 4.0, shape, jnp.float32)
    return base * spread


def draw_first_moment(key, part):
    size = kind_table(key, grad_levels())
    key = jax.random.fold_in(key, 61)
    first, second = jax.random.split(key)
    shape = (N_DP * OWN_CAP, N_TENSOR * BR, D)
    signs = jnp.where(jax.random.bernoulli(first, 0.5, shape), 1.0, -1.0)
    magnitude = jnp.exp(jax.random.uniform(second, shape, jnp.float32, math.log(0.5), math.log(2.0)))
    return signs * magnitude * size


def draw_second_moment(key, part):
    size = kind_table(key, grad_levels())
    key = jax.random.fold_in(key, 67)
    shape = (N_DP * OWN_CAP, N_TENSOR * BR, D)
    factor = jnp.exp(jax.random.uniform(key, shape, jnp.float32, 0.0, math.log(4.0)))
    return size * size * factor


def touch_ends(values, rng, low, largest):
    shape = values.shape
    index_at = [jax.random.randint(jax.random.fold_in(rng, axis), (), 0, shape[axis]) for axis in range(len(shape))]
    values = values.at[tuple(index_at)].set(low)
    longest = shape.index(max(shape))
    index_at[longest] = (index_at[longest] + 1) % shape[longest]
    return values.at[tuple(index_at)].set(largest)


def level_of(stream_key, extent, cuts, low, largest):
    gain, own = 1.0, jax.random.fold_in(stream_key, 6)
    for dim, shards_of in cuts:
        steps = jnp.exp(jax.random.uniform(jax.random.fold_in(own, dim), (shards_of,), jnp.float32, low / len(cuts), largest / len(cuts)))
        gain = gain * jnp.repeat(steps, extent[dim] // shards_of).reshape([-1 if axis == dim else 1 for axis in range(len(extent))])
    return gain


def normal_values(stream_key, dims, deviation, limit, cuts=(), kind=jnp.bfloat16):
    values = deviation * jax.random.normal(stream_key, dims, jnp.float32)
    if cuts:
        values = values * level_of(stream_key, dims, cuts, -0.22, 0.18)
    return jnp.clip(values, -limit, limit).astype(kind)


def setup_inputs(seed: int = 0) -> dict:
    keys = jax.random.split(jax.random.key(seed), 10)
    return {
        "inputs": draw_inputs(jax.random.fold_in(keys[9], 71), 0),
        "out_grad": normal_values(keys[1], (IMAGES, SEQ, D), 1.0, 6.0, ((0, 4),)),
        "bucket": touch_ends(jax.random.randint(keys[2], (N_DP,), 0, NBUCKET), jax.random.fold_in(keys[2], 1), 0, NBUCKET - 1).astype(jnp.int32),
        "counts": touch_ends(jax.random.randint(keys[3], (N_DP,), 1, 9), jax.random.fold_in(keys[3], 1), 1, 8).astype(jnp.int32),
        "images_held": draw_images_held(jax.random.fold_in(keys[9], 71), 0),
        "owners": draw_owners(jax.random.fold_in(keys[9], 71), 0),
        "master_weight": draw_master_weight(jax.random.fold_in(keys[9], 71), 0),
        "first_moment": draw_first_moment(jax.random.fold_in(keys[9], 71), 0),
        "second_moment": draw_second_moment(jax.random.fold_in(keys[9], 71), 0),
    }


@jax.custom_vjp
def low(v):
    return lax.optimization_barrier(v.astype(jnp.bfloat16)).astype(jnp.float32)

@jax.custom_vjp
def low_back(v):
    return v

def low_keep(v):
    return (low(v), None)

def low_pass(kept, grad):
    return (grad,)

def back_keep(v):
    return (v, None)

def back_low(kept, grad):
    return (low(grad),)
low.defvjp(low_keep, low_pass)
low_back.defvjp(back_keep, back_low)
HIGH = lax.Precision.HIGHEST
eps_norm = 1e-06
beta_one = 0.5
beta_two = 0.5
learn_rate = 0.03
decay_rate = 0.01
eps_adam = 1e-08

def time_token(bucket_value):
    half_width = D // 2
    freqs = jnp.exp(-math.log(10000.0) * jnp.arange(half_width, dtype=jnp.float32) / half_width)
    instant = (bucket_value.astype(jnp.float32) + 0.5) * (1000.0 / NBUCKET)
    angles = instant * freqs
    embed = jnp.concatenate([jnp.cos(angles), jnp.sin(angles)])
    return embed * jax.nn.sigmoid(embed)

def layer_norm(values):
    centred = values - lax.optimization_barrier(jnp.mean(values, axis=-1, keepdims=True))
    return centred * lax.rsqrt(lax.optimization_barrier(jnp.mean(centred * centred, axis=-1, keepdims=True)) + eps_norm)

def attend(block):
    queries, key_rows, values = block
    scores = low_back(jnp.einsum('bqhd,bkhd->bhqk', queries, key_rows, precision=HIGH) * HEAD_DIM ** (-0.5))
    soft = low(jax.nn.softmax(scores, axis=-1))
    return jnp.einsum('bhqk,bkhd->bqhd', soft, values, precision=HIGH)

def tensor_sum(acts, matrix):
    pieces = jnp.einsum('ntc,tcd->ntd', acts.reshape(acts.shape[0], N_TENSOR, -1), matrix.reshape(N_TENSOR, -1, D), precision=HIGH)
    return low_back(lax.optimization_barrier(jnp.sum(low(pieces), axis=1)))

def forward(params, inputs, token):
    w_mod, w_query, w_key, w_value, w_qtime, w_vtime, w_proj, w_up, w_down = params
    modulation = jnp.dot(w_mod, token, precision=HIGH, preferred_element_type=jnp.float32)
    shift_a, scale_a, gate_a, shift_m, scale_m, gate_m = jnp.split(modulation, 6)
    flat_rows = inputs.reshape(-1, D)
    mixed_a = low(layer_norm(flat_rows) * (1.0 + scale_a) + shift_a)
    queries = low_back(low(jnp.dot(mixed_a, w_query.T, precision=HIGH, preferred_element_type=jnp.float32) + jnp.dot(w_qtime, token, precision=HIGH, preferred_element_type=jnp.float32)))
    key_rows = low_back(low(jnp.dot(mixed_a, w_key.T, precision=HIGH, preferred_element_type=jnp.float32)))
    values = low_back(low(jnp.dot(mixed_a, w_value.T, precision=HIGH, preferred_element_type=jnp.float32) + jnp.dot(w_vtime, token, precision=HIGH, preferred_element_type=jnp.float32)))
    group_imgs = math.gcd(CAP, max(1, 512 // SEQ))
    block_shape = (CAP // group_imgs, group_imgs, SEQ, HEADS, HEAD_DIM)
    attended = lax.map(jax.checkpoint(attend), (queries.reshape(block_shape), key_rows.reshape(block_shape), values.reshape(block_shape)))
    heads_out = low_back(low(attended.reshape(-1, D)))
    resid = flat_rows + gate_a * tensor_sum(heads_out, w_proj)
    mixed_m = low(layer_norm(resid) * (1.0 + scale_m) + shift_m)
    hidden = low_back(jnp.dot(mixed_m, w_up.T, precision=HIGH, preferred_element_type=jnp.float32))
    acted = low(jax.nn.gelu(hidden, approximate=True))
    result = resid + gate_m * tensor_sum(acted, w_down)
    return result.reshape(inputs.shape)

def unpack(local):
    head_cols = D // N_TENSOR
    ffn_cols = FF // N_TENSOR
    edges = [0, 6 * head_cols, 7 * head_cols, 8 * head_cols, 9 * head_cols, 10 * head_cols, 11 * head_cols, 12 * head_cols, 12 * head_cols + ffn_cols, 12 * head_cols + 2 * ffn_cols]
    return tuple((local[:, lower:upper, :].reshape(-1, D) for lower, upper in zip(edges[:-1], edges[1:])))

def pack(grads):
    return jnp.concatenate([member.reshape(N_TENSOR, -1, D) for member in grads], axis=1)

def slot_table(owners):
    block_ids = jnp.arange(NBLK, dtype=jnp.int32)
    earlier = (owners[None, :] == owners[:, None]) & (block_ids[None, :] < block_ids[:, None])
    slot_of = (owners * OWN_CAP + lax.optimization_barrier(jnp.sum(earlier.astype(jnp.int32), axis=1))).astype(jnp.int32)
    owned = jnp.full((N_DP * OWN_CAP,), -1, jnp.int32).at[slot_of].set(block_ids)
    return (slot_of, owned)

def reference(inputs, out_grad, bucket, counts, images_held, owners, master_weight, first_moment, second_moment):
    slot_of, owned = slot_table(owners)
    rounded = master_weight.astype(jnp.bfloat16).astype(jnp.float32).reshape(N_DP * OWN_CAP, N_TENSOR, BR, D)
    local = jnp.transpose(rounded[slot_of], (1, 0, 2, 3)).reshape(N_TENSOR, ROWS_T, D)
    params = unpack(local)
    counts_f = counts.astype(jnp.float32)
    group_weight = counts_f * N_DP / jnp.sum(counts_f)
    images = inputs.astype(jnp.float32).reshape(N_DP, CAP, SEQ, D)
    cotangent = out_grad.astype(jnp.float32).reshape(N_DP, CAP, SEQ, D)
    live = (jnp.arange(CAP, dtype=jnp.int32)[None, :] < images_held[:, None]).astype(jnp.float32)

    def group(total, item):
        image, grad, bucket_value, scale, keep = item
        token = low(time_token(bucket_value))
        result, pullback = jax.vjp(lambda weights, values: forward(weights, values, token), params, image)
        mask = keep[:, None, None]
        dparams, dimage = pullback(grad * (scale * mask))
        total = tuple((left + right for left, right in zip(total, dparams)))
        return (total, (result * mask, dimage))
    zeros = tuple((jnp.zeros_like(member) for member in params))
    total, (outputs, dinputs) = lax.scan(group, zeros, (images, cotangent, bucket, group_weight, live))
    grad_blocks = pack(total).reshape(N_TENSOR, NBLK, BR, D)
    safe = jnp.maximum(owned, 0)
    reduced = jnp.transpose(grad_blocks[:, safe], (1, 0, 2, 3)).reshape(N_DP * OWN_CAP, N_TENSOR * BR, D)
    filled = (owned >= 0)[:, None, None]
    reduced = jnp.where(filled, reduced, 0.0)
    new_first = beta_one * first_moment + (1.0 - beta_one) * reduced
    new_second = beta_two * second_moment + (1.0 - beta_two) * reduced * reduced
    fix_one = 1.0 - beta_one ** STEP
    fix_two = 1.0 - beta_two ** STEP
    change = new_first / fix_one / (jnp.sqrt(new_second / fix_two) + eps_adam) + decay_rate * master_weight
    new_master = master_weight - learn_rate * change
    block_output = outputs.reshape(N_DP * CAP, SEQ, D).astype(jnp.bfloat16)
    input_grad = dinputs.reshape(N_DP * CAP, SEQ, D)
    return (block_output, input_grad, jnp.where(filled, new_first, 0.0), jnp.where(filled, new_second, 0.0), jnp.where(filled, new_master, 0.0))
```

```python
from functools import partial
import math
from types import SimpleNamespace

import jax
import jax.numpy as jnp
from jax import lax
from jax.experimental import pallas as pl
from jax.experimental.pallas import tpu as pltpu
from jax.sharding import PartitionSpec as P

D = 1152
HEADS = 16
HEAD_DIM = 72
FF = 4608
NBUCKET = 8
STEP = 10


eps_norm = 1e-06
beta_one = 0.5
beta_two = 0.5
learn_rate = 0.03
decay_rate = 0.01
eps_adam = 1e-08


def time_token(bucket_value):
    half_width = D // 2
    freqs = jnp.exp(-math.log(10000.0) * jnp.arange(half_width, dtype=jnp.float32) / half_width)
    instant = (bucket_value.astype(jnp.float32) + 0.5) * (1000.0 / NBUCKET)
    angles = instant * freqs
    embed = jnp.concatenate([jnp.cos(angles), jnp.sin(angles)])
    return embed * jax.nn.sigmoid(embed)


def norm_stats(values):
    centred = values - jnp.mean(values, axis=-1, keepdims=True)
    inverse = lax.rsqrt(jnp.mean(centred * centred, axis=-1, keepdims=True) + eps_norm)
    return (centred * inverse, inverse)


def norm_back(normed, inverse, upstream):
    return inverse * (
        upstream
        - jnp.mean(upstream, axis=-1, keepdims=True)
        - normed * jnp.mean(upstream * normed, axis=-1, keepdims=True)
    )


def times_transposed(left, right):
    return lax.dot_general(
        left, right, (((1,), (1,)), ((), ())), preferred_element_type=jnp.float32
    )


def transposed_times(left, right):
    return lax.dot_general(
        left, right, (((0,), (0,)), ((), ())), preferred_element_type=jnp.float32
    )


def attend_forward(block):
    queries, key_rows, values = block
    scores = jnp.einsum(
        "bqhd,bkhd->bhqk", queries, key_rows, preferred_element_type=jnp.float32
    ) * HEAD_DIM ** (-0.5)
    row_peak = jnp.max(scores, axis=-1, keepdims=True)
    exp_scores = jnp.exp(scores - row_peak)
    row_total = jnp.sum(exp_scores, axis=-1, keepdims=True)
    soft = (exp_scores / row_total).astype(jnp.bfloat16)
    attended = jnp.einsum("bhqk,bkhd->bqhd", soft, values, preferred_element_type=jnp.float32)
    return (attended, row_peak[..., 0] + jnp.log(row_total[..., 0]))


def attend_backward(block):
    queries, key_rows, values, log_total, upstream = block
    scale_factor = HEAD_DIM ** (-0.5)
    scores = (
        jnp.einsum("bqhd,bkhd->bhqk", queries, key_rows, preferred_element_type=jnp.float32)
        * scale_factor
    )
    soft = jnp.exp(scores - log_total[..., None])
    grad_soft = jnp.einsum("bqhd,bkhd->bhqk", upstream, values, preferred_element_type=jnp.float32)
    inner_sum = jnp.sum(soft * grad_soft, axis=-1, keepdims=True)
    grad_scores = (soft * (grad_soft - inner_sum)).astype(jnp.bfloat16)
    grad_query = (
        jnp.einsum("bhqk,bkhd->bqhd", grad_scores, key_rows, preferred_element_type=jnp.float32)
        * scale_factor
    )
    grad_key = (
        jnp.einsum("bhqk,bqhd->bkhd", grad_scores, queries, preferred_element_type=jnp.float32)
        * scale_factor
    )
    grad_value = jnp.einsum(
        "bhqk,bqhd->bkhd", soft.astype(jnp.bfloat16), upstream, preferred_element_type=jnp.float32
    )
    return (grad_query, grad_key, grad_value)


def per_device_plain(
    inputs,
    out_grad,
    bucket,
    counts,
    images_held,
    owners,
    master_weight,
    first_moment,
    second_moment,
):
    dp_count = lax.axis_size("dp")
    tensor_count = lax.axis_size("tensor")
    dp_rank = lax.axis_index("dp")
    tensor_rank = lax.axis_index("tensor")
    own_slots = master_weight.shape[0]
    block_rows = master_weight.shape[1]
    head_cols = D // tensor_count
    ffn_cols = FF // tensor_count
    local_heads = HEADS // tensor_count
    local_rows = 12 * head_cols + 2 * ffn_cols
    block_count = local_rows // block_rows
    image_count = inputs.shape[0]
    seq_len = inputs.shape[1]
    row_count = image_count * seq_len
    block_ids = jnp.arange(block_count, dtype=jnp.int32)
    earlier = (owners[None, :] == owners[:, None]) & (block_ids[None, :] < block_ids[:, None])
    slot_of = owners * own_slots + jnp.sum(earlier.astype(jnp.int32), axis=1)
    gathered = lax.all_gather(master_weight.astype(jnp.bfloat16), "dp", axis=0, tiled=True)
    weights = gathered[slot_of].reshape(local_rows, D)
    w_mod = weights[: 6 * head_cols]
    w_qkv = weights[6 * head_cols : 9 * head_cols]
    w_qtime = weights[9 * head_cols : 10 * head_cols]
    w_vtime = weights[10 * head_cols : 11 * head_cols]
    w_proj = weights[11 * head_cols : 12 * head_cols]
    w_up = weights[12 * head_cols : 12 * head_cols + ffn_cols]
    w_down = weights[12 * head_cols + ffn_cols :]
    token = time_token(bucket[0]).astype(jnp.bfloat16)
    token_wide = token.astype(jnp.float32)
    mod_piece = jnp.dot(w_mod, token, preferred_element_type=jnp.float32)
    modulation = lax.all_gather(mod_piece, "tensor", axis=0, tiled=True)
    shift_a, scale_a, gate_a, shift_m, scale_m, gate_m = jnp.split(modulation, 6)
    counts_f = counts.astype(jnp.float32)
    group_scale = counts_f[dp_rank] * dp_count / jnp.sum(counts_f)
    flat_rows = inputs.reshape(row_count, D).astype(jnp.float32)
    live = (jnp.arange(row_count, dtype=jnp.int32) // seq_len < images_held[0]).astype(jnp.float32)[
        :, None
    ]
    normed_a, inverse_a = norm_stats(flat_rows)
    mixed_a = (normed_a * (1.0 + scale_a) + shift_a).astype(jnp.bfloat16)
    projected = times_transposed(mixed_a, w_qkv)
    time_query = jnp.dot(w_qtime, token, preferred_element_type=jnp.float32)
    time_value = jnp.dot(w_vtime, token, preferred_element_type=jnp.float32)
    queries = (projected[:, :head_cols] + time_query).astype(jnp.bfloat16)
    key_rows = projected[:, head_cols : 2 * head_cols].astype(jnp.bfloat16)
    values = (projected[:, 2 * head_cols :] + time_value).astype(jnp.bfloat16)
    group_imgs = math.gcd(image_count, max(1, 512 // seq_len))
    block_shape = (image_count // group_imgs, group_imgs, seq_len, local_heads, HEAD_DIM)
    q_blocks = queries.reshape(block_shape)
    k_blocks = key_rows.reshape(block_shape)
    v_blocks = values.reshape(block_shape)
    attended, log_total = lax.map(attend_forward, (q_blocks, k_blocks, v_blocks))
    heads_out = attended.reshape(row_count, head_cols).astype(jnp.bfloat16)
    heads_share = lax.psum_scatter(
        jnp.dot(heads_out, w_proj, preferred_element_type=jnp.float32).astype(jnp.bfloat16),
        "tensor",
        scatter_dimension=0,
        tiled=True,
    ).astype(jnp.float32)
    branch_a = lax.all_gather(
        heads_share.astype(jnp.bfloat16), "tensor", axis=0, tiled=True
    ).astype(heads_share.dtype)
    resid = flat_rows + gate_a * branch_a
    normed_m, inverse_m = norm_stats(resid)
    mixed_m = (normed_m * (1.0 + scale_m) + shift_m).astype(jnp.bfloat16)
    hidden = times_transposed(mixed_m, w_up)
    acted = jax.nn.gelu(hidden, approximate=True).astype(jnp.bfloat16)
    hidden_share = lax.psum_scatter(
        jnp.dot(acted, w_down, preferred_element_type=jnp.float32).astype(jnp.bfloat16),
        "tensor",
        scatter_dimension=0,
        tiled=True,
    ).astype(jnp.float32)
    branch_m = lax.all_gather(
        hidden_share.astype(jnp.bfloat16), "tensor", axis=0, tiled=True
    ).astype(hidden_share.dtype)
    result = resid + gate_m * branch_m
    block_output = (result * live).astype(jnp.bfloat16).reshape(inputs.shape)
    grad_y = out_grad.reshape(row_count, D).astype(jnp.float32) * (group_scale * live)
    grad_branch_m = (gate_m * grad_y).astype(jnp.bfloat16)
    grad_gate_m = jnp.sum(grad_y * branch_m, axis=0)
    grad_acted = times_transposed(grad_branch_m, w_down)
    grad_down = transposed_times(acted, grad_branch_m)
    grad_hidden = jax.vjp(partial(jax.nn.gelu, approximate=True), hidden)[1](grad_acted)[0].astype(
        jnp.bfloat16
    )
    grad_up = transposed_times(grad_hidden, mixed_m)
    mlp_grad_share = lax.psum_scatter(
        jnp.dot(grad_hidden, w_up, preferred_element_type=jnp.float32).astype(jnp.bfloat16),
        "tensor",
        scatter_dimension=0,
        tiled=True,
    ).astype(jnp.float32)
    grad_mixed_m = lax.all_gather(
        mlp_grad_share.astype(jnp.bfloat16), "tensor", axis=0, tiled=True
    ).astype(mlp_grad_share.dtype)
    grad_shift_m = jnp.sum(grad_mixed_m, axis=0)
    grad_scale_m = jnp.sum(grad_mixed_m * normed_m, axis=0)
    grad_resid = grad_y + norm_back(normed_m, inverse_m, grad_mixed_m * (1.0 + scale_m))
    grad_branch_a = (gate_a * grad_resid).astype(jnp.bfloat16)
    grad_gate_a = jnp.sum(grad_resid * branch_a, axis=0)
    grad_heads = times_transposed(grad_branch_a, w_proj).astype(jnp.bfloat16)
    grad_proj = transposed_times(heads_out, grad_branch_a)
    grads_query, grads_key, grads_value = lax.map(
        attend_backward, (q_blocks, k_blocks, v_blocks, log_total, grad_heads.reshape(block_shape))
    )
    grad_qkv = jnp.concatenate(
        [
            grads_query.reshape(row_count, head_cols),
            grads_key.reshape(row_count, head_cols),
            grads_value.reshape(row_count, head_cols),
        ],
        axis=1,
    ).astype(jnp.bfloat16)
    grad_wqkv = transposed_times(grad_qkv, mixed_a)
    attn_grad_share = lax.psum_scatter(
        jnp.dot(grad_qkv, w_qkv, preferred_element_type=jnp.float32).astype(jnp.bfloat16),
        "tensor",
        scatter_dimension=0,
        tiled=True,
    ).astype(jnp.float32)
    grad_mixed_a = lax.all_gather(
        attn_grad_share.astype(jnp.bfloat16), "tensor", axis=0, tiled=True
    ).astype(attn_grad_share.dtype)
    token_sums = jnp.sum(grad_qkv, axis=0, dtype=jnp.float32)
    grad_qtime = token_sums[:head_cols, None] * token_wide[None, :]
    grad_vtime = token_sums[2 * head_cols :, None] * token_wide[None, :]
    grad_shift_a = jnp.sum(grad_mixed_a, axis=0)
    grad_scale_a = jnp.sum(grad_mixed_a * normed_a, axis=0)
    grad_in = grad_resid + norm_back(normed_a, inverse_a, grad_mixed_a * (1.0 + scale_a))
    grad_mod = jnp.concatenate(
        [grad_shift_a, grad_scale_a, grad_gate_a, grad_shift_m, grad_scale_m, grad_gate_m]
    )
    grad_mod_piece = lax.dynamic_slice_in_dim(grad_mod, tensor_rank * 6 * head_cols, 6 * head_cols)
    grad_wmod = grad_mod_piece[:, None] * token_wide[None, :]
    grads = jnp.concatenate(
        [grad_wmod, grad_wqkv, grad_qtime, grad_vtime, grad_proj, grad_up, grad_down], axis=0
    )
    grad_blocks = grads.reshape(block_count, block_rows, D)
    owned_blocks = jnp.full((dp_count * own_slots,), -1, jnp.int32).at[slot_of].set(block_ids)
    mine = lax.dynamic_slice_in_dim(owned_blocks, dp_rank * own_slots, own_slots)
    filled = (mine >= 0)[:, None, None]
    placed = (
        jnp.zeros((dp_count * own_slots, block_rows, D), jnp.float32).at[slot_of].set(grad_blocks)
    )
    reduced = lax.psum_scatter(
        placed.astype(jnp.bfloat16), "dp", scatter_dimension=0, tiled=True
    ).astype(jnp.float32)
    new_first = beta_one * first_moment + (1.0 - beta_one) * reduced
    new_second = beta_two * second_moment + (1.0 - beta_two) * reduced * reduced
    fix_one = 1.0 - beta_one**STEP
    fix_two = 1.0 - beta_two**STEP
    change = (
        new_first / fix_one / (jnp.sqrt(new_second / fix_two) + eps_adam)
        + decay_rate * master_weight
    )
    new_master = master_weight - learn_rate * change
    return (
        block_output,
        grad_in.reshape(inputs.shape),
        jnp.where(filled, new_first, 0.0),
        jnp.where(filled, new_second, 0.0),
        jnp.where(filled, new_master, 0.0),
    )


BF = jnp.bfloat16
F32 = jnp.float32
MESH = pl.DeviceIdType.MESH
TILE = 64
PAIR = 48
GELU_C = math.sqrt(2.0 / math.pi)
GELU_K = 0.044715


def rows_at(start, size):
    return pl.ds(pl.multiple_of(start, 16), size)


def remote(src, dst, send_sem, recv_sem, device):
    return pltpu.make_async_remote_copy(
        src_ref=src,
        dst_ref=dst,
        send_sem=send_sem,
        recv_sem=recv_sem,
        device_id=device,
        device_id_type=MESH,
    )


def times(left, right):
    return jnp.dot(left, right, preferred_element_type=F32)


class Sizes:
    def __init__(self, dp_count, tensor_count, slots, block_rows, images, seq):
        self.dp_count, self.tensor_count = dp_count, tensor_count
        self.slots, self.block_rows = slots, block_rows
        self.images, self.seq = images, seq
        self.rows = images * seq
        self.head_cols = D // tensor_count
        self.ffn_cols = FF // tensor_count
        self.heads = HEADS // tensor_count
        self.mod_rows = 6 * self.head_cols
        self.local_rows = 12 * self.head_cols + 2 * self.ffn_cols
        self.blocks = self.local_rows // block_rows
        self.wide = 4 * self.head_cols + 2 * self.ffn_cols
        self.thin = self.mod_rows + 2 * self.head_cols

    def fits(self):
        return (
            self.dp_count == 4
            and self.tensor_count == 8
            and 2 * self.block_rows == PAIR
            and self.rows == self.tensor_count * TILE
            and self.head_cols % PAIR == 0
            and self.ffn_cols % PAIR == 0
            and self.wide % (6 * PAIR) == 0
            and self.thin == D
            and self.mod_rows <= 1024
            and self.seq % 128 == 0
        )


def flatten(space):
    leaves = []
    for value in vars(space).values():
        leaves.extend(flatten(value) if isinstance(value, SimpleNamespace) else [value])
    return leaves


def rebuild(space, leaves):
    return SimpleNamespace(
        **{
            key: rebuild(value, leaves) if isinstance(value, SimpleNamespace) else next(leaves)
            for key, value in vars(space).items()
        }
    )


def scratch_plan(z):
    dma = pltpu.SemaphoreType.DMA
    vm = pltpu.VMEM
    half = z.wide // PAIR // 2

    def dp_sum():
        return SimpleNamespace(
            far=vm((half, PAIR, D), BF),
            fin=vm((z.wide, D), BF),
            s1=dma((half,)),
            r1=dma((half,)),
            s2=dma((half,)),
            r2=dma((half,)),
            s3=dma((half,)),
            r3=dma((half,)),
        )

    def hop_sems():
        return SimpleNamespace(xs=dma((4,)), xr=dma((4,)), zs=dma((3,)), zr=dma((3,)))

    def scatter():
        return SimpleNamespace(
            part=vm((z.rows, D), BF),
            xin=vm((4, TILE, D), BF),
            zout=vm((3, TILE, D), BF),
            zin=vm((3, TILE, D), BF),
            own=vm((TILE, D), F32),
            sem=hop_sems(),
        )

    def gather():
        return SimpleNamespace(buf=vm((z.rows, D), BF), sem=hop_sems())

    return SimpleNamespace(
        slot_table=pltpu.SMEM((z.blocks,), jnp.int32),
        master=vm((z.slots, z.block_rows, D), F32),
        master_sem=dma((3,)),
        placed=vm((z.local_rows, D), BF),
        tok_all=vm((16 * z.dp_count, D), BF),
        tok_s=dma((3,)),
        tok_r=dma((3,)),
        mod_prod=vm((16 * z.dp_count, D), F32),
        mod_pack=vm((z.dp_count, 16, 128), F32),
        mod_recv=vm((3, 16, 128), F32),
        mod_s=dma((3,)),
        mod_r=dma((3,)),
        mod_own=vm((16, 128), F32),
        mod_all=vm((z.tensor_count, 16, 128), F32),
        moda_s=dma((z.tensor_count - 1,)),
        moda_r=dma((z.tensor_count - 1,)),
        modv=vm((8, D), F32),
        time_qv=vm((8, 2 * 256), F32),
        u=vm((z.rows, D), BF),
        dmlp=vm((z.rows, D), BF),
        q=vm((z.rows, z.head_cols), BF),
        k=vm((z.rows, z.head_cols), BF),
        v=vm((z.rows, z.head_cols), BF),
        o=vm((z.rows, z.head_cols), BF),
        dq=vm((z.rows, z.head_cols), BF),
        dk=vm((z.rows, z.head_cols), BF),
        dv=vm((z.rows, z.head_cols), BF),
        soft=vm((z.images * z.heads, z.seq, z.seq), F32),
        dgact=vm((z.rows, z.ffn_cols), F32),
        gact=vm((z.rows, z.ffn_cols), BF),
        dz=vm((z.rows, z.ffn_cols), BF),
        h1=vm((TILE, D), F32),
        attn=vm((TILE, D), F32),
        dh1=vm((TILE, D), F32),
        dmod=vm((8, D), F32),
        dmod_pack=vm((z.tensor_count, 8, 128), F32),
        dmod_recv=vm((z.tensor_count - 1, 8, 128), F32),
        dmod_s=dma((z.tensor_count - 1,)),
        dmod_r=dma((z.tensor_count - 1,)),
        vec=vm((z.dp_count, 16, 256), F32),
        vec_s=dma((3,)),
        vec_r=dma((3,)),
        out_sem=dma((5,)),
        w=dp_sum(),
        g=dp_sum(),
        w_sib=vm((half, PAIR, D), BF),
        w_mrg=vm((half, PAIR, D), BF),
        rs1=scatter(),
        rs2=scatter(),
        rs3=scatter(),
        rs4=scatter(),
        ag1=gather(),
        ag2=gather(),
        ag3=gather(),
        ag4=gather(),
    )


def layer_kernel(z, plan, *refs):
    owners, counts, held, tok, x_ref, grad_ref, master_hbm = refs[:7]
    out_bo, out_ig, out_g, out_vec, out_tok = refs[7:12]
    s = rebuild(plan, iter(refs[12:]))
    s.w.src, s.w.sib, s.w.mrg = s.placed, s.w_sib, s.w_mrg
    s.g.src, s.g.sib, s.g.mrg = s.placed, s.w_sib, s.w_mrg
    nt_dims = (((1,), (1,)), ((), ()))
    tn_dims = (((0,), (0,)), ((), ()))

    def nt(left, right):
        return lax.dot_general(left, right, nt_dims, preferred_element_type=F32)

    def tn(left, right):
        return lax.dot_general(left, right, tn_dims, preferred_element_type=F32)

    hc, fc = z.head_cols, z.ffn_cols
    n_dp, n_t = z.dp_count, z.tensor_count
    dp, t = lax.axis_index("dp"), lax.axis_index("tensor")
    core = lax.rem(dp, 2)
    za, xb = t // 2, lax.rem(t, 2)
    sib = (dp + 1 - 2 * core, t)
    far = (lax.rem(dp + 2, 4), t)
    xp = (dp, t + 1 - 2 * xb)
    half = z.wide // PAIR // 2
    head_part = (4 * hc) // PAIR // 2
    pending = []

    def go(copy):
        copy.start()
        pending.append(copy)

    third = z.slots // 3
    loads = [
        pltpu.make_async_copy(
            master_hbm.at[pl.ds(i * third, third)],
            s.master.at[pl.ds(i * third, third)],
            s.master_sem.at[i],
        )
        for i in range(3)
    ]
    for load in loads:
        load.start()

    barrier = pltpu.get_barrier_semaphore()
    for i in range(1, n_dp):
        pl.semaphore_signal(
            barrier, inc=1, device_id=(lax.rem(dp + i, n_dp), t), device_id_type=MESH
        )
    for i in range(1, n_t):
        pl.semaphore_signal(
            barrier, inc=1, device_id=(dp, lax.rem(t + i, n_t)), device_id_type=MESH
        )
    pl.semaphore_wait(barrier, n_dp + n_t - 2)

    s.tok_all[rows_at(dp * 16, 16), :] = tok[...]

    def tok_copy(i, group):
        block = s.tok_all.at[rows_at(group * 16, 16)]
        return remote(
            block,
            block,
            s.tok_s.at[i - 1],
            s.tok_r.at[i - 1],
            (lax.rem(dp + i, n_dp), t),
        )

    for i in range(1, n_dp):
        go(tok_copy(i, dp))

    def note_slot(block, taken):
        mine = owners[block] == dp
        s.slot_table[block] = jnp.where(mine, taken, -1)
        return taken + mine.astype(jnp.int32)

    lax.fori_loop(0, z.blocks, note_slot, jnp.int32(0))
    for load in loads:
        load.wait()

    def place(lower, upper, shift):
        def one(pair, carry):
            halves = []
            for side in range(2):
                slot = s.slot_table[2 * (pair + shift) + side]
                block = s.master[jnp.clip(slot, 0, z.slots - 1)]
                halves.append(jnp.where(slot >= 0, block, 0.0))
            s.placed[rows_at(pair * PAIR, PAIR), :] = jnp.concatenate(halves, axis=0).astype(BF)
            return carry

        lax.fori_loop(lower, upper, one, 0)

    qkv_pairs, mod_pairs = 3 * hc // PAIR, z.mod_rows // PAIR
    time_pairs = 2 * hc // PAIR
    wide_pairs, all_pairs = z.wide // PAIR, z.local_rows // PAIR
    shift_qkv = mod_pairs
    shift_rest = mod_pairs + time_pairs

    def sum_step_one(ph, lower, upper):
        def one(i, carry):
            remote(
                ph.src.at[rows_at((2 * i + 1 - core) * PAIR, PAIR)],
                ph.sib.at[i],
                ph.s1.at[i],
                ph.r1.at[i],
                sib,
            ).start()
            return carry

        lax.fori_loop(lower, upper, one, 0)

    def sum_step_two(ph, lower, upper):
        def one(i, carry):
            remote(
                ph.src.at[rows_at((2 * i + 1 - core) * PAIR, PAIR)],
                ph.sib.at[i],
                ph.s1.at[i],
                ph.r1.at[i],
                sib,
            ).wait()
            mine = ph.src[rows_at((2 * i + core) * PAIR, PAIR), :].astype(F32)
            ph.mrg[i] = (mine + ph.sib[i].astype(F32)).astype(BF)
            remote(
                ph.mrg.at[i],
                ph.far.at[i],
                ph.s2.at[i],
                ph.r2.at[i],
                far,
            ).start()
            return carry

        lax.fori_loop(lower, upper, one, 0)

    def final_copy(ph, i, side):
        block = ph.fin.at[rows_at((2 * i + side) * PAIR, PAIR)]
        return remote(block, block, ph.s3.at[i], ph.r3.at[i], sib)

    def sum_step_three(ph, lower, upper):
        def one(i, carry):
            remote(
                ph.mrg.at[i],
                ph.far.at[i],
                ph.s2.at[i],
                ph.r2.at[i],
                far,
            ).wait()
            total = ph.mrg[i].astype(F32) + ph.far[i].astype(F32)
            ph.fin[rows_at((2 * i + core) * PAIR, PAIR), :] = total.astype(BF)
            final_copy(ph, i, core).start()
            return carry

        lax.fori_loop(lower, upper, one, 0)

    def sum_step_four(ph, lower, upper):
        def one(i, carry):
            final_copy(ph, i, core).wait_send()
            final_copy(ph, i, 1 - core).wait_recv()
            return carry

        lax.fori_loop(lower, upper, one, 0)

    place(0, qkv_pairs, shift_qkv)
    place(qkv_pairs, 2 * head_part, shift_rest)
    sum_step_one(s.w, 0, head_part)
    place(wide_pairs, wide_pairs + mod_pairs, -wide_pairs)
    place(wide_pairs + mod_pairs, all_pairs, -wide_pairs + qkv_pairs)

    for i in range(1, n_dp):
        tok_copy(i, lax.rem(dp - i + n_dp, n_dp)).wait_recv()
    for i in range(3):
        cols = D // 3
        s.mod_prod[:, i * cols : (i + 1) * cols] = nt(
            s.tok_all[...], s.placed[z.wide + i * cols : z.wide + (i + 1) * cols, :]
        )
    for group in range(n_dp):
        for i in range(D // 128):
            s.mod_pack[group, i : i + 1, :] = s.mod_prod[
                16 * group : 16 * group + 1, 128 * i : 128 * (i + 1)
            ]

    def mod_copy(i):
        group = lax.rem(dp + i, n_dp)
        return remote(
            s.mod_pack.at[group],
            s.mod_recv.at[i - 1],
            s.mod_s.at[i - 1],
            s.mod_r.at[i - 1],
            (group, t),
        )

    for i in range(1, n_dp):
        go(mod_copy(i))
    sum_step_two(s.w, 0, head_part)
    place(2 * head_part, wide_pairs, shift_rest)
    sum_step_one(s.w, head_part, half)
    for i in range(1, n_dp):
        mod_copy(i).wait_recv()
    s.mod_own[...] = (
        s.mod_pack[dp] + s.mod_recv[0] + s.mod_recv[1] + s.mod_recv[2]
    )
    s.mod_all[t] = s.mod_own[...]

    def mod_all_copy(i, member):
        block = s.mod_all.at[member, pl.ds(0, 8)]
        return remote(
            block,
            block,
            s.moda_s.at[i - 1],
            s.moda_r.at[i - 1],
            (dp, lax.rem(t + i, n_t)),
        )

    for i in range(1, n_t):
        go(mod_all_copy(i, t))
    sum_step_two(s.w, head_part, half)
    for i in range(1, n_t):
        mod_all_copy(i, lax.rem(t - i + n_t, n_t)).wait_recv()

    lane = lax.broadcasted_iota(jnp.int32, (8, D), 1)

    def spread(vector):
        return jnp.broadcast_to(vector, (8, D))

    def unpack_rows(block):
        return jnp.concatenate([block[i : i + 1, :] for i in range(block.shape[0])], axis=1)

    own_line = spread(unpack_rows(s.mod_own[0 : D // 128, :]))
    s.time_qv[:, 0:256] = pltpu.roll(own_line, D - z.mod_rows, 1)[:, 0:256]
    s.time_qv[:, 256:512] = pltpu.roll(own_line, D - z.mod_rows - hc, 1)[:, 0:256]
    lines = [jnp.zeros((8, D), F32) for _ in range(6)]
    for member in range(n_t):
        first = member * z.mod_rows
        line = jnp.concatenate(
            [s.mod_all[member, i : i + 1, :] for i in range(8)]
            + [jnp.zeros((1, D - 1024), F32)],
            axis=1,
        )
        line = spread(line)
        for piece in range(6):
            lower = max(first, piece * D) - piece * D
            upper = min(first + z.mod_rows, (piece + 1) * D) - piece * D
            if lower < upper:
                moved = pltpu.roll(line, (first - piece * D) % D, 1) if (first - piece * D) % D else line
                lines[piece] = jnp.where((lane >= lower) & (lane < upper), moved, lines[piece])
    for piece in range(6):
        s.modv[piece : piece + 1, :] = lines[piece][0:1, :]

    def mod_line(piece):
        return s.modv[piece : piece + 1, :]

    def norm_parts(values):
        centred = values - jnp.mean(values, axis=-1, keepdims=True)
        inverse = lax.rsqrt(jnp.mean(centred * centred, axis=-1, keepdims=True) + eps_norm)
        return centred * inverse, inverse

    count_sum = counts[0]
    for i in range(1, n_dp):
        count_sum = count_sum + counts[i]
    group_scale = jnp.full((1, 1), counts[dp], jnp.int32).astype(F32) * n_dp / jnp.full(
        (1, 1), count_sum, jnp.int32
    ).astype(F32)

    def live_of(image):
        return (jnp.full((1, 1), image, jnp.int32) < held[0]).astype(F32)

    def mix_tile(i, carry):
        at = rows_at(i * TILE, TILE)
        normed, _ = norm_parts(x_ref[at, :].astype(F32))
        s.u[at, :] = (normed * (1.0 + mod_line(1)) + mod_line(0)).astype(BF)
        dy = grad_ref[at, :].astype(F32) * (group_scale * live_of(i * TILE // z.seq))
        s.dmlp[at, :] = (mod_line(5) * dy).astype(BF)
        return carry

    lax.fori_loop(0, n_t, mix_tile, 0)

    sum_step_three(s.w, 0, head_part)
    sum_step_four(s.w, 0, head_part)
    w_fin = s.w.fin
    w_q, w_k, w_v, w_p = (w_fin.at[i * hc : (i + 1) * hc] for i in range(4))
    w_u = w_fin.at[4 * hc : 4 * hc + fc]
    w_d = w_fin.at[4 * hc + fc : 4 * hc + 2 * fc]

    head_of = lax.broadcasted_iota(jnp.int32, (1, hc), 1) // HEAD_DIM

    def only(values, head):
        return jnp.where(head_of == head, values, jnp.zeros_like(values))

    scale = HEAD_DIM ** (-0.5)
    time_q = s.time_qv[0:1, 0:hc]
    time_v = s.time_qv[0:1, 256 : 256 + hc]

    def attend(image, carry):
        at = rows_at(image * z.seq, z.seq)
        mixed = s.u[at, :]
        q = (nt(mixed, w_q[...]) + time_q).astype(BF)
        k = nt(mixed, w_k[...]).astype(BF)
        v = (nt(mixed, w_v[...]) + time_v).astype(BF)
        s.q[at, :] = q
        s.k[at, :] = k
        s.v[at, :] = v
        out = jnp.zeros((z.seq, hc), F32)
        for head in range(z.heads):
            scores = nt(only(q, head), k) * scale
            e = jnp.exp(scores - jnp.max(scores, axis=-1, keepdims=True))
            p = e / jnp.sum(e, axis=-1, keepdims=True)
            s.soft[image * z.heads + head] = p
            out = out + times(p.astype(BF), only(v, head))
        s.o[at, :] = out.astype(BF)
        s.rs1.part[at, :] = times(out.astype(BF), w_p[...]).astype(BF)
        return carry

    lax.fori_loop(0, z.images, attend, 0)

    def rs_x(ph, k):
        theirs = 2 * lax.rem(za + 1 + k, 4) + 1 - xb
        return remote(
            ph.part.at[rows_at(theirs * TILE, TILE)],
            ph.xin.at[k],
            ph.sem.xs.at[k],
            ph.sem.xr.at[k],
            xp,
        )

    def rs_z(ph, k):
        return remote(
            ph.zout.at[k],
            ph.zin.at[k],
            ph.sem.zs.at[k],
            ph.sem.zr.at[k],
            (dp, 2 * lax.rem(za + 1 + k, 4) + xb),
        )

    def rs_start(ph):
        for k in range(4):
            go(rs_x(ph, k))

    def rs_middle(ph):
        for k in range(4):
            rs_x(ph, k).wait_recv()
            mine = 2 * lax.rem(za + 1 + k, 4) + xb
            total = ph.part[rows_at(mine * TILE, TILE), :].astype(F32) + ph.xin[k].astype(F32)
            if k < 3:
                ph.zout[k] = total.astype(BF)
                go(rs_z(ph, k))
            else:
                ph.own[...] = total

    def rs_end(ph):
        total = ph.own[...]
        for k in range(3):
            rs_z(ph, k).wait_recv()
            total = total + ph.zin[k].astype(F32)
        return total

    def ag_z(ph, shard, k):
        block = ph.buf.at[rows_at(shard * TILE, TILE)]
        device = (dp, 2 * lax.rem(za + 1 + k, 4) + xb)
        return remote(block, block, ph.sem.zs.at[k], ph.sem.zr.at[k], device)

    def ag_x(ph, shard, k):
        block = ph.buf.at[rows_at(shard * TILE, TILE)]
        return remote(block, block, ph.sem.xs.at[k], ph.sem.xr.at[k], xp)

    def ag_start(ph, value):
        ph.buf[rows_at(t * TILE, TILE), :] = value
        for k in range(3):
            go(ag_z(ph, t, k))
        go(ag_x(ph, t, 0))

    def ag_middle(ph):
        for k in range(3):
            origin = lax.rem(za + 3 - k, 4)
            ag_z(ph, 2 * origin + xb, k).wait_recv()
            go(ag_x(ph, 2 * origin + xb, k + 1))

    def ag_end(ph):
        for k in range(4):
            origin = lax.rem(za + 4 - k, 4)
            ag_x(ph, 2 * origin + 1 - xb, k).wait_recv()

    rs_start(s.rs1)
    rs_middle(s.rs1)

    mine_at = rows_at(t * TILE, TILE)
    live = live_of(t * TILE // z.seq)
    attn = rs_end(s.rs1)
    s.attn[...] = attn
    h1 = x_ref[mine_at, :].astype(F32) + mod_line(2) * attn
    s.h1[...] = h1
    normed_m, _ = norm_parts(h1)
    ag_start(s.ag1, (normed_m * (1.0 + mod_line(4)) + mod_line(3)).astype(BF))
    sum_step_three(s.w, head_part, half)
    ag_middle(s.ag1)
    sum_step_four(s.w, head_part, half)

    step_rows = 128

    def up_tile(i, carry):
        at = rows_at(i * step_rows, step_rows)
        s.dgact[at, :] = nt(s.dmlp[at, :], w_d[...])
        return carry

    lax.fori_loop(0, z.rows // step_rows, up_tile, 0)
    ag_end(s.ag1)

    def mlp_tile(i, carry):
        at = rows_at(i * step_rows, step_rows)
        hidden = nt(s.ag1.buf[at, :], w_u[...])
        square = hidden * hidden
        bend = jnp.tanh(GELU_C * hidden * (1.0 + GELU_K * square))
        s.gact[at, :] = (0.5 * hidden * (1.0 + bend)).astype(BF)
        slope = 0.5 * (1.0 + bend) + 0.5 * hidden * (1.0 - bend * bend) * (
            GELU_C * (1.0 + 3.0 * GELU_K * square)
        )
        dz = (s.dgact[at, :] * slope).astype(BF)
        s.dz[at, :] = dz
        s.rs2.part[at, :] = times(dz, w_u[...]).astype(BF)
        return carry

    lax.fori_loop(0, z.rows // step_rows, mlp_tile, 0)
    rs_start(s.rs2)
    rs_middle(s.rs2)

    cols = 384

    def grad_tile(i, carry):
        at = pl.ds(pl.multiple_of(i * cols, 128), cols)
        s.g.src[4 * hc : 4 * hc + fc, at] = tn(s.dz[...], s.ag1.buf[:, at]).astype(BF)
        s.g.src[4 * hc + fc : z.wide, at] = tn(s.gact[...], s.dmlp[:, at]).astype(BF)
        return carry

    lax.fori_loop(0, D // cols, grad_tile, 0)
    sum_step_one(s.g, head_part, half)

    def down_tile(i, carry):
        at = rows_at(i * step_rows, step_rows)
        s.rs4.part[at, :] = times(s.gact[at, :], w_d[...]).astype(BF)
        return carry

    lax.fori_loop(0, z.rows // step_rows, down_tile, 0)

    def norm_back_of(normed, inverse, upstream):
        return inverse * (
            upstream
            - jnp.mean(upstream, axis=-1, keepdims=True)
            - normed * jnp.mean(upstream * normed, axis=-1, keepdims=True)
        )

    def column_sum(values):
        return jnp.sum(values, axis=0, keepdims=True)

    dw = rs_end(s.rs2)
    dy_mine = grad_ref[mine_at, :].astype(F32) * (group_scale * live)
    normed_m, inverse_m = norm_parts(s.h1[...])
    dh1 = dy_mine + norm_back_of(normed_m, inverse_m, dw * (1.0 + mod_line(4)))
    ag_start(s.ag2, (mod_line(2) * dh1).astype(BF))
    s.dh1[...] = dh1
    s.dmod[2:3, :] = column_sum(dh1 * s.attn[...])
    s.dmod[3:4, :] = column_sum(dw)
    s.dmod[4:5, :] = column_sum(dw * normed_m)
    sum_step_two(s.g, head_part, half)
    ag_middle(s.ag2)
    ag_end(s.ag2)
    rs_start(s.rs4)

    def attend_back(image, carry):
        at = rows_at(image * z.seq, z.seq)
        do = nt(s.ag2.buf[at, :], w_p[...]).astype(BF)
        q, k, v = s.q[at, :], s.k[at, :], s.v[at, :]
        dq = jnp.zeros((z.seq, hc), F32)
        dk = jnp.zeros((z.seq, hc), F32)
        dv = jnp.zeros((z.seq, hc), F32)
        for head in range(z.heads):
            p = s.soft[image * z.heads + head]
            do_head = only(do, head)
            dp_soft = nt(do_head, v)
            inner = jnp.sum(p * dp_soft, axis=-1, keepdims=True)
            ds = (p * (dp_soft - inner)).astype(BF)
            dq = dq + times(ds, only(k, head))
            dk = dk + tn(ds, only(q, head))
            dv = dv + tn(p.astype(BF), do_head)
        dq = (dq * scale).astype(BF)
        dk = (dk * scale).astype(BF)
        dv = dv.astype(BF)
        s.dq[at, :] = dq
        s.dk[at, :] = dk
        s.dv[at, :] = dv
        s.rs3.part[at, :] = (
            times(dq, w_q[...]) + times(dk, w_k[...]) + times(dv, w_v[...])
        ).astype(BF)
        return carry

    lax.fori_loop(0, z.images, attend_back, 0)
    rs_start(s.rs3)
    rs_middle(s.rs4)

    def attn_grad_tile(i, carry):
        at = pl.ds(pl.multiple_of(i * cols, 128), cols)
        mixed = s.u[:, at]
        s.g.src[0:hc, at] = tn(s.dq[...], mixed).astype(BF)
        s.g.src[hc : 2 * hc, at] = tn(s.dk[...], mixed).astype(BF)
        s.g.src[2 * hc : 3 * hc, at] = tn(s.dv[...], mixed).astype(BF)
        s.g.src[3 * hc : 4 * hc, at] = tn(s.o[...], s.ag2.buf[:, at]).astype(BF)
        return carry

    lax.fori_loop(0, D // cols, attn_grad_tile, 0)
    sum_step_one(s.g, 0, head_part)
    rs_middle(s.rs3)
    s.vec[dp] = jnp.zeros((16, 256), F32)
    s.vec[dp, 8:9, 0:hc] = column_sum(s.dq[...].astype(F32))
    s.vec[dp, 9:10, 0:hc] = column_sum(s.dv[...].astype(F32))
    sum_step_two(s.g, 0, head_part)

    mlp = rs_end(s.rs4)
    s.dmod[5:6, :] = column_sum(dy_mine * mlp)
    ag_start(s.ag4, ((s.h1[...] + mod_line(5) * mlp) * live).astype(BF))
    sum_step_three(s.g, head_part, half)
    ag_middle(s.ag4)

    du = rs_end(s.rs3)
    normed_a, inverse_a = norm_parts(x_ref[mine_at, :].astype(F32))
    ag_start(
        s.ag3,
        (s.dh1[...] + norm_back_of(normed_a, inverse_a, du * (1.0 + mod_line(1)))).astype(BF),
    )
    s.dmod[0:1, :] = column_sum(du)
    s.dmod[1:2, :] = column_sum(du * normed_a)
    s.dmod[6:8, :] = jnp.zeros((2, D), F32)

    dlines = [spread(s.dmod[i : i + 1, :]) for i in range(6)]
    for member in range(n_t):
        first = member * z.mod_rows
        line = jnp.zeros((8, D), F32)
        for piece in range(6):
            lower = max(first, piece * D) - first
            upper = min(first + z.mod_rows, (piece + 1) * D) - first
            if lower < upper:
                back = (piece * D - first) % D
                moved = pltpu.roll(dlines[piece], back, 1) if back else dlines[piece]
                line = jnp.where((lane >= lower) & (lane < upper), moved, line)
        for i in range(8):
            s.dmod_pack[member, i : i + 1, :] = line[0:1, 128 * i : 128 * (i + 1)]

    def dmod_copy(i):
        member = lax.rem(t + i, n_t)
        return remote(
            s.dmod_pack.at[member],
            s.dmod_recv.at[i - 1],
            s.dmod_s.at[i - 1],
            s.dmod_r.at[i - 1],
            (dp, member),
        )

    for i in range(1, n_t):
        go(dmod_copy(i))
    ag_middle(s.ag3)
    sum_step_three(s.g, 0, head_part)
    total = s.dmod_pack[t]
    for i in range(1, n_t):
        dmod_copy(i).wait_recv()
        total = total + s.dmod_recv[i - 1]
    s.vec[dp, 0:8, 0:128] = total

    def vec_copy(i, group):
        return remote(
            s.vec.at[group],
            s.vec.at[group],
            s.vec_s.at[i - 1],
            s.vec_r.at[i - 1],
            (lax.rem(dp + i, n_dp), t),
        )

    for i in range(1, n_dp):
        go(vec_copy(i, dp))
    sum_step_four(s.g, 0, half)
    ag_end(s.ag4)
    ag_end(s.ag3)
    for i in range(1, n_dp):
        vec_copy(i, lax.rem(dp - i + n_dp, n_dp)).wait_recv()
    for copy in pending:
        copy.wait_send()

    outs = (
        (s.ag4.buf, out_bo),
        (s.ag3.buf, out_ig),
        (s.g.fin, out_g),
        (s.vec, out_vec),
        (s.tok_all, out_tok),
    )
    stores = [
        pltpu.make_async_copy(src, dst, s.out_sem.at[i]) for i, (src, dst) in enumerate(outs)
    ]
    for store in stores:
        store.start()
    for store in stores:
        store.wait()


def update_kernel(z, group_slots, owners, grads, table, tokens, master, first, second, new_first, new_second, new_master, bos):
    step = pl.program_id(0)
    dp = lax.axis_index("dp")

    @pl.when(step == 0)
    def _():
        def clear(slot, carry):
            bos[slot] = -1
            return carry

        lax.fori_loop(0, z.slots, clear, 0)

        def note(block, taken):
            mine = owners[block] == dp

            @pl.when(mine & (taken < z.slots))
            def _():
                bos[taken] = block

            return taken + mine.astype(jnp.int32)

        lax.fori_loop(0, z.blocks, note, jnp.int32(0))

    rows = z.block_rows
    mod_blocks = z.mod_rows // rows
    head_blocks = z.head_cols // rows
    fix_one = 1.0 - beta_one**STEP
    fix_two = 1.0 - beta_two**STEP

    def put(i, grad):
        weight = master[i]
        one = beta_one * first[i] + (1.0 - beta_one) * grad
        two = beta_two * second[i] + (1.0 - beta_two) * grad * grad
        new_first[i] = one
        new_second[i] = two
        change = one / fix_one / (jnp.sqrt(two / fix_two) + eps_adam) + decay_rate * weight
        new_master[i] = weight - learn_rate * change

    def slot(i, carry):
        block = bos[step * group_slots + i]
        is_mod = block < mod_blocks
        is_time = (block >= mod_blocks + 3 * head_blocks) & (block < mod_blocks + 5 * head_blocks)

        @pl.when(block < 0)
        def _():
            new_first[i] = jnp.zeros((rows, D), F32)
            new_second[i] = jnp.zeros((rows, D), F32)
            new_master[i] = jnp.zeros((rows, D), F32)

        @pl.when((block >= 0) & (is_mod | is_time))
        def _():
            index = jnp.where(is_mod, block, block - 3 * head_blocks)
            columns = table[index]
            grad = columns[:, 0:1] * tokens[0:1, :].astype(F32)
            for group in range(1, z.dp_count):
                grad = grad + columns[:, group : group + 1] * tokens[
                    16 * group : 16 * group + 1, :
                ].astype(F32)
            put(i, grad)

        @pl.when((block >= 0) & jnp.logical_not(is_mod | is_time))
        def _():
            index = jnp.where(
                block < mod_blocks + 3 * head_blocks,
                block - mod_blocks,
                block - mod_blocks - 2 * head_blocks,
            )
            both = grads[rows_at(index // 2 * PAIR, PAIR), :].astype(F32)
            put(i, jnp.where(lax.rem(index, 2) == 0, both[:rows], both[rows:]))

        return carry

    lax.fori_loop(0, group_slots, slot, 0)


def per_device_fast(
    z,
    inputs,
    out_grad,
    bucket,
    counts,
    images_held,
    owners,
    master_weight,
    first_moment,
    second_moment,
):
    token = jnp.broadcast_to(time_token(bucket[0]).astype(BF)[None, :], (16, D))
    plan = scratch_plan(z)
    smem = pl.BlockSpec(memory_space=pltpu.SMEM)
    vmem = pl.BlockSpec(memory_space=pltpu.VMEM)
    hbm = pl.BlockSpec(memory_space=pl.ANY)
    flops = 6 * z.rows * D * z.wide
    block_output, input_grad, grads, vectors, tokens = pl.pallas_call(
        partial(layer_kernel, z, plan),
        out_shape=(
            jax.ShapeDtypeStruct((z.rows, D), BF),
            jax.ShapeDtypeStruct((z.rows, D), BF),
            jax.ShapeDtypeStruct((z.wide, D), BF),
            jax.ShapeDtypeStruct((z.dp_count, 16, 256), F32),
            jax.ShapeDtypeStruct((16 * z.dp_count, D), BF),
        ),
        in_specs=[smem, smem, smem, vmem, vmem, vmem, hbm],
        out_specs=(hbm,) * 5,
        scratch_shapes=flatten(plan),
        compiler_params=pltpu.CompilerParams(
            collective_id=0, has_side_effects=True, vmem_limit_bytes=62 * 2**20
        ),
        cost_estimate=pl.CostEstimate(
            flops=flops, bytes_accessed=20 * 2**20, transcendentals=z.rows * z.ffn_cols
        ),
        name="layer",
    )(
        owners,
        counts,
        images_held,
        token,
        inputs.reshape(z.rows, D),
        out_grad.reshape(z.rows, D),
        master_weight,
    )
    columns = jnp.concatenate(
        [
            vectors[:, :8, :128].reshape(z.dp_count, 1024)[:, : z.mod_rows],
            vectors[:, 8, : z.head_cols],
            vectors[:, 9, : z.head_cols],
        ],
        axis=1,
    ).T.reshape(z.thin // z.block_rows, z.block_rows, z.dp_count)
    group_slots = next(size for size in (6, 5, 4, 3, 2, 1) if z.slots % size == 0)
    block = pl.BlockSpec((group_slots, z.block_rows, D), lambda i: (i, 0, 0))
    state = jax.ShapeDtypeStruct(master_weight.shape, F32)
    new_first, new_second, new_master = pl.pallas_call(
        partial(update_kernel, z, group_slots),
        grid=(z.slots // group_slots,),
        out_shape=(state,) * 3,
        in_specs=[smem, vmem, vmem, vmem, block, block, block],
        out_specs=(block,) * 3,
        scratch_shapes=[pltpu.SMEM((z.slots,), jnp.int32)],
        compiler_params=pltpu.CompilerParams(vmem_limit_bytes=48 * 2**20),
        name="update",
    )(owners, grads, columns, tokens, master_weight, first_moment, second_moment)
    return (
        block_output.reshape(inputs.shape),
        input_grad.astype(F32).reshape(inputs.shape),
        new_first,
        new_second,
        new_master,
    )


def per_device(inputs, out_grad, bucket, counts, images_held, owners, master, first, second):
    sizes = Sizes(
        lax.axis_size("dp"),
        lax.axis_size("tensor"),
        master.shape[0],
        master.shape[1],
        inputs.shape[0],
        inputs.shape[1],
    )
    run = partial(per_device_fast, sizes) if sizes.fits() else per_device_plain
    return run(inputs, out_grad, bucket, counts, images_held, owners, master, first, second)


def solution(mesh):
    return jax.shard_map(
        per_device,
        mesh=mesh,
        in_specs=(
            P("dp", None, None),
            P("dp", None, None),
            P("dp"),
            P(),
            P("dp"),
            P(),
            P("dp", "tensor", None),
            P("dp", "tensor", None),
            P("dp", "tensor", None),
        ),
        out_specs=(
            P("dp", None, None),
            P("dp", None, None),
            P("dp", "tensor", None),
            P("dp", "tensor", None),
            P("dp", "tensor", None),
        ),
        check_vma=False,
    )
```

```python
from functools import partial
import math
from types import SimpleNamespace

import jax
import jax.numpy as jnp
from jax import lax
from jax.experimental import pallas as pl
from jax.experimental.pallas import tpu as pltpu
from jax.sharding import PartitionSpec as P

D = 1152
HEADS = 16
HEAD_DIM = 72
FF = 4608
NBUCKET = 8
STEP = 10


eps_norm = 1e-06
beta_one = 0.5
beta_two = 0.5
learn_rate = 0.03
decay_rate = 0.01
eps_adam = 1e-08


def time_token(bucket_value):
    half_width = D // 2
    freqs = jnp.exp(-math.log(10000.0) * jnp.arange(half_width, dtype=jnp.float32) / half_width)
    instant = (bucket_value.astype(jnp.float32) + 0.5) * (1000.0 / NBUCKET)
    angles = instant * freqs
    embed = jnp.concatenate([jnp.cos(angles), jnp.sin(angles)])
    return embed * jax.nn.sigmoid(embed)


def norm_stats(values):
    centred = values - jnp.mean(values, axis=-1, keepdims=True)
    inverse = lax.rsqrt(jnp.mean(centred * centred, axis=-1, keepdims=True) + eps_norm)
    return (centred * inverse, inverse)


def norm_back(normed, inverse, upstream):
    return inverse * (
        upstream
        - jnp.mean(upstream, axis=-1, keepdims=True)
        - normed * jnp.mean(upstream * normed, axis=-1, keepdims=True)
    )


def times_transposed(left, right):
    return lax.dot_general(
        left, right, (((1,), (1,)), ((), ())), preferred_element_type=jnp.float32
    )


def transposed_times(left, right):
    return lax.dot_general(
        left, right, (((0,), (0,)), ((), ())), preferred_element_type=jnp.float32
    )


def attend_forward(block):
    queries, key_rows, values = block
    scores = jnp.einsum(
        "bqhd,bkhd->bhqk", queries, key_rows, preferred_element_type=jnp.float32
    ) * HEAD_DIM ** (-0.5)
    row_peak = jnp.max(scores, axis=-1, keepdims=True)
    exp_scores = jnp.exp(scores - row_peak)
    row_total = jnp.sum(exp_scores, axis=-1, keepdims=True)
    soft = (exp_scores / row_total).astype(jnp.bfloat16)
    attended = jnp.einsum("bhqk,bkhd->bqhd", soft, values, preferred_element_type=jnp.float32)
    return (attended, row_peak[..., 0] + jnp.log(row_total[..., 0]))


def attend_backward(block):
    queries, key_rows, values, log_total, upstream = block
    scale_factor = HEAD_DIM ** (-0.5)
    scores = (
        jnp.einsum("bqhd,bkhd->bhqk", queries, key_rows, preferred_element_type=jnp.float32)
        * scale_factor
    )
    soft = jnp.exp(scores - log_total[..., None])
    grad_soft = jnp.einsum("bqhd,bkhd->bhqk", upstream, values, preferred_element_type=jnp.float32)
    inner_sum = jnp.sum(soft * grad_soft, axis=-1, keepdims=True)
    grad_scores = (soft * (grad_soft - inner_sum)).astype(jnp.bfloat16)
    grad_query = (
        jnp.einsum("bhqk,bkhd->bqhd", grad_scores, key_rows, preferred_element_type=jnp.float32)
        * scale_factor
    )
    grad_key = (
        jnp.einsum("bhqk,bqhd->bkhd", grad_scores, queries, preferred_element_type=jnp.float32)
        * scale_factor
    )
    grad_value = jnp.einsum(
        "bhqk,bqhd->bkhd", soft.astype(jnp.bfloat16), upstream, preferred_element_type=jnp.float32
    )
    return (grad_query, grad_key, grad_value)


def per_device_plain(
    inputs,
    out_grad,
    bucket,
    counts,
    images_held,
    owners,
    master_weight,
    first_moment,
    second_moment,
):
    dp_count = lax.axis_size("dp")
    tensor_count = lax.axis_size("tensor")
    dp_rank = lax.axis_index("dp")
    tensor_rank = lax.axis_index("tensor")
    own_slots = master_weight.shape[0]
    block_rows = master_weight.shape[1]
    head_cols = D // tensor_count
    ffn_cols = FF // tensor_count
    local_heads = HEADS // tensor_count
    local_rows = 12 * head_cols + 2 * ffn_cols
    block_count = local_rows // block_rows
    image_count = inputs.shape[0]
    seq_len = inputs.shape[1]
    row_count = image_count * seq_len
    block_ids = jnp.arange(block_count, dtype=jnp.int32)
    earlier = (owners[None, :] == owners[:, None]) & (block_ids[None, :] < block_ids[:, None])
    slot_of = owners * own_slots + jnp.sum(earlier.astype(jnp.int32), axis=1)
    gathered = lax.all_gather(master_weight.astype(jnp.bfloat16), "dp", axis=0, tiled=True)
    weights = gathered[slot_of].reshape(local_rows, D)
    w_mod = weights[: 6 * head_cols]
    w_qkv = weights[6 * head_cols : 9 * head_cols]
    w_qtime = weights[9 * head_cols : 10 * head_cols]
    w_vtime = weights[10 * head_cols : 11 * head_cols]
    w_proj = weights[11 * head_cols : 12 * head_cols]
    w_up = weights[12 * head_cols : 12 * head_cols + ffn_cols]
    w_down = weights[12 * head_cols + ffn_cols :]
    token = time_token(bucket[0]).astype(jnp.bfloat16)
    token_wide = token.astype(jnp.float32)
    mod_piece = jnp.dot(w_mod, token, preferred_element_type=jnp.float32)
    modulation = lax.all_gather(mod_piece, "tensor", axis=0, tiled=True)
    shift_a, scale_a, gate_a, shift_m, scale_m, gate_m = jnp.split(modulation, 6)
    counts_f = counts.astype(jnp.float32)
    group_scale = counts_f[dp_rank] * dp_count / jnp.sum(counts_f)
    flat_rows = inputs.reshape(row_count, D).astype(jnp.float32)
    live = (jnp.arange(row_count, dtype=jnp.int32) // seq_len < images_held[0]).astype(jnp.float32)[
        :, None
    ]
    normed_a, inverse_a = norm_stats(flat_rows)
    mixed_a = (normed_a * (1.0 + scale_a) + shift_a).astype(jnp.bfloat16)
    projected = times_transposed(mixed_a, w_qkv)
    time_query = jnp.dot(w_qtime, token, preferred_element_type=jnp.float32)
    time_value = jnp.dot(w_vtime, token, preferred_element_type=jnp.float32)
    queries = (projected[:, :head_cols] + time_query).astype(jnp.bfloat16)
    key_rows = projected[:, head_cols : 2 * head_cols].astype(jnp.bfloat16)
    values = (projected[:, 2 * head_cols :] + time_value).astype(jnp.bfloat16)
    group_imgs = math.gcd(image_count, max(1, 512 // seq_len))
    block_shape = (image_count // group_imgs, group_imgs, seq_len, local_heads, HEAD_DIM)
    q_blocks = queries.reshape(block_shape)
    k_blocks = key_rows.reshape(block_shape)
    v_blocks = values.reshape(block_shape)
    attended, log_total = lax.map(attend_forward, (q_blocks, k_blocks, v_blocks))
    heads_out = attended.reshape(row_count, head_cols).astype(jnp.bfloat16)
    heads_share = lax.psum_scatter(
        jnp.dot(heads_out, w_proj, preferred_element_type=jnp.float32).astype(jnp.bfloat16),
        "tensor",
        scatter_dimension=0,
        tiled=True,
    ).astype(jnp.float32)
    branch_a = lax.all_gather(
        heads_share.astype(jnp.bfloat16), "tensor", axis=0, tiled=True
    ).astype(heads_share.dtype)
    resid = flat_rows + gate_a * branch_a
    normed_m, inverse_m = norm_stats(resid)
    mixed_m = (normed_m * (1.0 + scale_m) + shift_m).astype(jnp.bfloat16)
    hidden = times_transposed(mixed_m, w_up)
    acted = jax.nn.gelu(hidden, approximate=True).astype(jnp.bfloat16)
    hidden_share = lax.psum_scatter(
        jnp.dot(acted, w_down, preferred_element_type=jnp.float32).astype(jnp.bfloat16),
        "tensor",
        scatter_dimension=0,
        tiled=True,
    ).astype(jnp.float32)
    branch_m = lax.all_gather(
        hidden_share.astype(jnp.bfloat16), "tensor", axis=0, tiled=True
    ).astype(hidden_share.dtype)
    result = resid + gate_m * branch_m
    block_output = (result * live).astype(jnp.bfloat16).reshape(inputs.shape)
    grad_y = out_grad.reshape(row_count, D).astype(jnp.float32) * (group_scale * live)
    grad_branch_m = (gate_m * grad_y).astype(jnp.bfloat16)
    grad_gate_m = jnp.sum(grad_y * branch_m, axis=0)
    grad_acted = times_transposed(grad_branch_m, w_down)
    grad_down = transposed_times(acted, grad_branch_m)
    grad_hidden = jax.vjp(partial(jax.nn.gelu, approximate=True), hidden)[1](grad_acted)[0].astype(
        jnp.bfloat16
    )
    grad_up = transposed_times(grad_hidden, mixed_m)
    mlp_grad_share = lax.psum_scatter(
        jnp.dot(grad_hidden, w_up, preferred_element_type=jnp.float32).astype(jnp.bfloat16),
        "tensor",
        scatter_dimension=0,
        tiled=True,
    ).astype(jnp.float32)
    grad_mixed_m = lax.all_gather(
        mlp_grad_share.astype(jnp.bfloat16), "tensor", axis=0, tiled=True
    ).astype(mlp_grad_share.dtype)
    grad_shift_m = jnp.sum(grad_mixed_m, axis=0)
    grad_scale_m = jnp.sum(grad_mixed_m * normed_m, axis=0)
    grad_resid = grad_y + norm_back(normed_m, inverse_m, grad_mixed_m * (1.0 + scale_m))
    grad_branch_a = (gate_a * grad_resid).astype(jnp.bfloat16)
    grad_gate_a = jnp.sum(grad_resid * branch_a, axis=0)
    grad_heads = times_transposed(grad_branch_a, w_proj).astype(jnp.bfloat16)
    grad_proj = transposed_times(heads_out, grad_branch_a)
    grads_query, grads_key, grads_value = lax.map(
        attend_backward, (q_blocks, k_blocks, v_blocks, log_total, grad_heads.reshape(block_shape))
    )
    grad_qkv = jnp.concatenate(
        [
            grads_query.reshape(row_count, head_cols),
            grads_key.reshape(row_count, head_cols),
            grads_value.reshape(row_count, head_cols),
        ],
        axis=1,
    ).astype(jnp.bfloat16)
    grad_wqkv = transposed_times(grad_qkv, mixed_a)
    attn_grad_share = lax.psum_scatter(
        jnp.dot(grad_qkv, w_qkv, preferred_element_type=jnp.float32).astype(jnp.bfloat16),
        "tensor",
        scatter_dimension=0,
        tiled=True,
    ).astype(jnp.float32)
    grad_mixed_a = lax.all_gather(
        attn_grad_share.astype(jnp.bfloat16), "tensor", axis=0, tiled=True
    ).astype(attn_grad_share.dtype)
    token_sums = jnp.sum(grad_qkv, axis=0, dtype=jnp.float32)
    grad_qtime = token_sums[:head_cols, None] * token_wide[None, :]
    grad_vtime = token_sums[2 * head_cols :, None] * token_wide[None, :]
    grad_shift_a = jnp.sum(grad_mixed_a, axis=0)
    grad_scale_a = jnp.sum(grad_mixed_a * normed_a, axis=0)
    grad_in = grad_resid + norm_back(normed_a, inverse_a, grad_mixed_a * (1.0 + scale_a))
    grad_mod = jnp.concatenate(
        [grad_shift_a, grad_scale_a, grad_gate_a, grad_shift_m, grad_scale_m, grad_gate_m]
    )
    grad_mod_piece = lax.dynamic_slice_in_dim(grad_mod, tensor_rank * 6 * head_cols, 6 * head_cols)
    grad_wmod = grad_mod_piece[:, None] * token_wide[None, :]
    grads = jnp.concatenate(
        [grad_wmod, grad_wqkv, grad_qtime, grad_vtime, grad_proj, grad_up, grad_down], axis=0
    )
    grad_blocks = grads.reshape(block_count, block_rows, D)
    owned_blocks = jnp.full((dp_count * own_slots,), -1, jnp.int32).at[slot_of].set(block_ids)
    mine = lax.dynamic_slice_in_dim(owned_blocks, dp_rank * own_slots, own_slots)
    filled = (mine >= 0)[:, None, None]
    placed = (
        jnp.zeros((dp_count * own_slots, block_rows, D), jnp.float32).at[slot_of].set(grad_blocks)
    )
    reduced = lax.psum_scatter(
        placed.astype(jnp.bfloat16), "dp", scatter_dimension=0, tiled=True
    ).astype(jnp.float32)
    new_first = beta_one * first_moment + (1.0 - beta_one) * reduced
    new_second = beta_two * second_moment + (1.0 - beta_two) * reduced * reduced
    fix_one = 1.0 - beta_one**STEP
    fix_two = 1.0 - beta_two**STEP
    change = (
        new_first / fix_one / (jnp.sqrt(new_second / fix_two) + eps_adam)
        + decay_rate * master_weight
    )
    new_master = master_weight - learn_rate * change
    return (
        block_output,
        grad_in.reshape(inputs.shape),
        jnp.where(filled, new_first, 0.0),
        jnp.where(filled, new_second, 0.0),
        jnp.where(filled, new_master, 0.0),
    )


BF = jnp.bfloat16
F32 = jnp.float32
MESH = pl.DeviceIdType.MESH
TILE = 64
HOP_ROWS = 16
PAIR = 48
GELU_C = math.sqrt(2.0 / math.pi)
GELU_K = 0.044715


def rows_at(start, size):
    return pl.ds(pl.multiple_of(start, 16), size)


def remote(src, dst, send_sem, recv_sem, device):
    return pltpu.make_async_remote_copy(
        src_ref=src,
        dst_ref=dst,
        send_sem=send_sem,
        recv_sem=recv_sem,
        device_id=device,
        device_id_type=MESH,
    )


def times(left, right):
    return jnp.dot(left, right, preferred_element_type=F32)


class Sizes:
    def __init__(self, dp_count, tensor_count, slots, block_rows, images, seq):
        self.dp_count, self.tensor_count = dp_count, tensor_count
        self.slots, self.block_rows = slots, block_rows
        self.images, self.seq = images, seq
        self.rows = images * seq
        self.shard = seq // tensor_count
        self.head_cols = D // tensor_count
        self.ffn_cols = FF // tensor_count
        self.heads = HEADS // tensor_count
        self.mod_rows = 6 * self.head_cols
        self.local_rows = 12 * self.head_cols + 2 * self.ffn_cols
        self.blocks = self.local_rows // block_rows
        self.wide = 4 * self.head_cols + 2 * self.ffn_cols
        self.thin = self.mod_rows + 2 * self.head_cols

    def fits(self):
        return (
            self.dp_count == 4
            and self.tensor_count == 8
            and 2 * self.block_rows == PAIR
            and self.shard % HOP_ROWS == 0
            and self.rows % TILE == 0
            and self.head_cols % PAIR == 0
            and self.ffn_cols % PAIR == 0
            and self.wide % (6 * PAIR) == 0
            and self.thin == D
            and self.mod_rows <= 1024
            and self.seq % 128 == 0
        )


def flatten(plan):
    if isinstance(plan, SimpleNamespace):
        return flatten(list(vars(plan).values()))
    if isinstance(plan, list):
        return [leaf for member in plan for leaf in flatten(member)]
    return [plan]


def rebuild(plan, leaves):
    if isinstance(plan, SimpleNamespace):
        return SimpleNamespace(**{key: rebuild(value, leaves) for key, value in vars(plan).items()})
    if isinstance(plan, list):
        return [rebuild(member, leaves) for member in plan]
    return next(leaves)


def scratch_plan(z):
    dma = pltpu.SemaphoreType.DMA
    vm = pltpu.VMEM
    half = z.wide // PAIR // 2

    def dp_sum():
        return SimpleNamespace(
            far=vm((half, PAIR, D), BF),
            fin=vm((z.wide, D), BF),
            s1=dma((half,)),
            r1=dma((half,)),
            s2=dma((half,)),
            r2=dma((half,)),
            s3=dma((half,)),
            r3=dma((half,)),
        )

    def hop_sems():
        return SimpleNamespace(xs=dma((4,)), xr=dma((4,)), zs=dma((3,)), zr=dma((3,)))

    def scatter():
        return SimpleNamespace(
            part=vm((z.seq, D), BF),
            xin=vm((4, z.shard, D), BF),
            zout=vm((3, z.shard, D), BF),
            zin=vm((3, z.shard, D), BF),
            own=vm((z.shard, D), F32),
            sem=hop_sems(),
        )

    def gather():
        return SimpleNamespace(buf=vm((z.seq, D), BF), sem=hop_sems())

    def each(make):
        return [make() for _ in range(z.images)]

    return SimpleNamespace(
        slot_table=pltpu.SMEM((z.blocks,), jnp.int32),
        master=vm((z.slots, z.block_rows, D), F32),
        master_sem=dma((3,)),
        placed=vm((z.local_rows, D), BF),
        tok_all=vm((16 * z.dp_count, D), BF),
        tok_s=dma((3,)),
        tok_r=dma((3,)),
        mod_prod=vm((16 * z.dp_count, D), F32),
        mod_pack=vm((z.dp_count, 16, 128), F32),
        mod_recv=vm((3, 16, 128), F32),
        mod_s=dma((3,)),
        mod_r=dma((3,)),
        mod_own=vm((16, 128), F32),
        mod_all=vm((z.tensor_count, 16, 128), F32),
        moda_s=dma((z.tensor_count - 1,)),
        moda_r=dma((z.tensor_count - 1,)),
        modv=vm((8, D), F32),
        time_qv=vm((8, 2 * 256), F32),
        u=vm((z.rows, D), BF),
        dmlp=vm((z.rows, D), BF),
        q=vm((z.rows, z.head_cols), BF),
        k=vm((z.rows, z.head_cols), BF),
        v=vm((z.rows, z.head_cols), BF),
        o=vm((z.rows, z.head_cols), BF),
        dq=vm((z.rows, z.head_cols), BF),
        dk=vm((z.rows, z.head_cols), BF),
        dv=vm((z.rows, z.head_cols), BF),
        soft=vm((z.images * z.heads, z.seq, z.seq), F32),
        dgact=vm((z.rows, z.ffn_cols), F32),
        gact=vm((z.rows, z.ffn_cols), BF),
        dz=vm((z.rows, z.ffn_cols), BF),
        h1=vm((z.images, z.shard, D), F32),
        attn=vm((z.images, z.shard, D), F32),
        dh1=vm((z.images, z.shard, D), F32),
        dmod=vm((8, D), F32),
        dmod_pack=vm((z.tensor_count, 8, 128), F32),
        dmod_recv=vm((z.tensor_count - 1, 8, 128), F32),
        dmod_s=dma((z.tensor_count - 1,)),
        dmod_r=dma((z.tensor_count - 1,)),
        vec=vm((z.dp_count, 16, 256), F32),
        vec_s=dma((3,)),
        vec_r=dma((3,)),
        out_sem=dma((3 + 2 * z.images,)),
        w=dp_sum(),
        g=dp_sum(),
        w_sib=vm((half, PAIR, D), BF),
        w_mrg=vm((half, PAIR, D), BF),
        rs1=each(scatter),
        rs2=each(scatter),
        rs3=each(scatter),
        rs4=each(scatter),
        ag1=each(gather),
        ag2=each(gather),
        ag3=each(gather),
        ag4=each(gather),
    )


def layer_kernel(z, plan, *refs):
    owners, counts, held, tok, x_ref, grad_ref, master_hbm = refs[:7]
    out_bo, out_ig, out_g, out_vec, out_tok = refs[7:12]
    s = rebuild(plan, iter(refs[12:]))
    s.w.src, s.w.sib, s.w.mrg = s.placed, s.w_sib, s.w_mrg
    s.g.src, s.g.sib, s.g.mrg = s.placed, s.w_sib, s.w_mrg
    nt_dims = (((1,), (1,)), ((), ()))
    tn_dims = (((0,), (0,)), ((), ()))

    def nt(left, right):
        return lax.dot_general(left, right, nt_dims, preferred_element_type=F32)

    def tn(left, right):
        return lax.dot_general(left, right, tn_dims, preferred_element_type=F32)

    hc, fc = z.head_cols, z.ffn_cols
    n_dp, n_t = z.dp_count, z.tensor_count
    dp, t = lax.axis_index("dp"), lax.axis_index("tensor")
    core = lax.rem(dp, 2)
    za, xb = t // 2, lax.rem(t, 2)
    sib = (dp + 1 - 2 * core, t)
    far = (lax.rem(dp + 2, 4), t)
    xp = (dp, t + 1 - 2 * xb)
    half = z.wide // PAIR // 2
    head_part = (4 * hc) // PAIR // 2
    pending = []

    def go(copy):
        copy.start()
        pending.append(copy)

    third = z.slots // 3
    loads = [
        pltpu.make_async_copy(
            master_hbm.at[pl.ds(i * third, third)],
            s.master.at[pl.ds(i * third, third)],
            s.master_sem.at[i],
        )
        for i in range(3)
    ]
    for load in loads:
        load.start()

    barrier = pltpu.get_barrier_semaphore()
    for i in range(1, n_dp):
        pl.semaphore_signal(
            barrier, inc=1, device_id=(lax.rem(dp + i, n_dp), t), device_id_type=MESH
        )
    for i in range(1, n_t):
        pl.semaphore_signal(
            barrier, inc=1, device_id=(dp, lax.rem(t + i, n_t)), device_id_type=MESH
        )
    pl.semaphore_wait(barrier, n_dp + n_t - 2)

    s.tok_all[rows_at(dp * 16, 16), :] = tok[...]

    def tok_copy(i, group):
        block = s.tok_all.at[rows_at(group * 16, 16)]
        return remote(
            block,
            block,
            s.tok_s.at[i - 1],
            s.tok_r.at[i - 1],
            (lax.rem(dp + i, n_dp), t),
        )

    for i in range(1, n_dp):
        go(tok_copy(i, dp))

    def note_slot(block, taken):
        mine = owners[block] == dp
        s.slot_table[block] = jnp.where(mine, taken, -1)
        return taken + mine.astype(jnp.int32)

    lax.fori_loop(0, z.blocks, note_slot, jnp.int32(0))
    for load in loads:
        load.wait()

    def place(lower, upper, shift):
        def one(pair, carry):
            halves = []
            for side in range(2):
                slot = s.slot_table[2 * (pair + shift) + side]
                block = s.master[jnp.clip(slot, 0, z.slots - 1)]
                halves.append(jnp.where(slot >= 0, block, 0.0))
            s.placed[rows_at(pair * PAIR, PAIR), :] = jnp.concatenate(halves, axis=0).astype(BF)
            return carry

        lax.fori_loop(lower, upper, one, 0)

    qkv_pairs, mod_pairs = 3 * hc // PAIR, z.mod_rows // PAIR
    time_pairs = 2 * hc // PAIR
    wide_pairs, all_pairs = z.wide // PAIR, z.local_rows // PAIR
    shift_qkv = mod_pairs
    shift_rest = mod_pairs + time_pairs

    def sum_step_one(ph, lower, upper):
        def one(i, carry):
            remote(
                ph.src.at[rows_at((2 * i + 1 - core) * PAIR, PAIR)],
                ph.sib.at[i],
                ph.s1.at[i],
                ph.r1.at[i],
                sib,
            ).start()
            return carry

        lax.fori_loop(lower, upper, one, 0)

    def sum_step_two(ph, lower, upper):
        def one(i, carry):
            remote(
                ph.src.at[rows_at((2 * i + 1 - core) * PAIR, PAIR)],
                ph.sib.at[i],
                ph.s1.at[i],
                ph.r1.at[i],
                sib,
            ).wait()
            mine = ph.src[rows_at((2 * i + core) * PAIR, PAIR), :].astype(F32)
            ph.mrg[i] = (mine + ph.sib[i].astype(F32)).astype(BF)
            remote(
                ph.mrg.at[i],
                ph.far.at[i],
                ph.s2.at[i],
                ph.r2.at[i],
                far,
            ).start()
            return carry

        lax.fori_loop(lower, upper, one, 0)

    def final_copy(ph, i, side):
        block = ph.fin.at[rows_at((2 * i + side) * PAIR, PAIR)]
        return remote(block, block, ph.s3.at[i], ph.r3.at[i], sib)

    def sum_step_three(ph, lower, upper):
        def one(i, carry):
            remote(
                ph.mrg.at[i],
                ph.far.at[i],
                ph.s2.at[i],
                ph.r2.at[i],
                far,
            ).wait()
            total = ph.mrg[i].astype(F32) + ph.far[i].astype(F32)
            ph.fin[rows_at((2 * i + core) * PAIR, PAIR), :] = total.astype(BF)
            final_copy(ph, i, core).start()
            return carry

        lax.fori_loop(lower, upper, one, 0)

    def sum_step_four(ph, lower, upper):
        def one(i, carry):
            final_copy(ph, i, core).wait_send()
            final_copy(ph, i, 1 - core).wait_recv()
            return carry

        lax.fori_loop(lower, upper, one, 0)

    place(0, qkv_pairs, shift_qkv)
    place(qkv_pairs, 2 * head_part, shift_rest)
    sum_step_one(s.w, 0, head_part)
    place(wide_pairs, wide_pairs + mod_pairs, -wide_pairs)
    place(wide_pairs + mod_pairs, all_pairs, -wide_pairs + qkv_pairs)

    for i in range(1, n_dp):
        tok_copy(i, lax.rem(dp - i + n_dp, n_dp)).wait_recv()
    for i in range(3):
        cols = D // 3
        s.mod_prod[:, i * cols : (i + 1) * cols] = nt(
            s.tok_all[...], s.placed[z.wide + i * cols : z.wide + (i + 1) * cols, :]
        )
    for group in range(n_dp):
        for i in range(D // 128):
            s.mod_pack[group, i : i + 1, :] = s.mod_prod[
                16 * group : 16 * group + 1, 128 * i : 128 * (i + 1)
            ]

    def mod_copy(i):
        group = lax.rem(dp + i, n_dp)
        return remote(
            s.mod_pack.at[group],
            s.mod_recv.at[i - 1],
            s.mod_s.at[i - 1],
            s.mod_r.at[i - 1],
            (group, t),
        )

    for i in range(1, n_dp):
        go(mod_copy(i))
    sum_step_two(s.w, 0, head_part)
    place(2 * head_part, wide_pairs, shift_rest)
    sum_step_one(s.w, head_part, half)
    for i in range(1, n_dp):
        mod_copy(i).wait_recv()
    s.mod_own[...] = (
        s.mod_pack[dp] + s.mod_recv[0] + s.mod_recv[1] + s.mod_recv[2]
    )
    s.mod_all[t] = s.mod_own[...]

    def mod_all_copy(i, member):
        block = s.mod_all.at[member, pl.ds(0, 8)]
        return remote(
            block,
            block,
            s.moda_s.at[i - 1],
            s.moda_r.at[i - 1],
            (dp, lax.rem(t + i, n_t)),
        )

    for i in range(1, n_t):
        go(mod_all_copy(i, t))
    sum_step_two(s.w, head_part, half)
    for i in range(1, n_t):
        mod_all_copy(i, lax.rem(t - i + n_t, n_t)).wait_recv()

    lane = lax.broadcasted_iota(jnp.int32, (8, D), 1)

    def spread(vector):
        return jnp.broadcast_to(vector, (8, D))

    def unpack_rows(block):
        return jnp.concatenate([block[i : i + 1, :] for i in range(block.shape[0])], axis=1)

    own_line = spread(unpack_rows(s.mod_own[0 : D // 128, :]))
    s.time_qv[:, 0:256] = pltpu.roll(own_line, D - z.mod_rows, 1)[:, 0:256]
    s.time_qv[:, 256:512] = pltpu.roll(own_line, D - z.mod_rows - hc, 1)[:, 0:256]
    lines = [jnp.zeros((8, D), F32) for _ in range(6)]
    for member in range(n_t):
        first = member * z.mod_rows
        line = jnp.concatenate(
            [s.mod_all[member, i : i + 1, :] for i in range(8)]
            + [jnp.zeros((1, D - 1024), F32)],
            axis=1,
        )
        line = spread(line)
        for piece in range(6):
            lower = max(first, piece * D) - piece * D
            upper = min(first + z.mod_rows, (piece + 1) * D) - piece * D
            if lower < upper:
                moved = pltpu.roll(line, (first - piece * D) % D, 1) if (first - piece * D) % D else line
                lines[piece] = jnp.where((lane >= lower) & (lane < upper), moved, lines[piece])
    for piece in range(6):
        s.modv[piece : piece + 1, :] = lines[piece][0:1, :]

    def mod_line(piece):
        return s.modv[piece : piece + 1, :]

    def norm_parts(values):
        centred = values - jnp.mean(values, axis=-1, keepdims=True)
        inverse = lax.rsqrt(jnp.mean(centred * centred, axis=-1, keepdims=True) + eps_norm)
        return centred * inverse, inverse

    count_sum = counts[0]
    for i in range(1, n_dp):
        count_sum = count_sum + counts[i]
    group_scale = jnp.full((1, 1), counts[dp], jnp.int32).astype(F32) * n_dp / jnp.full(
        (1, 1), count_sum, jnp.int32
    ).astype(F32)

    def live_of(image):
        return (jnp.full((1, 1), image, jnp.int32) < held[0]).astype(F32)

    def mix_tile(i, carry):
        at = rows_at(i * TILE, TILE)
        normed, _ = norm_parts(x_ref[at, :].astype(F32))
        s.u[at, :] = (normed * (1.0 + mod_line(1)) + mod_line(0)).astype(BF)
        dy = grad_ref[at, :].astype(F32) * (group_scale * live_of(i * TILE // z.seq))
        s.dmlp[at, :] = (mod_line(5) * dy).astype(BF)
        return carry

    lax.fori_loop(0, z.rows // TILE, mix_tile, 0)

    sum_step_three(s.w, 0, head_part)
    sum_step_four(s.w, 0, head_part)
    w_fin = s.w.fin
    w_q, w_k, w_v, w_p = (w_fin.at[i * hc : (i + 1) * hc] for i in range(4))
    w_u = w_fin.at[4 * hc : 4 * hc + fc]
    w_d = w_fin.at[4 * hc + fc : 4 * hc + 2 * fc]

    head_of = lax.broadcasted_iota(jnp.int32, (1, hc), 1) // HEAD_DIM

    def only(values, head):
        return jnp.where(head_of == head, values, jnp.zeros_like(values))

    scale = HEAD_DIM ** (-0.5)
    time_q = s.time_qv[0:1, 0:hc]
    time_v = s.time_qv[0:1, 256 : 256 + hc]

    def attend(image):
        at = rows_at(image * z.seq, z.seq)
        mixed = s.u[at, :]
        q = (nt(mixed, w_q[...]) + time_q).astype(BF)
        k = nt(mixed, w_k[...]).astype(BF)
        v = (nt(mixed, w_v[...]) + time_v).astype(BF)
        s.q[at, :] = q
        s.k[at, :] = k
        s.v[at, :] = v
        out = jnp.zeros((z.seq, hc), F32)
        for head in range(z.heads):
            scores = nt(only(q, head), k) * scale
            e = jnp.exp(scores - jnp.max(scores, axis=-1, keepdims=True))
            p = e / jnp.sum(e, axis=-1, keepdims=True)
            s.soft[image * z.heads + head] = p
            out = out + times(p.astype(BF), only(v, head))
        s.o[at, :] = out.astype(BF)
        s.rs1[image].part[...] = times(out.astype(BF), w_p[...]).astype(BF)

    sh = z.shard

    def rs_x(ph, k):
        theirs = 2 * lax.rem(za + 1 + k, 4) + 1 - xb
        part = ph.part.at[rows_at(theirs * sh, sh)]
        return remote(part, ph.xin.at[k], ph.sem.xs.at[k], ph.sem.xr.at[k], xp)

    def rs_z(ph, k):
        device = (dp, 2 * lax.rem(za + 1 + k, 4) + xb)
        return remote(ph.zout.at[k], ph.zin.at[k], ph.sem.zs.at[k], ph.sem.zr.at[k], device)

    def rs_start(ph):
        for k in range(4):
            go(rs_x(ph, k))

    def rs_middle(ph):
        for k in range(4):
            rs_x(ph, k).wait_recv()
            mine = 2 * lax.rem(za + 1 + k, 4) + xb
            total = ph.part[rows_at(mine * sh, sh), :].astype(F32) + ph.xin[k].astype(F32)
            if k < 3:
                ph.zout[k] = total.astype(BF)
                go(rs_z(ph, k))
            else:
                ph.own[...] = total

    def rs_end(ph):
        total = ph.own[...]
        for k in range(3):
            rs_z(ph, k).wait_recv()
            total = total + ph.zin[k].astype(F32)
        return total

    def ag_z(ph, shard, k):
        block = ph.buf.at[rows_at(shard * sh, sh)]
        device = (dp, 2 * lax.rem(za + 1 + k, 4) + xb)
        return remote(block, block, ph.sem.zs.at[k], ph.sem.zr.at[k], device)

    def ag_x(ph, shard, k):
        block = ph.buf.at[rows_at(shard * sh, sh)]
        return remote(block, block, ph.sem.xs.at[k], ph.sem.xr.at[k], xp)

    def ag_start(ph, value):
        ph.buf[rows_at(t * sh, sh), :] = value
        for k in range(3):
            go(ag_z(ph, t, k))
        go(ag_x(ph, t, 0))

    def ag_middle(ph):
        for k in range(3):
            shard = 2 * lax.rem(za + 3 - k, 4) + xb
            ag_z(ph, shard, k).wait_recv()
            go(ag_x(ph, shard, k + 1))

    def ag_end(ph):
        for k in range(4):
            ag_x(ph, 2 * lax.rem(za + 4 - k, 4) + 1 - xb, k).wait_recv()

    images = range(z.images)
    for i in images:
        attend(i)
        rs_start(s.rs1[i])
    for i in images:
        rs_middle(s.rs1[i])

    def mine_at(image):
        return rows_at(image * z.seq + t * sh, sh)

    for i in images:
        attn = rs_end(s.rs1[i])
        h1 = x_ref[mine_at(i), :].astype(F32) + mod_line(2) * attn
        normed_m, _ = norm_parts(h1)
        ag_start(s.ag1[i], (normed_m * (1.0 + mod_line(4)) + mod_line(3)).astype(BF))
        s.attn[i] = attn
        s.h1[i] = h1
    ag_middle(s.ag1[0])
    sum_step_three(s.w, head_part, half)
    for i in images[1:]:
        ag_middle(s.ag1[i])
    sum_step_four(s.w, head_part, half)

    step_rows = 128

    def up_tile(i, carry):
        at = rows_at(i * step_rows, step_rows)
        s.dgact[at, :] = nt(s.dmlp[at, :], w_d[...])
        return carry

    lax.fori_loop(0, z.rows // step_rows, up_tile, 0)

    def mlp(image):
        def tile(i, carry):
            at = rows_at(image * z.seq + i * step_rows, step_rows)
            hidden = nt(s.ag1[image].buf[rows_at(i * step_rows, step_rows), :], w_u[...])
            square = hidden * hidden
            bend = jnp.tanh(GELU_C * hidden * (1.0 + GELU_K * square))
            s.gact[at, :] = (0.5 * hidden * (1.0 + bend)).astype(BF)
            slope = 0.5 * (1.0 + bend) + 0.5 * hidden * (1.0 - bend * bend) * (
                GELU_C * (1.0 + 3.0 * GELU_K * square)
            )
            dz = (s.dgact[at, :] * slope).astype(BF)
            s.dz[at, :] = dz
            s.rs2[image].part[rows_at(i * step_rows, step_rows), :] = times(dz, w_u[...]).astype(BF)
            return carry

        lax.fori_loop(0, z.seq // step_rows, tile, 0)

    def down(image):
        def tile(i, carry):
            at = rows_at(image * z.seq + i * step_rows, step_rows)
            s.rs4[image].part[rows_at(i * step_rows, step_rows), :] = times(
                s.gact[at, :], w_d[...]
            ).astype(BF)
            return carry

        lax.fori_loop(0, z.seq // step_rows, tile, 0)

    for i in images:
        ag_end(s.ag1[i])
        mlp(i)
        rs_start(s.rs2[i])
    for i in images:
        rs_middle(s.rs2[i])

    cols = 384

    def over_images(left, gathered, at):
        total = 0.0
        for image in images:
            total = total + tn(
                left[image * z.seq : (image + 1) * z.seq, :], gathered[image].buf[:, at]
            )
        return total.astype(BF)

    def grad_tile(i, carry):
        at = pl.ds(pl.multiple_of(i * cols, 128), cols)
        s.g.src[4 * hc : 4 * hc + fc, at] = over_images(s.dz, s.ag1, at)
        s.g.src[4 * hc + fc : z.wide, at] = tn(s.gact[...], s.dmlp[:, at]).astype(BF)
        return carry

    lax.fori_loop(0, D // cols, grad_tile, 0)
    sum_step_one(s.g, head_part, half)
    for i in images:
        down(i)

    def norm_back_of(normed, inverse, upstream):
        return inverse * (
            upstream
            - jnp.mean(upstream, axis=-1, keepdims=True)
            - normed * jnp.mean(upstream * normed, axis=-1, keepdims=True)
        )

    def column_sum(values):
        return jnp.sum(values, axis=0, keepdims=True)

    def dy_of(image):
        return grad_ref[mine_at(image), :].astype(F32) * (group_scale * live_of(image))

    gate_a_sum = shift_m_sum = scale_m_sum = 0.0
    for i in images:
        dw = rs_end(s.rs2[i])
        normed_m, inverse_m = norm_parts(s.h1[i])
        dh1 = dy_of(i) + norm_back_of(normed_m, inverse_m, dw * (1.0 + mod_line(4)))
        ag_start(s.ag2[i], (mod_line(2) * dh1).astype(BF))
        s.dh1[i] = dh1
        gate_a_sum = gate_a_sum + column_sum(dh1 * s.attn[i])
        shift_m_sum = shift_m_sum + column_sum(dw)
        scale_m_sum = scale_m_sum + column_sum(dw * normed_m)
    s.dmod[2:3, :] = gate_a_sum
    s.dmod[3:4, :] = shift_m_sum
    s.dmod[4:5, :] = scale_m_sum
    for i in images:
        ag_middle(s.ag2[i])
    sum_step_two(s.g, head_part, half)

    def attend_back(image):
        at = rows_at(image * z.seq, z.seq)
        do = nt(s.ag2[image].buf[...], w_p[...]).astype(BF)
        q, k, v = s.q[at, :], s.k[at, :], s.v[at, :]
        dq = jnp.zeros((z.seq, hc), F32)
        dk = jnp.zeros((z.seq, hc), F32)
        dv = jnp.zeros((z.seq, hc), F32)
        for head in range(z.heads):
            p = s.soft[image * z.heads + head]
            do_head = only(do, head)
            dp_soft = nt(do_head, v)
            inner = jnp.sum(p * dp_soft, axis=-1, keepdims=True)
            ds = (p * (dp_soft - inner)).astype(BF)
            dq = dq + times(ds, only(k, head))
            dk = dk + tn(ds, only(q, head))
            dv = dv + tn(p.astype(BF), do_head)
        dq = (dq * scale).astype(BF)
        dk = (dk * scale).astype(BF)
        dv = dv.astype(BF)
        s.dq[at, :] = dq
        s.dk[at, :] = dk
        s.dv[at, :] = dv
        s.rs3[image].part[...] = (
            times(dq, w_q[...]) + times(dk, w_k[...]) + times(dv, w_v[...])
        ).astype(BF)

    for i in images:
        ag_end(s.ag2[i])
        attend_back(i)
        rs_start(s.rs3[i])
        rs_start(s.rs4[i])
    for i in images:
        rs_middle(s.rs3[i])
        rs_middle(s.rs4[i])

    def attn_grad_tile(i, carry):
        at = pl.ds(pl.multiple_of(i * cols, 128), cols)
        mixed = s.u[:, at]
        s.g.src[0:hc, at] = tn(s.dq[...], mixed).astype(BF)
        s.g.src[hc : 2 * hc, at] = tn(s.dk[...], mixed).astype(BF)
        s.g.src[2 * hc : 3 * hc, at] = tn(s.dv[...], mixed).astype(BF)
        s.g.src[3 * hc : 4 * hc, at] = over_images(s.o, s.ag2, at)
        return carry

    lax.fori_loop(0, D // cols, attn_grad_tile, 0)
    sum_step_one(s.g, 0, head_part)
    shift_a_sum = scale_a_sum = gate_m_sum = 0.0
    for i in images:
        du = rs_end(s.rs3[i])
        normed_a, inverse_a = norm_parts(x_ref[mine_at(i), :].astype(F32))
        dx = s.dh1[i] + norm_back_of(normed_a, inverse_a, du * (1.0 + mod_line(1)))
        ag_start(s.ag3[i], dx.astype(BF))
        shift_a_sum = shift_a_sum + column_sum(du)
        scale_a_sum = scale_a_sum + column_sum(du * normed_a)
        mlp_sum = rs_end(s.rs4[i])
        gate_m_sum = gate_m_sum + column_sum(dy_of(i) * mlp_sum)
        result = (s.h1[i] + mod_line(5) * mlp_sum) * live_of(i)
        ag_start(s.ag4[i], result.astype(BF))
    s.dmod[0:1, :] = shift_a_sum
    s.dmod[1:2, :] = scale_a_sum
    s.dmod[5:6, :] = gate_m_sum
    sum_step_two(s.g, 0, head_part)
    s.vec[dp] = jnp.zeros((16, 256), F32)
    s.vec[dp, 8:9, 0:hc] = column_sum(s.dq[...].astype(F32))
    s.vec[dp, 9:10, 0:hc] = column_sum(s.dv[...].astype(F32))
    s.dmod[6:8, :] = jnp.zeros((2, D), F32)

    dlines = [spread(s.dmod[i : i + 1, :]) for i in range(6)]
    for member in range(n_t):
        first = member * z.mod_rows
        line = jnp.zeros((8, D), F32)
        for piece in range(6):
            lower = max(first, piece * D) - first
            upper = min(first + z.mod_rows, (piece + 1) * D) - first
            if lower < upper:
                back = (piece * D - first) % D
                moved = pltpu.roll(dlines[piece], back, 1) if back else dlines[piece]
                line = jnp.where((lane >= lower) & (lane < upper), moved, line)
        for i in range(8):
            s.dmod_pack[member, i : i + 1, :] = line[0:1, 128 * i : 128 * (i + 1)]

    def dmod_copy(i):
        member = lax.rem(t + i, n_t)
        return remote(
            s.dmod_pack.at[member],
            s.dmod_recv.at[i - 1],
            s.dmod_s.at[i - 1],
            s.dmod_r.at[i - 1],
            (dp, member),
        )

    for i in range(1, n_t):
        go(dmod_copy(i))
    for i in images:
        ag_middle(s.ag3[i])
        ag_middle(s.ag4[i])
    sum_step_three(s.g, 0, half)
    total = s.dmod_pack[t]
    for i in range(1, n_t):
        dmod_copy(i).wait_recv()
        total = total + s.dmod_recv[i - 1]
    s.vec[dp, 0:8, 0:128] = total

    def vec_copy(i, group):
        return remote(
            s.vec.at[group],
            s.vec.at[group],
            s.vec_s.at[i - 1],
            s.vec_r.at[i - 1],
            (lax.rem(dp + i, n_dp), t),
        )

    for i in range(1, n_dp):
        go(vec_copy(i, dp))
    sum_step_four(s.g, 0, half)
    for i in images:
        ag_end(s.ag3[i])
        ag_end(s.ag4[i])
    for i in range(1, n_dp):
        vec_copy(i, lax.rem(dp - i + n_dp, n_dp)).wait_recv()
    for copy in pending:
        copy.wait_send()

    outs = [(s.g.fin, out_g), (s.vec, out_vec), (s.tok_all, out_tok)]
    for i in images:
        outs.append((s.ag4[i].buf, out_bo.at[i]))
        outs.append((s.ag3[i].buf, out_ig.at[i]))
    stores = [
        pltpu.make_async_copy(src, dst, s.out_sem.at[i]) for i, (src, dst) in enumerate(outs)
    ]
    for store in stores:
        store.start()
    for store in stores:
        store.wait()


def update_kernel(z, group_slots, owners, grads, table, tokens, master, first, second, new_first, new_second, new_master, bos):
    step = pl.program_id(0)
    dp = lax.axis_index("dp")

    @pl.when(step == 0)
    def _():
        def clear(slot, carry):
            bos[slot] = -1
            return carry

        lax.fori_loop(0, z.slots, clear, 0)

        def note(block, taken):
            mine = owners[block] == dp

            @pl.when(mine & (taken < z.slots))
            def _():
                bos[taken] = block

            return taken + mine.astype(jnp.int32)

        lax.fori_loop(0, z.blocks, note, jnp.int32(0))

    rows = z.block_rows
    mod_blocks = z.mod_rows // rows
    head_blocks = z.head_cols // rows
    fix_one = 1.0 - beta_one**STEP
    fix_two = 1.0 - beta_two**STEP

    def put(i, grad):
        weight = master[i]
        one = beta_one * first[i] + (1.0 - beta_one) * grad
        two = beta_two * second[i] + (1.0 - beta_two) * grad * grad
        new_first[i] = one
        new_second[i] = two
        spread = two * (1.0 / fix_two)
        root = spread * lax.rsqrt(spread)
        change = one * (1.0 / fix_one) * pltpu.reciprocal(root + eps_adam) + decay_rate * weight
        new_master[i] = weight - learn_rate * change

    def slot(i, carry):
        block = bos[step * group_slots + i]
        is_mod = block < mod_blocks
        is_time = (block >= mod_blocks + 3 * head_blocks) & (block < mod_blocks + 5 * head_blocks)

        @pl.when(block < 0)
        def _():
            new_first[i] = jnp.zeros((rows, D), F32)
            new_second[i] = jnp.zeros((rows, D), F32)
            new_master[i] = jnp.zeros((rows, D), F32)

        @pl.when((block >= 0) & (is_mod | is_time))
        def _():
            index = jnp.where(is_mod, block, block - 3 * head_blocks)
            columns = table[index]
            grad = columns[:, 0:1] * tokens[0:1, :].astype(F32)
            for group in range(1, z.dp_count):
                grad = grad + columns[:, group : group + 1] * tokens[
                    16 * group : 16 * group + 1, :
                ].astype(F32)
            put(i, grad)

        @pl.when((block >= 0) & jnp.logical_not(is_mod | is_time))
        def _():
            index = jnp.where(
                block < mod_blocks + 3 * head_blocks,
                block - mod_blocks,
                block - mod_blocks - 2 * head_blocks,
            )
            both = grads[rows_at(index // 2 * PAIR, PAIR), :].astype(F32)
            put(i, jnp.where(lax.rem(index, 2) == 0, both[:rows], both[rows:]))

        return carry

    lax.fori_loop(0, group_slots, slot, 0)


def per_device_fast(
    z,
    inputs,
    out_grad,
    bucket,
    counts,
    images_held,
    owners,
    master_weight,
    first_moment,
    second_moment,
):
    token = jnp.broadcast_to(time_token(bucket[0]).astype(BF)[None, :], (16, D))
    plan = scratch_plan(z)
    smem = pl.BlockSpec(memory_space=pltpu.SMEM)
    vmem = pl.BlockSpec(memory_space=pltpu.VMEM)
    hbm = pl.BlockSpec(memory_space=pl.ANY)
    flops = 6 * z.rows * D * z.wide
    block_output, input_grad, grads, vectors, tokens = pl.pallas_call(
        partial(layer_kernel, z, plan),
        out_shape=(
            jax.ShapeDtypeStruct(inputs.shape, BF),
            jax.ShapeDtypeStruct(inputs.shape, BF),
            jax.ShapeDtypeStruct((z.wide, D), BF),
            jax.ShapeDtypeStruct((z.dp_count, 16, 256), F32),
            jax.ShapeDtypeStruct((16 * z.dp_count, D), BF),
        ),
        in_specs=[smem, smem, smem, vmem, vmem, vmem, hbm],
        out_specs=(hbm,) * 5,
        scratch_shapes=flatten(plan),
        compiler_params=pltpu.CompilerParams(
            collective_id=0, has_side_effects=True, vmem_limit_bytes=62 * 2**20
        ),
        cost_estimate=pl.CostEstimate(
            flops=flops, bytes_accessed=20 * 2**20, transcendentals=z.rows * z.ffn_cols
        ),
        name="layer",
    )(
        owners,
        counts,
        images_held,
        token,
        inputs.reshape(z.rows, D),
        out_grad.reshape(z.rows, D),
        master_weight,
    )
    columns = jnp.concatenate(
        [
            vectors[:, :8, :128].reshape(z.dp_count, 1024)[:, : z.mod_rows],
            vectors[:, 8, : z.head_cols],
            vectors[:, 9, : z.head_cols],
        ],
        axis=1,
    ).T.reshape(z.thin // z.block_rows, z.block_rows, z.dp_count)
    group_slots = next(size for size in (15, 12, 10, 8, 6, 5, 4, 3, 2, 1) if z.slots % size == 0)
    block = pl.BlockSpec((group_slots, z.block_rows, D), lambda i: (i, 0, 0))
    state = jax.ShapeDtypeStruct(master_weight.shape, F32)
    new_first, new_second, new_master = pl.pallas_call(
        partial(update_kernel, z, group_slots),
        grid=(z.slots // group_slots,),
        out_shape=(state,) * 3,
        in_specs=[smem, vmem, vmem, vmem, block, block, block],
        out_specs=(block,) * 3,
        scratch_shapes=[pltpu.SMEM((z.slots,), jnp.int32)],
        compiler_params=pltpu.CompilerParams(vmem_limit_bytes=48 * 2**20),
        name="update",
    )(owners, grads, columns, tokens, master_weight, first_moment, second_moment)
    return (
        block_output,
        input_grad.astype(F32),
        new_first,
        new_second,
        new_master,
    )


def per_device(inputs, out_grad, bucket, counts, images_held, owners, master, first, second):
    sizes = Sizes(
        lax.axis_size("dp"),
        lax.axis_size("tensor"),
        master.shape[0],
        master.shape[1],
        inputs.shape[0],
        inputs.shape[1],
    )
    run = partial(per_device_fast, sizes) if sizes.fits() else per_device_plain
    return run(inputs, out_grad, bucket, counts, images_held, owners, master, first, second)


def solution(mesh):
    return jax.shard_map(
        per_device,
        mesh=mesh,
        in_specs=(
            P("dp", None, None),
            P("dp", None, None),
            P("dp"),
            P(),
            P("dp"),
            P(),
            P("dp", "tensor", None),
            P("dp", "tensor", None),
            P("dp", "tensor", None),
        ),
        out_specs=(
            P("dp", None, None),
            P("dp", None, None),
            P("dp", "tensor", None),
            P("dp", "tensor", None),
            P("dp", "tensor", None),
        ),
        check_vma=False,
    )
```

```python
from functools import partial
import math
from types import SimpleNamespace

import jax
import jax.numpy as jnp
from jax import lax
from jax.experimental import pallas as pl
from jax.experimental.pallas import tpu as pltpu
from jax.sharding import PartitionSpec as P

D = 1152
HEADS = 16
HEAD_DIM = 72
FF = 4608
NBUCKET = 8
STEP = 10


eps_norm = 1e-06
beta_one = 0.5
beta_two = 0.5
learn_rate = 0.03
decay_rate = 0.01
eps_adam = 1e-08


def time_token(bucket_value):
    half_width = D // 2
    freqs = jnp.exp(-math.log(10000.0) * jnp.arange(half_width, dtype=jnp.float32) / half_width)
    instant = (bucket_value.astype(jnp.float32) + 0.5) * (1000.0 / NBUCKET)
    angles = instant * freqs
    embed = jnp.concatenate([jnp.cos(angles), jnp.sin(angles)])
    return embed * jax.nn.sigmoid(embed)


def norm_stats(values):
    centred = values - jnp.mean(values, axis=-1, keepdims=True)
    inverse = lax.rsqrt(jnp.mean(centred * centred, axis=-1, keepdims=True) + eps_norm)
    return (centred * inverse, inverse)


def norm_back(normed, inverse, upstream):
    return inverse * (
        upstream
        - jnp.mean(upstream, axis=-1, keepdims=True)
        - normed * jnp.mean(upstream * normed, axis=-1, keepdims=True)
    )


def times_transposed(left, right):
    return lax.dot_general(
        left, right, (((1,), (1,)), ((), ())), preferred_element_type=jnp.float32
    )


def transposed_times(left, right):
    return lax.dot_general(
        left, right, (((0,), (0,)), ((), ())), preferred_element_type=jnp.float32
    )


def attend_forward(block):
    queries, key_rows, values = block
    scores = jnp.einsum(
        "bqhd,bkhd->bhqk", queries, key_rows, preferred_element_type=jnp.float32
    ) * HEAD_DIM ** (-0.5)
    row_peak = jnp.max(scores, axis=-1, keepdims=True)
    exp_scores = jnp.exp(scores - row_peak)
    row_total = jnp.sum(exp_scores, axis=-1, keepdims=True)
    soft = (exp_scores / row_total).astype(jnp.bfloat16)
    attended = jnp.einsum("bhqk,bkhd->bqhd", soft, values, preferred_element_type=jnp.float32)
    return (attended, row_peak[..., 0] + jnp.log(row_total[..., 0]))


def attend_backward(block):
    queries, key_rows, values, log_total, upstream = block
    scale_factor = HEAD_DIM ** (-0.5)
    scores = (
        jnp.einsum("bqhd,bkhd->bhqk", queries, key_rows, preferred_element_type=jnp.float32)
        * scale_factor
    )
    soft = jnp.exp(scores - log_total[..., None])
    grad_soft = jnp.einsum("bqhd,bkhd->bhqk", upstream, values, preferred_element_type=jnp.float32)
    inner_sum = jnp.sum(soft * grad_soft, axis=-1, keepdims=True)
    grad_scores = (soft * (grad_soft - inner_sum)).astype(jnp.bfloat16)
    grad_query = (
        jnp.einsum("bhqk,bkhd->bqhd", grad_scores, key_rows, preferred_element_type=jnp.float32)
        * scale_factor
    )
    grad_key = (
        jnp.einsum("bhqk,bqhd->bkhd", grad_scores, queries, preferred_element_type=jnp.float32)
        * scale_factor
    )
    grad_value = jnp.einsum(
        "bhqk,bqhd->bkhd", soft.astype(jnp.bfloat16), upstream, preferred_element_type=jnp.float32
    )
    return (grad_query, grad_key, grad_value)


def per_device_plain(
    inputs,
    out_grad,
    bucket,
    counts,
    images_held,
    owners,
    master_weight,
    first_moment,
    second_moment,
):
    dp_count = lax.axis_size("dp")
    tensor_count = lax.axis_size("tensor")
    dp_rank = lax.axis_index("dp")
    tensor_rank = lax.axis_index("tensor")
    own_slots = master_weight.shape[0]
    block_rows = master_weight.shape[1]
    head_cols = D // tensor_count
    ffn_cols = FF // tensor_count
    local_heads = HEADS // tensor_count
    local_rows = 12 * head_cols + 2 * ffn_cols
    block_count = local_rows // block_rows
    image_count = inputs.shape[0]
    seq_len = inputs.shape[1]
    row_count = image_count * seq_len
    block_ids = jnp.arange(block_count, dtype=jnp.int32)
    earlier = (owners[None, :] == owners[:, None]) & (block_ids[None, :] < block_ids[:, None])
    slot_of = owners * own_slots + jnp.sum(earlier.astype(jnp.int32), axis=1)
    gathered = lax.all_gather(master_weight.astype(jnp.bfloat16), "dp", axis=0, tiled=True)
    weights = gathered[slot_of].reshape(local_rows, D)
    w_mod = weights[: 6 * head_cols]
    w_qkv = weights[6 * head_cols : 9 * head_cols]
    w_qtime = weights[9 * head_cols : 10 * head_cols]
    w_vtime = weights[10 * head_cols : 11 * head_cols]
    w_proj = weights[11 * head_cols : 12 * head_cols]
    w_up = weights[12 * head_cols : 12 * head_cols + ffn_cols]
    w_down = weights[12 * head_cols + ffn_cols :]
    token = time_token(bucket[0]).astype(jnp.bfloat16)
    token_wide = token.astype(jnp.float32)
    mod_piece = jnp.dot(w_mod, token, preferred_element_type=jnp.float32)
    modulation = lax.all_gather(mod_piece, "tensor", axis=0, tiled=True)
    shift_a, scale_a, gate_a, shift_m, scale_m, gate_m = jnp.split(modulation, 6)
    counts_f = counts.astype(jnp.float32)
    group_scale = counts_f[dp_rank] * dp_count / jnp.sum(counts_f)
    flat_rows = inputs.reshape(row_count, D).astype(jnp.float32)
    live = (jnp.arange(row_count, dtype=jnp.int32) // seq_len < images_held[0]).astype(jnp.float32)[
        :, None
    ]
    normed_a, inverse_a = norm_stats(flat_rows)
    mixed_a = (normed_a * (1.0 + scale_a) + shift_a).astype(jnp.bfloat16)
    projected = times_transposed(mixed_a, w_qkv)
    time_query = jnp.dot(w_qtime, token, preferred_element_type=jnp.float32)
    time_value = jnp.dot(w_vtime, token, preferred_element_type=jnp.float32)
    queries = (projected[:, :head_cols] + time_query).astype(jnp.bfloat16)
    key_rows = projected[:, head_cols : 2 * head_cols].astype(jnp.bfloat16)
    values = (projected[:, 2 * head_cols :] + time_value).astype(jnp.bfloat16)
    group_imgs = math.gcd(image_count, max(1, 512 // seq_len))
    block_shape = (image_count // group_imgs, group_imgs, seq_len, local_heads, HEAD_DIM)
    q_blocks = queries.reshape(block_shape)
    k_blocks = key_rows.reshape(block_shape)
    v_blocks = values.reshape(block_shape)
    attended, log_total = lax.map(attend_forward, (q_blocks, k_blocks, v_blocks))
    heads_out = attended.reshape(row_count, head_cols).astype(jnp.bfloat16)
    heads_share = lax.psum_scatter(
        jnp.dot(heads_out, w_proj, preferred_element_type=jnp.float32).astype(jnp.bfloat16),
        "tensor",
        scatter_dimension=0,
        tiled=True,
    ).astype(jnp.float32)
    branch_a = lax.all_gather(
        heads_share.astype(jnp.bfloat16), "tensor", axis=0, tiled=True
    ).astype(heads_share.dtype)
    resid = flat_rows + gate_a * branch_a
    normed_m, inverse_m = norm_stats(resid)
    mixed_m = (normed_m * (1.0 + scale_m) + shift_m).astype(jnp.bfloat16)
    hidden = times_transposed(mixed_m, w_up)
    acted = jax.nn.gelu(hidden, approximate=True).astype(jnp.bfloat16)
    hidden_share = lax.psum_scatter(
        jnp.dot(acted, w_down, preferred_element_type=jnp.float32).astype(jnp.bfloat16),
        "tensor",
        scatter_dimension=0,
        tiled=True,
    ).astype(jnp.float32)
    branch_m = lax.all_gather(
        hidden_share.astype(jnp.bfloat16), "tensor", axis=0, tiled=True
    ).astype(hidden_share.dtype)
    result = resid + gate_m * branch_m
    block_output = (result * live).astype(jnp.bfloat16).reshape(inputs.shape)
    grad_y = out_grad.reshape(row_count, D).astype(jnp.float32) * (group_scale * live)
    grad_branch_m = (gate_m * grad_y).astype(jnp.bfloat16)
    grad_gate_m = jnp.sum(grad_y * branch_m, axis=0)
    grad_acted = times_transposed(grad_branch_m, w_down)
    grad_down = transposed_times(acted, grad_branch_m)
    grad_hidden = jax.vjp(partial(jax.nn.gelu, approximate=True), hidden)[1](grad_acted)[0].astype(
        jnp.bfloat16
    )
    grad_up = transposed_times(grad_hidden, mixed_m)
    mlp_grad_share = lax.psum_scatter(
        jnp.dot(grad_hidden, w_up, preferred_element_type=jnp.float32).astype(jnp.bfloat16),
        "tensor",
        scatter_dimension=0,
        tiled=True,
    ).astype(jnp.float32)
    grad_mixed_m = lax.all_gather(
        mlp_grad_share.astype(jnp.bfloat16), "tensor", axis=0, tiled=True
    ).astype(mlp_grad_share.dtype)
    grad_shift_m = jnp.sum(grad_mixed_m, axis=0)
    grad_scale_m = jnp.sum(grad_mixed_m * normed_m, axis=0)
    grad_resid = grad_y + norm_back(normed_m, inverse_m, grad_mixed_m * (1.0 + scale_m))
    grad_branch_a = (gate_a * grad_resid).astype(jnp.bfloat16)
    grad_gate_a = jnp.sum(grad_resid * branch_a, axis=0)
    grad_heads = times_transposed(grad_branch_a, w_proj).astype(jnp.bfloat16)
    grad_proj = transposed_times(heads_out, grad_branch_a)
    grads_query, grads_key, grads_value = lax.map(
        attend_backward, (q_blocks, k_blocks, v_blocks, log_total, grad_heads.reshape(block_shape))
    )
    grad_qkv = jnp.concatenate(
        [
            grads_query.reshape(row_count, head_cols),
            grads_key.reshape(row_count, head_cols),
            grads_value.reshape(row_count, head_cols),
        ],
        axis=1,
    ).astype(jnp.bfloat16)
    grad_wqkv = transposed_times(grad_qkv, mixed_a)
    attn_grad_share = lax.psum_scatter(
        jnp.dot(grad_qkv, w_qkv, preferred_element_type=jnp.float32).astype(jnp.bfloat16),
        "tensor",
        scatter_dimension=0,
        tiled=True,
    ).astype(jnp.float32)
    grad_mixed_a = lax.all_gather(
        attn_grad_share.astype(jnp.bfloat16), "tensor", axis=0, tiled=True
    ).astype(attn_grad_share.dtype)
    token_sums = jnp.sum(grad_qkv, axis=0, dtype=jnp.float32)
    grad_qtime = token_sums[:head_cols, None] * token_wide[None, :]
    grad_vtime = token_sums[2 * head_cols :, None] * token_wide[None, :]
    grad_shift_a = jnp.sum(grad_mixed_a, axis=0)
    grad_scale_a = jnp.sum(grad_mixed_a * normed_a, axis=0)
    grad_in = grad_resid + norm_back(normed_a, inverse_a, grad_mixed_a * (1.0 + scale_a))
    grad_mod = jnp.concatenate(
        [grad_shift_a, grad_scale_a, grad_gate_a, grad_shift_m, grad_scale_m, grad_gate_m]
    )
    grad_mod_piece = lax.dynamic_slice_in_dim(grad_mod, tensor_rank * 6 * head_cols, 6 * head_cols)
    grad_wmod = grad_mod_piece[:, None] * token_wide[None, :]
    grads = jnp.concatenate(
        [grad_wmod, grad_wqkv, grad_qtime, grad_vtime, grad_proj, grad_up, grad_down], axis=0
    )
    grad_blocks = grads.reshape(block_count, block_rows, D)
    owned_blocks = jnp.full((dp_count * own_slots,), -1, jnp.int32).at[slot_of].set(block_ids)
    mine = lax.dynamic_slice_in_dim(owned_blocks, dp_rank * own_slots, own_slots)
    filled = (mine >= 0)[:, None, None]
    placed = (
        jnp.zeros((dp_count * own_slots, block_rows, D), jnp.float32).at[slot_of].set(grad_blocks)
    )
    reduced = lax.psum_scatter(
        placed.astype(jnp.bfloat16), "dp", scatter_dimension=0, tiled=True
    ).astype(jnp.float32)
    new_first = beta_one * first_moment + (1.0 - beta_one) * reduced
    new_second = beta_two * second_moment + (1.0 - beta_two) * reduced * reduced
    fix_one = 1.0 - beta_one**STEP
    fix_two = 1.0 - beta_two**STEP
    change = (
        new_first / fix_one / (jnp.sqrt(new_second / fix_two) + eps_adam)
        + decay_rate * master_weight
    )
    new_master = master_weight - learn_rate * change
    return (
        block_output,
        grad_in.reshape(inputs.shape),
        jnp.where(filled, new_first, 0.0),
        jnp.where(filled, new_second, 0.0),
        jnp.where(filled, new_master, 0.0),
    )


BF = jnp.bfloat16
F32 = jnp.float32
MESH = pl.DeviceIdType.MESH
TILE = 64
PAIR = 48
GELU_C = math.sqrt(2.0 / math.pi)
GELU_K = 0.044715


def rows_at(start, size):
    return pl.ds(pl.multiple_of(start, 16), size)


def remote(src, dst, send_sem, recv_sem, device):
    return pltpu.make_async_remote_copy(
        src_ref=src,
        dst_ref=dst,
        send_sem=send_sem,
        recv_sem=recv_sem,
        device_id=device,
        device_id_type=MESH,
    )


def times(left, right):
    return jnp.dot(left, right, preferred_element_type=F32)


class Sizes:
    def __init__(self, dp_count, tensor_count, slots, block_rows, images, seq):
        self.dp_count, self.tensor_count = dp_count, tensor_count
        self.slots, self.block_rows = slots, block_rows
        self.images, self.seq = images, seq
        self.parts = 2
        self.part_rows = seq // self.parts
        self.shard = self.part_rows // 4
        self.head_cols = D // tensor_count
        self.ffn_cols = FF // tensor_count
        self.heads = HEADS // tensor_count
        self.mod_rows = 6 * self.head_cols
        self.local_rows = 12 * self.head_cols + 2 * self.ffn_cols
        self.blocks = self.local_rows // block_rows
        self.wide = 4 * self.head_cols + 2 * self.ffn_cols
        self.thin = self.mod_rows + 2 * self.head_cols

    def fits(self):
        return (
            self.dp_count == 4
            and self.tensor_count == 8
            and self.images == 2
            and 2 * self.block_rows == PAIR
            and self.slots % 3 == 0
            and self.seq % 128 == 0
            and self.head_cols % PAIR == 0
            and self.ffn_cols % PAIR == 0
            and self.wide % (6 * PAIR) == 0
            and self.thin == D
            and self.thin == 2 * self.ffn_cols
            and self.mod_rows <= 1024
        )


def flatten(plan):
    if isinstance(plan, SimpleNamespace):
        return flatten(list(vars(plan).values()))
    if isinstance(plan, list):
        return [leaf for member in plan for leaf in flatten(member)]
    return [plan]


def rebuild(plan, leaves):
    if isinstance(plan, SimpleNamespace):
        return SimpleNamespace(**{key: rebuild(value, leaves) for key, value in vars(plan).items()})
    if isinstance(plan, list):
        return [rebuild(member, leaves) for member in plan]
    return next(leaves)


def scratch_plan(z):
    dma = pltpu.SemaphoreType.DMA
    vm = pltpu.VMEM
    half = z.wide // PAIR // 2

    def pairs():
        return vm((half, PAIR, D), BF)

    def attention():
        names = 7
        q, k, v, o, dq, dk, dv = (vm((z.seq, z.head_cols), BF) for _ in range(names))
        return SimpleNamespace(q=q, k=k, v=v, o=o, dq=dq, dk=dk, dv=dv)

    def hidden():
        return SimpleNamespace(
            dgact=vm((z.seq, z.ffn_cols), F32),
            gact=vm((z.seq, z.ffn_cols), BF),
            dz=vm((z.seq, z.ffn_cols), BF),
        )

    def scatter():
        return SimpleNamespace(
            part=vm((z.part_rows, D), BF),
            zout=vm((z.shard, D), BF),
            zin=vm((3, z.shard, D), BF),
            zs=dma((3,)),
            zr=dma((3,)),
        )

    def gather():
        return SimpleNamespace(buf=vm((z.part_rows, D), BF), zs=dma((3,)), zr=dma((3,)))

    def gather_x():
        return SimpleNamespace(
            buf=vm((z.part_rows, D), BF),
            xbuf=vm((z.part_rows, D), BF),
            zs=dma((3,)),
            zr=dma((3,)),
            xs=dma((4,)),
            xr=dma((4,)),
        )

    def each(make):
        return [make() for _ in range(z.parts)]

    return SimpleNamespace(
        slot_table=pltpu.SMEM((z.blocks,), jnp.int32),
        master=vm((z.slots, z.block_rows, D), F32),
        master_sem=dma((3,)),
        x=vm((z.seq, D), BF),
        grad=vm((z.seq, D), BF),
        in_sem=dma((2,)),
        placed=vm((z.local_rows, D), BF),
        extra=vm((4 * z.head_cols, D), BF),
        tok_all=vm((16 * z.dp_count, D), BF),
        tok_s=dma((3,)),
        tok_r=dma((3,)),
        mod_prod=vm((16 * z.dp_count, D), F32),
        mod_pack=vm((z.dp_count, 16, 128), F32),
        mod_recv=vm((3, 16, 128), F32),
        mod_s=dma((3,)),
        mod_r=dma((3,)),
        mod_all=vm((z.tensor_count, 16, 128), F32),
        moda_s=dma((z.tensor_count - 1,)),
        moda_r=dma((z.tensor_count - 1,)),
        modv=vm((8, D), F32),
        time_qv=vm((8, 4 * 256), F32),
        u=vm((z.seq, D), BF),
        dmlp=vm((z.seq, D), BF),
        heads=[attention(), attention()],
        soft=vm((2 * z.heads, z.seq, z.seq), F32),
        hid=[hidden(), hidden()],
        h1=vm((z.parts, z.shard, D), F32),
        attn=vm((z.parts, z.shard, D), F32),
        dh1=vm((z.parts, z.shard, D), F32),
        dmod=vm((8, D), F32),
        dmod_pack=vm((z.tensor_count, 8, 128), F32),
        dmod_recv=vm((z.tensor_count - 1, 8, 128), F32),
        dmod_s=dma((z.tensor_count - 1,)),
        dmod_r=dma((z.tensor_count - 1,)),
        dsum=vm((8, 256), F32),
        dsum_in=vm((8, 256), F32),
        dsum_s=dma((1,)),
        dsum_r=dma((1,)),
        vec=vm((z.dp_count, 16, 256), F32),
        vec_s=dma((3,)),
        vec_r=dma((3,)),
        out_sem=dma((3 + 4 * z.parts,)),
        sib=pairs(),
        mrg=pairs(),
        w=SimpleNamespace(
            far=pairs(),
            fin=vm((z.wide, D), BF),
            oth=vm((z.wide, D), BF),
            s1=dma((half,)),
            r1=dma((half,)),
            s2=dma((half,)),
            r2=dma((half,)),
            s3=dma((half,)),
            r3=dma((half,)),
            s4=dma((half,)),
            r4=dma((half,)),
            s5=dma((half,)),
            r5=dma((half,)),
        ),
        g=SimpleNamespace(
            far=pairs(),
            fin=vm((z.wide, D), BF),
            sib1=pairs(),
            mrg1=pairs(),
            xin=pairs(),
            s0=dma((half,)),
            r0=dma((half,)),
            s1=dma((half,)),
            r1=dma((half,)),
            s2=dma((half,)),
            r2=dma((half,)),
            s3=dma((half,)),
            r3=dma((half,)),
            s4=dma((half,)),
            r4=dma((half,)),
        ),
        rs1=each(scatter),
        rs2=each(scatter),
        rs3=each(scatter),
        rs4=each(scatter),
        ag1=each(gather),
        ag2=each(gather),
        ag3=each(gather_x),
        ag4=each(gather_x),
    )


def layer_kernel(z, plan, *refs):
    owners, counts, held, tok, x_hbm, grad_hbm, master_hbm = refs[:7]
    out_bo, out_ig, out_g, out_vec, out_tok = refs[7:12]
    s = rebuild(plan, iter(refs[12:]))
    nt_dims = (((1,), (1,)), ((), ()))
    tn_dims = (((0,), (0,)), ((), ()))

    def nt(left, right):
        return lax.dot_general(left, right, nt_dims, preferred_element_type=F32)

    def tn(left, right):
        return lax.dot_general(left, right, tn_dims, preferred_element_type=F32)

    hc, fc = z.head_cols, z.ffn_cols
    n_dp, n_t = z.dp_count, z.tensor_count
    dp, t = lax.axis_index("dp"), lax.axis_index("tensor")
    core = lax.rem(dp, 2)
    za, xb = t // 2, lax.rem(t, 2)
    near_z = za + 1 - 2 * lax.rem(za, 2)
    far_z = lax.rem(za + 2, 4)
    cross_z = 3 - za
    sib = (dp + 1 - 2 * core, t)
    far = (lax.rem(dp + 2, 4), t)
    xp = (dp, t + 1 - 2 * xb)
    near, across = (dp, 2 * near_z + xb), (dp, 2 * far_z + xb)
    half = z.wide // PAIR // 2
    head_part = (4 * hc) // PAIR // 2
    pending = []

    def go(copy):
        copy.start()
        pending.append(copy)

    third = z.slots // 3
    loads = [
        pltpu.make_async_copy(
            master_hbm.at[pl.ds(i * third, third)],
            s.master.at[pl.ds(i * third, third)],
            s.master_sem.at[i],
        )
        for i in range(3)
    ]
    image_loads = [
        pltpu.make_async_copy(x_hbm.at[xb], s.x, s.in_sem.at[0]),
        pltpu.make_async_copy(grad_hbm.at[xb], s.grad, s.in_sem.at[1]),
    ]
    for load in loads + image_loads:
        load.start()

    barrier = pltpu.get_barrier_semaphore()
    for i in range(1, n_dp):
        pl.semaphore_signal(
            barrier, inc=1, device_id=(lax.rem(dp + i, n_dp), t), device_id_type=MESH
        )
    for i in range(1, n_t):
        pl.semaphore_signal(
            barrier, inc=1, device_id=(dp, lax.rem(t + i, n_t)), device_id_type=MESH
        )
    pl.semaphore_wait(barrier, n_dp + n_t - 2)

    s.tok_all[rows_at(dp * 16, 16), :] = tok[...]

    def tok_copy(i, group):
        block = s.tok_all.at[rows_at(group * 16, 16)]
        return remote(
            block,
            block,
            s.tok_s.at[i - 1],
            s.tok_r.at[i - 1],
            (lax.rem(dp + i, n_dp), t),
        )

    for i in range(1, n_dp):
        go(tok_copy(i, dp))

    def note_slot(block, taken):
        mine = owners[block] == dp
        s.slot_table[block] = jnp.where(mine, taken, -1)
        return taken + mine.astype(jnp.int32)

    lax.fori_loop(0, z.blocks, note_slot, jnp.int32(0))
    for load in loads:
        load.wait()

    def place(lower, upper, shift):
        def one(pair, carry):
            halves = []
            for side in range(2):
                slot = s.slot_table[2 * (pair + shift) + side]
                block = s.master[jnp.clip(slot, 0, z.slots - 1)]
                halves.append(jnp.where(slot >= 0, block, 0.0))
            s.placed[rows_at(pair * PAIR, PAIR), :] = jnp.concatenate(halves, axis=0).astype(BF)
            return carry

        lax.fori_loop(lower, upper, one, 0)

    qkv_pairs, mod_pairs = 3 * hc // PAIR, z.mod_rows // PAIR
    time_pairs = 2 * hc // PAIR
    wide_pairs, all_pairs = z.wide // PAIR, z.local_rows // PAIR
    shift_qkv = mod_pairs
    shift_rest = mod_pairs + time_pairs

    def loop(lower, upper, body):
        lax.fori_loop(lower, upper, lambda i, carry: (body(i), carry)[1], 0)

    def pair_at(ref, i, side, first=0):
        return ref.at[rows_at(first + (2 * i + side) * PAIR, PAIR)]

    def w_core(i):
        return remote(
            pair_at(s.placed, i, 1 - core), s.sib.at[i], s.w.s1.at[i], s.w.r1.at[i], sib
        )

    def w_far(i):
        return remote(s.mrg.at[i], s.w.far.at[i], s.w.s2.at[i], s.w.r2.at[i], far)

    def w_back(i, side):
        block = pair_at(s.w.fin, i, side)
        return remote(block, block, s.w.s3.at[i], s.w.r3.at[i], sib)

    def w_x(i):
        return remote(
            pair_at(s.w.fin, i, core),
            pair_at(s.w.oth, i, core),
            s.w.s4.at[i],
            s.w.r4.at[i],
            xp,
        )

    def w_pass(i, side):
        block = pair_at(s.w.oth, i, side)
        return remote(block, block, s.w.s5.at[i], s.w.r5.at[i], sib)

    def w_one(lower, upper):
        loop(lower, upper, lambda i: w_core(i).start())

    def w_two(lower, upper):
        def one(i):
            w_core(i).wait()
            mine = s.placed[rows_at((2 * i + core) * PAIR, PAIR), :].astype(F32)
            s.mrg[i] = (mine + s.sib[i].astype(F32)).astype(BF)
            w_far(i).start()

        loop(lower, upper, one)

    def w_three(lower, upper):
        def one(i):
            w_far(i).wait()
            total = s.mrg[i].astype(F32) + s.w.far[i].astype(F32)
            s.w.fin[rows_at((2 * i + core) * PAIR, PAIR), :] = total.astype(BF)
            w_x(i).start()
            w_back(i, core).start()

        loop(lower, upper, one)

    def w_four(lower, upper):
        def one(i):
            w_x(i).wait()
            w_pass(i, core).start()

        loop(lower, upper, one)

    def w_end_own(lower, upper):
        def one(i):
            w_back(i, core).wait_send()
            w_back(i, 1 - core).wait_recv()

        loop(lower, upper, one)

    def w_end_other(lower, upper):
        def one(i):
            w_pass(i, core).wait_send()
            w_pass(i, 1 - core).wait_recv()

        loop(lower, upper, one)

    def g_core(i, index, src, first):
        into, send, recv = ((s.sib, s.g.s0, s.g.r0), (s.g.sib1, s.g.s1, s.g.r1))[index]
        return remote(
            pair_at(src, i, 1 - core, first), into.at[i], send.at[i], recv.at[i], sib
        )

    def g_x(i):
        return remote(s.g.mrg1.at[i], s.g.xin.at[i], s.g.s2.at[i], s.g.r2.at[i], xp)

    def g_far(i):
        return remote(s.mrg.at[i], s.g.far.at[i], s.g.s3.at[i], s.g.r3.at[i], far)

    def g_back(i, side):
        block = pair_at(s.g.fin, i, side)
        return remote(block, block, s.g.s4.at[i], s.g.r4.at[i], sib)

    def g_one(lower, upper, src, first):
        def one(i):
            g_core(i, 1, src, first).start()
            g_core(i, 0, s.placed, 0).start()

        loop(lower, upper, one)

    def g_two(lower, upper, src, first):
        def one(i):
            g_core(i, 1, src, first).wait()
            g_core(i, 0, s.placed, 0).wait()
            mine = src[rows_at(first + (2 * i + core) * PAIR, PAIR), :].astype(F32)
            s.g.mrg1[i] = (mine + s.g.sib1[i].astype(F32)).astype(BF)
            g_x(i).start()

        loop(lower, upper, one)

    def g_three(lower, upper):
        def one(i):
            g_x(i).wait()
            mine = s.placed[rows_at((2 * i + core) * PAIR, PAIR), :].astype(F32)
            total = mine + s.sib[i].astype(F32) + s.g.xin[i].astype(F32)
            s.mrg[i] = total.astype(BF)
            g_far(i).start()

        loop(lower, upper, one)

    def g_four(lower, upper):
        def one(i):
            g_far(i).wait()
            total = s.mrg[i].astype(F32) + s.g.far[i].astype(F32)
            s.g.fin[rows_at((2 * i + core) * PAIR, PAIR), :] = total.astype(BF)
            g_back(i, core).start()

        loop(lower, upper, one)

    def g_end(lower, upper):
        def one(i):
            g_back(i, core).wait_send()
            g_back(i, 1 - core).wait_recv()

        loop(lower, upper, one)

    place(0, qkv_pairs, shift_qkv)
    place(qkv_pairs, 2 * head_part, shift_rest)
    w_one(0, head_part)
    place(wide_pairs, wide_pairs + mod_pairs, -wide_pairs)
    place(wide_pairs + mod_pairs, all_pairs, -wide_pairs + qkv_pairs)

    for i in range(1, n_dp):
        tok_copy(i, lax.rem(dp - i + n_dp, n_dp)).wait_recv()
    for i in range(3):
        cols = D // 3
        s.mod_prod[:, i * cols : (i + 1) * cols] = nt(
            s.tok_all[...], s.placed[z.wide + i * cols : z.wide + (i + 1) * cols, :]
        )
    for group in range(n_dp):
        for i in range(D // 128):
            s.mod_pack[group, i : i + 1, :] = s.mod_prod[
                16 * group : 16 * group + 1, 128 * i : 128 * (i + 1)
            ]

    def mod_copy(i):
        group = lax.rem(dp + i, n_dp)
        return remote(
            s.mod_pack.at[group],
            s.mod_recv.at[i - 1],
            s.mod_s.at[i - 1],
            s.mod_r.at[i - 1],
            (group, t),
        )

    for i in range(1, n_dp):
        go(mod_copy(i))
    w_two(0, head_part)
    place(2 * head_part, wide_pairs, shift_rest)
    w_one(head_part, half)
    for i in range(1, n_dp):
        mod_copy(i).wait_recv()
    s.mod_all[t] = s.mod_pack[dp] + s.mod_recv[0] + s.mod_recv[1] + s.mod_recv[2]

    def mod_all_copy(i, member):
        block = s.mod_all.at[member]
        return remote(
            block,
            block,
            s.moda_s.at[i - 1],
            s.moda_r.at[i - 1],
            (dp, lax.rem(t + i, n_t)),
        )

    for i in range(1, n_t):
        go(mod_all_copy(i, t))
    w_two(head_part, half)
    for i in range(1, n_t):
        mod_all_copy(i, lax.rem(t - i + n_t, n_t)).wait_recv()

    lane = lax.broadcasted_iota(jnp.int32, (8, D), 1)

    def spread(vector):
        return jnp.broadcast_to(vector, (8, D))

    def unpack_rows(block):
        return jnp.concatenate([block[i : i + 1, :] for i in range(block.shape[0])], axis=1)

    for index, member in enumerate((t, t + 1 - 2 * xb)):
        line = spread(unpack_rows(s.mod_all[member][0 : D // 128, :]))
        moved = pltpu.roll(line, D - z.mod_rows, 1)
        s.time_qv[:, 512 * index : 512 * index + 256] = moved[:, 0:256]
        moved = pltpu.roll(line, D - z.mod_rows - hc, 1)
        s.time_qv[:, 512 * index + 256 : 512 * index + 512] = moved[:, 0:256]
    lines = [jnp.zeros((8, D), F32) for _ in range(6)]
    for member in range(n_t):
        first = member * z.mod_rows
        line = jnp.concatenate(
            [s.mod_all[member, i : i + 1, :] for i in range(8)]
            + [jnp.zeros((1, D - 1024), F32)],
            axis=1,
        )
        line = spread(line)
        for piece in range(6):
            lower = max(first, piece * D) - piece * D
            upper = min(first + z.mod_rows, (piece + 1) * D) - piece * D
            if lower < upper:
                moved = pltpu.roll(line, (first - piece * D) % D, 1) if (first - piece * D) % D else line
                lines[piece] = jnp.where((lane >= lower) & (lane < upper), moved, lines[piece])
    for piece in range(6):
        s.modv[piece : piece + 1, :] = lines[piece][0:1, :]

    def mod_line(piece):
        return s.modv[piece : piece + 1, :]

    def norm_parts(values):
        centred = values - jnp.mean(values, axis=-1, keepdims=True)
        inverse = lax.rsqrt(jnp.mean(centred * centred, axis=-1, keepdims=True) + eps_norm)
        return centred * inverse, inverse

    count_sum = counts[0]
    for i in range(1, n_dp):
        count_sum = count_sum + counts[i]
    group_scale = jnp.full((1, 1), counts[dp], jnp.int32).astype(F32) * n_dp / jnp.full(
        (1, 1), count_sum, jnp.int32
    ).astype(F32)

    live = (jnp.full((1, 1), xb, jnp.int32) < held[0]).astype(F32)
    for load in image_loads:
        load.wait()

    def mix_tile(i, carry):
        at = rows_at(i * TILE, TILE)
        normed, _ = norm_parts(s.x[at, :].astype(F32))
        s.u[at, :] = (normed * (1.0 + mod_line(1)) + mod_line(0)).astype(BF)
        dy = s.grad[at, :].astype(F32) * (group_scale * live)
        s.dmlp[at, :] = (mod_line(5) * dy).astype(BF)
        return carry

    lax.fori_loop(0, z.seq // TILE, mix_tile, 0)

    sets = range(2)
    weights = []
    for ref in (s.w.fin, s.w.oth):
        q, k, v, p = (ref.at[i * hc : (i + 1) * hc] for i in range(4))
        up = ref.at[4 * hc : 4 * hc + fc]
        down = ref.at[4 * hc + fc : 4 * hc + 2 * fc]
        weights.append(SimpleNamespace(q=q, k=k, v=v, p=p, up=up, down=down))

    head_of = lax.broadcasted_iota(jnp.int32, (1, hc), 1) // HEAD_DIM

    def only(values, head):
        return jnp.where(head_of == head, values, jnp.zeros_like(values))

    scale = HEAD_DIM ** (-0.5)

    def attend(index):
        own, at = weights[index], s.heads[index]
        mixed = s.u[...]
        q_bias = s.time_qv[0:1, 512 * index : 512 * index + hc]
        v_bias = s.time_qv[0:1, 512 * index + 256 : 512 * index + 256 + hc]
        q = (nt(mixed, own.q[...]) + q_bias).astype(BF)
        k = nt(mixed, own.k[...]).astype(BF)
        v = (nt(mixed, own.v[...]) + v_bias).astype(BF)
        at.q[...] = q
        at.k[...] = k
        at.v[...] = v
        out = jnp.zeros((z.seq, hc), F32)
        for head in range(z.heads):
            scores = nt(only(q, head), k) * scale
            e = jnp.exp(scores - jnp.max(scores, axis=-1, keepdims=True))
            p = e / jnp.sum(e, axis=-1, keepdims=True)
            s.soft[index * z.heads + head] = p
            out = out + times(p.astype(BF), only(v, head))
        at.o[...] = out.astype(BF)

    sh = z.shard

    def shard_of(ref, chip):
        return ref.at[rows_at(chip * sh, sh)]

    def rs_z(ph, k):
        if k == 2:
            return remote(ph.zout, ph.zin.at[2], ph.zs.at[2], ph.zr.at[2], across)
        block = shard_of(ph.part, (cross_z, near_z)[k])
        return remote(block, ph.zin.at[k], ph.zs.at[k], ph.zr.at[k], near)

    def rs_start(ph):
        go(rs_z(ph, 0))
        go(rs_z(ph, 1))

    def rs_middle(ph):
        rs_z(ph, 0).wait_recv()
        to_far = ph.part[rows_at(far_z * sh, sh), :].astype(F32)
        ph.zout[...] = (to_far + ph.zin[0].astype(F32)).astype(BF)
        go(rs_z(ph, 2))

    def rs_end(ph):
        total = ph.part[rows_at(za * sh, sh), :].astype(F32)
        for k in (1, 2):
            rs_z(ph, k).wait_recv()
            total = total + ph.zin[k].astype(F32)
        return total

    def ag_z(ph, chip, k):
        block = shard_of(ph.buf, chip)
        return remote(block, block, ph.zs.at[k], ph.zr.at[k], across if k == 0 else near)

    def ag_x(ph, chip, k):
        source, target = shard_of(ph.buf, chip), shard_of(ph.xbuf, chip)
        return remote(source, target, ph.xs.at[k], ph.xr.at[k], xp)

    def ag_start(ph, value, out=False):
        ph.buf[rows_at(za * sh, sh), :] = value
        go(ag_z(ph, za, 0))
        go(ag_z(ph, za, 1))
        if out:
            go(ag_x(ph, za, 0))

    def ag_middle(ph, out=False):
        ag_z(ph, far_z, 0).wait_recv()
        go(ag_z(ph, far_z, 2))
        if out:
            go(ag_x(ph, far_z, 1))

    def ag_end(ph, out=False):
        ag_z(ph, near_z, 1).wait_recv()
        if out:
            go(ag_x(ph, near_z, 2))
        ag_z(ph, cross_z, 2).wait_recv()
        if out:
            go(ag_x(ph, cross_z, 3))

    def ag_end_x(ph):
        for k, chip in enumerate((za, far_z, near_z, cross_z)):
            ag_x(ph, chip, k).wait_recv()

    parts = range(z.parts)
    quarter = (half - head_part) // 4

    def part_at(part):
        return slice(part * z.part_rows, (part + 1) * z.part_rows)

    w_three(0, head_part)
    w_end_own(0, head_part)
    attend(0)
    w_four(0, head_part)
    w_end_other(0, head_part)
    attend(1)
    for i in parts:
        total = 0.0
        for index in sets:
            total = total + times(s.heads[index].o[part_at(i), :], weights[index].p[...])
        s.rs1[i].part[...] = total.astype(BF)
        rs_start(s.rs1[i])
    w_three(head_part, head_part + 2 * quarter)
    for i in parts:
        rs_middle(s.rs1[i])

    def mine_at(part):
        return rows_at(part * z.part_rows + za * sh, sh)

    w_four(head_part, head_part + quarter)
    for i in parts:
        attn = rs_end(s.rs1[i])
        h1 = s.x[mine_at(i), :].astype(F32) + mod_line(2) * attn
        normed_m, _ = norm_parts(h1)
        ag_start(s.ag1[i], (normed_m * (1.0 + mod_line(4)) + mod_line(3)).astype(BF))
        s.attn[i] = attn
        s.h1[i] = h1
    w_three(head_part + 2 * quarter, half)
    for i in parts:
        ag_middle(s.ag1[i])
    w_four(head_part + quarter, half)
    w_end_own(head_part, half)
    w_end_other(head_part, half)

    for index in sets:
        s.hid[index].dgact[...] = nt(s.dmlp[...], weights[index].down[...])

    def mlp(part):
        at = part_at(part)
        total = 0.0
        for index in sets:
            hid = s.hid[index]
            hidden = nt(s.ag1[part].buf[...], weights[index].up[...])
            square = hidden * hidden
            bend = jnp.tanh(GELU_C * hidden * (1.0 + GELU_K * square))
            hid.gact[at, :] = (0.5 * hidden * (1.0 + bend)).astype(BF)
            slope = 0.5 * (1.0 + bend) + 0.5 * hidden * (1.0 - bend * bend) * (
                GELU_C * (1.0 + 3.0 * GELU_K * square)
            )
            dz = (hid.dgact[at, :] * slope).astype(BF)
            hid.dz[at, :] = dz
            total = total + times(dz, weights[index].up[...])
        s.rs2[part].part[...] = total.astype(BF)

    def down(part):
        total = 0.0
        for index in sets:
            total = total + times(s.hid[index].gact[part_at(part), :], weights[index].down[...])
        s.rs4[part].part[...] = total.astype(BF)

    for i in parts:
        ag_end(s.ag1[i])
        mlp(i)
        rs_start(s.rs2[i])

    cols = 384

    def over_parts(left, gathered, at):
        total = 0.0
        for part in parts:
            total = total + tn(left[part_at(part), :], gathered[part].buf[:, at])
        return total.astype(BF)

    def grad_tile(i, carry):
        at = pl.ds(pl.multiple_of(i * cols, 128), cols)
        for index, first in ((1, z.wide), (0, 4 * hc)):
            hid = s.hid[index]
            s.placed[first : first + fc, at] = over_parts(hid.dz, s.ag1, at)
            down_grad = tn(hid.gact[...], s.dmlp[:, at]).astype(BF)
            s.placed[first + fc : first + 2 * fc, at] = down_grad
        return carry

    lax.fori_loop(0, D // cols, grad_tile, 0)
    first_one = z.wide - 4 * hc
    g_one(head_part, half, s.placed, first_one)
    for i in parts:
        rs_middle(s.rs2[i])
    g_two(head_part, half, s.placed, first_one)
    for i in parts:
        down(i)

    def norm_back_of(normed, inverse, upstream):
        return inverse * (
            upstream
            - jnp.mean(upstream, axis=-1, keepdims=True)
            - normed * jnp.mean(upstream * normed, axis=-1, keepdims=True)
        )

    def column_sum(values):
        return jnp.sum(values, axis=0, keepdims=True)

    def dy_of(part):
        return s.grad[mine_at(part), :].astype(F32) * (group_scale * live)

    step = (half - head_part) // 6
    g_three(head_part, head_part + step)
    gate_a_sum = shift_m_sum = scale_m_sum = 0.0
    for i in parts:
        dw = rs_end(s.rs2[i])
        normed_m, inverse_m = norm_parts(s.h1[i])
        dh1 = dy_of(i) + norm_back_of(normed_m, inverse_m, dw * (1.0 + mod_line(4)))
        ag_start(s.ag2[i], (mod_line(2) * dh1).astype(BF))
        s.dh1[i] = dh1
        gate_a_sum = gate_a_sum + column_sum(dh1 * s.attn[i])
        shift_m_sum = shift_m_sum + column_sum(dw)
        scale_m_sum = scale_m_sum + column_sum(dw * normed_m)
    s.dmod[2:3, :] = gate_a_sum
    s.dmod[3:4, :] = shift_m_sum
    s.dmod[4:5, :] = scale_m_sum
    g_three(head_part + step, head_part + 2 * step)
    for i in parts:
        ag_middle(s.ag2[i])
    for i in parts:
        rs_start(s.rs4[i])
    g_three(head_part + 2 * step, head_part + 3 * step)

    def attend_back(index):
        own, at = weights[index], s.heads[index]
        do = jnp.concatenate([nt(s.ag2[i].buf[...], own.p[...]) for i in parts], axis=0)
        do = do.astype(BF)
        q, k, v = at.q[...], at.k[...], at.v[...]
        dq = jnp.zeros((z.seq, hc), F32)
        dk = jnp.zeros((z.seq, hc), F32)
        dv = jnp.zeros((z.seq, hc), F32)
        for head in range(z.heads):
            p = s.soft[index * z.heads + head]
            do_head = only(do, head)
            dp_soft = nt(do_head, v)
            inner = jnp.sum(p * dp_soft, axis=-1, keepdims=True)
            ds = (p * (dp_soft - inner)).astype(BF)
            dq = dq + times(ds, only(k, head))
            dk = dk + tn(ds, only(q, head))
            dv = dv + tn(p.astype(BF), do_head)
        at.dq[...] = (dq * scale).astype(BF)
        at.dk[...] = (dk * scale).astype(BF)
        at.dv[...] = dv.astype(BF)

    for i in parts:
        ag_end(s.ag2[i])
    for index in sets:
        attend_back(index)
    for i in parts:
        total = 0.0
        for index in sets:
            own, at = weights[index], s.heads[index]
            rows = part_at(i)
            total = total + times(at.dq[rows, :], own.q[...])
            total = total + times(at.dk[rows, :], own.k[...])
            total = total + times(at.dv[rows, :], own.v[...])
        s.rs3[i].part[...] = total.astype(BF)
        rs_start(s.rs3[i])
    for i in parts:
        rs_middle(s.rs4[i])

    def attn_grad_tile(i, carry):
        at = pl.ds(pl.multiple_of(i * cols, 128), cols)
        mixed = s.u[:, at]
        for index, target in ((1, s.extra), (0, s.placed)):
            own = s.heads[index]
            target[0:hc, at] = tn(own.dq[...], mixed).astype(BF)
            target[hc : 2 * hc, at] = tn(own.dk[...], mixed).astype(BF)
            target[2 * hc : 3 * hc, at] = tn(own.dv[...], mixed).astype(BF)
            target[3 * hc : 4 * hc, at] = over_parts(own.o, s.ag2, at)
        return carry

    lax.fori_loop(0, D // cols, attn_grad_tile, 0)
    g_one(0, head_part, s.extra, 0)
    for i in parts:
        rs_middle(s.rs3[i])
    g_two(0, head_part, s.extra, 0)

    def dsum_copy():
        return remote(s.dsum, s.dsum_in, s.dsum_s.at[0], s.dsum_r.at[0], xp)

    s.dsum[...] = jnp.zeros((8, 256), F32)
    s.dsum[0:1, 0:hc] = column_sum(s.heads[1].dq[...].astype(F32))
    s.dsum[1:2, 0:hc] = column_sum(s.heads[1].dv[...].astype(F32))
    go(dsum_copy())
    g_three(head_part + 3 * step, head_part + 5 * step)

    shift_a_sum = scale_a_sum = gate_m_sum = 0.0
    for i in parts:
        du = rs_end(s.rs3[i])
        normed_a, inverse_a = norm_parts(s.x[mine_at(i), :].astype(F32))
        dx = s.dh1[i] + norm_back_of(normed_a, inverse_a, du * (1.0 + mod_line(1)))
        ag_start(s.ag3[i], dx.astype(BF), True)
        shift_a_sum = shift_a_sum + column_sum(du)
        scale_a_sum = scale_a_sum + column_sum(du * normed_a)
    for i in parts:
        mlp_sum = rs_end(s.rs4[i])
        gate_m_sum = gate_m_sum + column_sum(dy_of(i) * mlp_sum)
        result = (s.h1[i] + mod_line(5) * mlp_sum) * live
        ag_start(s.ag4[i], result.astype(BF), True)
    s.dmod[0:1, :] = shift_a_sum
    s.dmod[1:2, :] = scale_a_sum
    s.dmod[5:6, :] = gate_m_sum
    s.dmod[6:8, :] = jnp.zeros((2, D), F32)

    dlines = [spread(s.dmod[i : i + 1, :]) for i in range(6)]
    for member in range(n_t):
        first = member * z.mod_rows
        line = jnp.zeros((8, D), F32)
        for piece in range(6):
            lower = max(first, piece * D) - first
            upper = min(first + z.mod_rows, (piece + 1) * D) - first
            if lower < upper:
                back = (piece * D - first) % D
                moved = pltpu.roll(dlines[piece], back, 1) if back else dlines[piece]
                line = jnp.where((lane >= lower) & (lane < upper), moved, line)
        for i in range(8):
            s.dmod_pack[member, i : i + 1, :] = line[0:1, 128 * i : 128 * (i + 1)]

    def dmod_copy(i):
        member = lax.rem(t + i, n_t)
        return remote(
            s.dmod_pack.at[member],
            s.dmod_recv.at[i - 1],
            s.dmod_s.at[i - 1],
            s.dmod_r.at[i - 1],
            (dp, member),
        )

    for i in range(1, n_t):
        go(dmod_copy(i))
    g_three(head_part + 5 * step, half)
    for i in parts:
        ag_middle(s.ag3[i], True)
        ag_middle(s.ag4[i], True)
    g_three(0, head_part)
    g_four(head_part, half)
    for i in parts:
        ag_end(s.ag3[i], True)
        ag_end(s.ag4[i], True)
    dsum_copy().wait_recv()
    total = s.dmod_pack[t]
    for i in range(1, n_t):
        dmod_copy(i).wait_recv()
        total = total + s.dmod_recv[i - 1]
    s.vec[dp] = jnp.zeros((16, 256), F32)
    s.vec[dp, 0:8, 0:128] = total
    own_sums = (column_sum(s.heads[0].dq[...].astype(F32)), column_sum(s.heads[0].dv[...].astype(F32)))
    s.vec[dp, 8:9, 0:hc] = own_sums[0] + s.dsum_in[0:1, 0:hc]
    s.vec[dp, 9:10, 0:hc] = own_sums[1] + s.dsum_in[1:2, 0:hc]

    def vec_copy(i, group):
        return remote(
            s.vec.at[group],
            s.vec.at[group],
            s.vec_s.at[i - 1],
            s.vec_r.at[i - 1],
            (lax.rem(dp + i, n_dp), t),
        )

    for i in range(1, n_dp):
        go(vec_copy(i, dp))
    g_four(0, head_part)
    g_end(0, half)
    for i in parts:
        ag_end_x(s.ag3[i])
        ag_end_x(s.ag4[i])
    for i in range(1, n_dp):
        vec_copy(i, lax.rem(dp - i + n_dp, n_dp)).wait_recv()
    for copy in pending:
        copy.wait_send()

    outs = [(s.g.fin, out_g), (s.vec, out_vec), (s.tok_all, out_tok)]
    for i in parts:
        at = pl.ds(i * z.part_rows, z.part_rows)
        for ph, out in ((s.ag4[i], out_bo), (s.ag3[i], out_ig)):
            outs.append((ph.buf, out.at[xb, at]))
            outs.append((ph.xbuf, out.at[1 - xb, at]))
    stores = [
        pltpu.make_async_copy(src, dst, s.out_sem.at[i]) for i, (src, dst) in enumerate(outs)
    ]
    for store in stores:
        store.start()
    for store in stores:
        store.wait()


def update_kernel(z, group_slots, owners, grads, table, tokens, master, first, second, new_first, new_second, new_master, bos):
    step = pl.program_id(0)
    dp = lax.axis_index("dp")

    @pl.when(step == 0)
    def _():
        def clear(slot, carry):
            bos[slot] = -1
            return carry

        lax.fori_loop(0, z.slots, clear, 0)

        def note(block, taken):
            mine = owners[block] == dp

            @pl.when(mine & (taken < z.slots))
            def _():
                bos[taken] = block

            return taken + mine.astype(jnp.int32)

        lax.fori_loop(0, z.blocks, note, jnp.int32(0))

    rows = z.block_rows
    mod_blocks = z.mod_rows // rows
    head_blocks = z.head_cols // rows
    fix_one = 1.0 - beta_one**STEP
    fix_two = 1.0 - beta_two**STEP

    def put(i, grad):
        weight = master[i]
        one = beta_one * first[i] + (1.0 - beta_one) * grad
        two = beta_two * second[i] + (1.0 - beta_two) * grad * grad
        new_first[i] = one
        new_second[i] = two
        spread = two * (1.0 / fix_two)
        root = spread * lax.rsqrt(spread)
        change = one * (1.0 / fix_one) * pltpu.reciprocal(root + eps_adam) + decay_rate * weight
        new_master[i] = weight - learn_rate * change

    def slot(i, carry):
        block = bos[step * group_slots + i]
        is_mod = block < mod_blocks
        is_time = (block >= mod_blocks + 3 * head_blocks) & (block < mod_blocks + 5 * head_blocks)

        @pl.when(block < 0)
        def _():
            new_first[i] = jnp.zeros((rows, D), F32)
            new_second[i] = jnp.zeros((rows, D), F32)
            new_master[i] = jnp.zeros((rows, D), F32)

        @pl.when((block >= 0) & (is_mod | is_time))
        def _():
            index = jnp.where(is_mod, block, block - 3 * head_blocks)
            columns = table[index]
            grad = columns[:, 0:1] * tokens[0:1, :].astype(F32)
            for group in range(1, z.dp_count):
                grad = grad + columns[:, group : group + 1] * tokens[
                    16 * group : 16 * group + 1, :
                ].astype(F32)
            put(i, grad)

        @pl.when((block >= 0) & jnp.logical_not(is_mod | is_time))
        def _():
            index = jnp.where(
                block < mod_blocks + 3 * head_blocks,
                block - mod_blocks,
                block - mod_blocks - 2 * head_blocks,
            )
            both = grads[rows_at(index // 2 * PAIR, PAIR), :].astype(F32)
            put(i, jnp.where(lax.rem(index, 2) == 0, both[:rows], both[rows:]))

        return carry

    lax.fori_loop(0, group_slots, slot, 0)


def per_device_fast(
    z,
    inputs,
    out_grad,
    bucket,
    counts,
    images_held,
    owners,
    master_weight,
    first_moment,
    second_moment,
):
    token = jnp.broadcast_to(time_token(bucket[0]).astype(BF)[None, :], (16, D))
    plan = scratch_plan(z)
    smem = pl.BlockSpec(memory_space=pltpu.SMEM)
    vmem = pl.BlockSpec(memory_space=pltpu.VMEM)
    hbm = pl.BlockSpec(memory_space=pl.ANY)
    flops = 12 * z.seq * D * z.wide
    block_output, input_grad, grads, vectors, tokens = pl.pallas_call(
        partial(layer_kernel, z, plan),
        out_shape=(
            jax.ShapeDtypeStruct(inputs.shape, BF),
            jax.ShapeDtypeStruct(inputs.shape, BF),
            jax.ShapeDtypeStruct((z.wide, D), BF),
            jax.ShapeDtypeStruct((z.dp_count, 16, 256), F32),
            jax.ShapeDtypeStruct((16 * z.dp_count, D), BF),
        ),
        in_specs=[smem, smem, smem, vmem, hbm, hbm, hbm],
        out_specs=(hbm,) * 5,
        scratch_shapes=flatten(plan),
        compiler_params=pltpu.CompilerParams(
            collective_id=0, has_side_effects=True, vmem_limit_bytes=62 * 2**20
        ),
        cost_estimate=pl.CostEstimate(
            flops=flops, bytes_accessed=20 * 2**20, transcendentals=2 * z.seq * z.ffn_cols
        ),
        name="layer",
    )(
        owners,
        counts,
        images_held,
        token,
        inputs,
        out_grad,
        master_weight,
    )
    columns = jnp.concatenate(
        [
            vectors[:, :8, :128].reshape(z.dp_count, 1024)[:, : z.mod_rows],
            vectors[:, 8, : z.head_cols],
            vectors[:, 9, : z.head_cols],
        ],
        axis=1,
    ).T.reshape(z.thin // z.block_rows, z.block_rows, z.dp_count)
    group_slots = next(size for size in (15, 12, 10, 8, 6, 5, 4, 3, 2, 1) if z.slots % size == 0)
    block = pl.BlockSpec((group_slots, z.block_rows, D), lambda i: (i, 0, 0))
    state = jax.ShapeDtypeStruct(master_weight.shape, F32)
    new_first, new_second, new_master = pl.pallas_call(
        partial(update_kernel, z, group_slots),
        grid=(z.slots // group_slots,),
        out_shape=(state,) * 3,
        in_specs=[smem, vmem, vmem, vmem, block, block, block],
        out_specs=(block,) * 3,
        scratch_shapes=[pltpu.SMEM((z.slots,), jnp.int32)],
        compiler_params=pltpu.CompilerParams(vmem_limit_bytes=48 * 2**20),
        name="update",
    )(owners, grads, columns, tokens, master_weight, first_moment, second_moment)
    return (
        block_output,
        input_grad.astype(F32),
        new_first,
        new_second,
        new_master,
    )


def per_device(inputs, out_grad, bucket, counts, images_held, owners, master, first, second):
    sizes = Sizes(
        lax.axis_size("dp"),
        lax.axis_size("tensor"),
        master.shape[0],
        master.shape[1],
        inputs.shape[0],
        inputs.shape[1],
    )
    run = partial(per_device_fast, sizes) if sizes.fits() else per_device_plain
    return run(inputs, out_grad, bucket, counts, images_held, owners, master, first, second)


def solution(mesh):
    return jax.shard_map(
        per_device,
        mesh=mesh,
        in_specs=(
            P("dp", None, None),
            P("dp", None, None),
            P("dp"),
            P(),
            P("dp"),
            P(),
            P("dp", "tensor", None),
            P("dp", "tensor", None),
            P("dp", "tensor", None),
        ),
        out_specs=(
            P("dp", None, None),
            P("dp", None, None),
            P("dp", "tensor", None),
            P("dp", "tensor", None),
            P("dp", "tensor", None),
        ),
        check_vma=False,
    )
```

```python
from functools import partial
import math
from types import SimpleNamespace

import jax
import jax.numpy as jnp
from jax import lax
from jax.experimental import pallas as pl
from jax.experimental.pallas import tpu as pltpu
from jax.sharding import PartitionSpec as P

D = 1152
HEADS = 16
HEAD_DIM = 72
FF = 4608
NBUCKET = 8
STEP = 10


eps_norm = 1e-06
beta_one = 0.5
beta_two = 0.5
learn_rate = 0.03
decay_rate = 0.01
eps_adam = 1e-08


def time_token(bucket_value):
    half_width = D // 2
    freqs = jnp.exp(-math.log(10000.0) * jnp.arange(half_width, dtype=jnp.float32) / half_width)
    instant = (bucket_value.astype(jnp.float32) + 0.5) * (1000.0 / NBUCKET)
    angles = instant * freqs
    embed = jnp.concatenate([jnp.cos(angles), jnp.sin(angles)])
    return embed * jax.nn.sigmoid(embed)


def norm_stats(values):
    centred = values - jnp.mean(values, axis=-1, keepdims=True)
    inverse = lax.rsqrt(jnp.mean(centred * centred, axis=-1, keepdims=True) + eps_norm)
    return (centred * inverse, inverse)


def norm_back(normed, inverse, upstream):
    return inverse * (
        upstream
        - jnp.mean(upstream, axis=-1, keepdims=True)
        - normed * jnp.mean(upstream * normed, axis=-1, keepdims=True)
    )


def times_transposed(left, right):
    return lax.dot_general(
        left, right, (((1,), (1,)), ((), ())), preferred_element_type=jnp.float32
    )


def transposed_times(left, right):
    return lax.dot_general(
        left, right, (((0,), (0,)), ((), ())), preferred_element_type=jnp.float32
    )


def attend_forward(block):
    queries, key_rows, values = block
    scores = jnp.einsum(
        "bqhd,bkhd->bhqk", queries, key_rows, preferred_element_type=jnp.float32
    ) * HEAD_DIM ** (-0.5)
    row_peak = jnp.max(scores, axis=-1, keepdims=True)
    exp_scores = jnp.exp(scores - row_peak)
    row_total = jnp.sum(exp_scores, axis=-1, keepdims=True)
    soft = (exp_scores / row_total).astype(jnp.bfloat16)
    attended = jnp.einsum("bhqk,bkhd->bqhd", soft, values, preferred_element_type=jnp.float32)
    return (attended, row_peak[..., 0] + jnp.log(row_total[..., 0]))


def attend_backward(block):
    queries, key_rows, values, log_total, upstream = block
    scale_factor = HEAD_DIM ** (-0.5)
    scores = (
        jnp.einsum("bqhd,bkhd->bhqk", queries, key_rows, preferred_element_type=jnp.float32)
        * scale_factor
    )
    soft = jnp.exp(scores - log_total[..., None])
    grad_soft = jnp.einsum("bqhd,bkhd->bhqk", upstream, values, preferred_element_type=jnp.float32)
    inner_sum = jnp.sum(soft * grad_soft, axis=-1, keepdims=True)
    grad_scores = (soft * (grad_soft - inner_sum)).astype(jnp.bfloat16)
    grad_query = (
        jnp.einsum("bhqk,bkhd->bqhd", grad_scores, key_rows, preferred_element_type=jnp.float32)
        * scale_factor
    )
    grad_key = (
        jnp.einsum("bhqk,bqhd->bkhd", grad_scores, queries, preferred_element_type=jnp.float32)
        * scale_factor
    )
    grad_value = jnp.einsum(
        "bhqk,bqhd->bkhd", soft.astype(jnp.bfloat16), upstream, preferred_element_type=jnp.float32
    )
    return (grad_query, grad_key, grad_value)


def per_device_plain(
    inputs,
    out_grad,
    bucket,
    counts,
    images_held,
    owners,
    master_weight,
    first_moment,
    second_moment,
):
    dp_count = lax.axis_size("dp")
    tensor_count = lax.axis_size("tensor")
    dp_rank = lax.axis_index("dp")
    tensor_rank = lax.axis_index("tensor")
    own_slots = master_weight.shape[0]
    block_rows = master_weight.shape[1]
    head_cols = D // tensor_count
    ffn_cols = FF // tensor_count
    local_heads = HEADS // tensor_count
    local_rows = 12 * head_cols + 2 * ffn_cols
    block_count = local_rows // block_rows
    image_count = inputs.shape[0]
    seq_len = inputs.shape[1]
    row_count = image_count * seq_len
    block_ids = jnp.arange(block_count, dtype=jnp.int32)
    earlier = (owners[None, :] == owners[:, None]) & (block_ids[None, :] < block_ids[:, None])
    slot_of = owners * own_slots + jnp.sum(earlier.astype(jnp.int32), axis=1)
    gathered = lax.all_gather(master_weight.astype(jnp.bfloat16), "dp", axis=0, tiled=True)
    weights = gathered[slot_of].reshape(local_rows, D)
    w_mod = weights[: 6 * head_cols]
    w_qkv = weights[6 * head_cols : 9 * head_cols]
    w_qtime = weights[9 * head_cols : 10 * head_cols]
    w_vtime = weights[10 * head_cols : 11 * head_cols]
    w_proj = weights[11 * head_cols : 12 * head_cols]
    w_up = weights[12 * head_cols : 12 * head_cols + ffn_cols]
    w_down = weights[12 * head_cols + ffn_cols :]
    token = time_token(bucket[0]).astype(jnp.bfloat16)
    token_wide = token.astype(jnp.float32)
    mod_piece = jnp.dot(w_mod, token, preferred_element_type=jnp.float32)
    modulation = lax.all_gather(mod_piece, "tensor", axis=0, tiled=True)
    shift_a, scale_a, gate_a, shift_m, scale_m, gate_m = jnp.split(modulation, 6)
    counts_f = counts.astype(jnp.float32)
    group_scale = counts_f[dp_rank] * dp_count / jnp.sum(counts_f)
    flat_rows = inputs.reshape(row_count, D).astype(jnp.float32)
    live = (jnp.arange(row_count, dtype=jnp.int32) // seq_len < images_held[0]).astype(jnp.float32)[
        :, None
    ]
    normed_a, inverse_a = norm_stats(flat_rows)
    mixed_a = (normed_a * (1.0 + scale_a) + shift_a).astype(jnp.bfloat16)
    projected = times_transposed(mixed_a, w_qkv)
    time_query = jnp.dot(w_qtime, token, preferred_element_type=jnp.float32)
    time_value = jnp.dot(w_vtime, token, preferred_element_type=jnp.float32)
    queries = (projected[:, :head_cols] + time_query).astype(jnp.bfloat16)
    key_rows = projected[:, head_cols : 2 * head_cols].astype(jnp.bfloat16)
    values = (projected[:, 2 * head_cols :] + time_value).astype(jnp.bfloat16)
    group_imgs = math.gcd(image_count, max(1, 512 // seq_len))
    block_shape = (image_count // group_imgs, group_imgs, seq_len, local_heads, HEAD_DIM)
    q_blocks = queries.reshape(block_shape)
    k_blocks = key_rows.reshape(block_shape)
    v_blocks = values.reshape(block_shape)
    attended, log_total = lax.map(attend_forward, (q_blocks, k_blocks, v_blocks))
    heads_out = attended.reshape(row_count, head_cols).astype(jnp.bfloat16)
    heads_share = lax.psum_scatter(
        jnp.dot(heads_out, w_proj, preferred_element_type=jnp.float32).astype(jnp.bfloat16),
        "tensor",
        scatter_dimension=0,
        tiled=True,
    ).astype(jnp.float32)
    branch_a = lax.all_gather(
        heads_share.astype(jnp.bfloat16), "tensor", axis=0, tiled=True
    ).astype(heads_share.dtype)
    resid = flat_rows + gate_a * branch_a
    normed_m, inverse_m = norm_stats(resid)
    mixed_m = (normed_m * (1.0 + scale_m) + shift_m).astype(jnp.bfloat16)
    hidden = times_transposed(mixed_m, w_up)
    acted = jax.nn.gelu(hidden, approximate=True).astype(jnp.bfloat16)
    hidden_share = lax.psum_scatter(
        jnp.dot(acted, w_down, preferred_element_type=jnp.float32).astype(jnp.bfloat16),
        "tensor",
        scatter_dimension=0,
        tiled=True,
    ).astype(jnp.float32)
    branch_m = lax.all_gather(
        hidden_share.astype(jnp.bfloat16), "tensor", axis=0, tiled=True
    ).astype(hidden_share.dtype)
    result = resid + gate_m * branch_m
    block_output = (result * live).astype(jnp.bfloat16).reshape(inputs.shape)
    grad_y = out_grad.reshape(row_count, D).astype(jnp.float32) * (group_scale * live)
    grad_branch_m = (gate_m * grad_y).astype(jnp.bfloat16)
    grad_gate_m = jnp.sum(grad_y * branch_m, axis=0)
    grad_acted = times_transposed(grad_branch_m, w_down)
    grad_down = transposed_times(acted, grad_branch_m)
    grad_hidden = jax.vjp(partial(jax.nn.gelu, approximate=True), hidden)[1](grad_acted)[0].astype(
        jnp.bfloat16
    )
    grad_up = transposed_times(grad_hidden, mixed_m)
    mlp_grad_share = lax.psum_scatter(
        jnp.dot(grad_hidden, w_up, preferred_element_type=jnp.float32).astype(jnp.bfloat16),
        "tensor",
        scatter_dimension=0,
        tiled=True,
    ).astype(jnp.float32)
    grad_mixed_m = lax.all_gather(
        mlp_grad_share.astype(jnp.bfloat16), "tensor", axis=0, tiled=True
    ).astype(mlp_grad_share.dtype)
    grad_shift_m = jnp.sum(grad_mixed_m, axis=0)
    grad_scale_m = jnp.sum(grad_mixed_m * normed_m, axis=0)
    grad_resid = grad_y + norm_back(normed_m, inverse_m, grad_mixed_m * (1.0 + scale_m))
    grad_branch_a = (gate_a * grad_resid).astype(jnp.bfloat16)
    grad_gate_a = jnp.sum(grad_resid * branch_a, axis=0)
    grad_heads = times_transposed(grad_branch_a, w_proj).astype(jnp.bfloat16)
    grad_proj = transposed_times(heads_out, grad_branch_a)
    grads_query, grads_key, grads_value = lax.map(
        attend_backward, (q_blocks, k_blocks, v_blocks, log_total, grad_heads.reshape(block_shape))
    )
    grad_qkv = jnp.concatenate(
        [
            grads_query.reshape(row_count, head_cols),
            grads_key.reshape(row_count, head_cols),
            grads_value.reshape(row_count, head_cols),
        ],
        axis=1,
    ).astype(jnp.bfloat16)
    grad_wqkv = transposed_times(grad_qkv, mixed_a)
    attn_grad_share = lax.psum_scatter(
        jnp.dot(grad_qkv, w_qkv, preferred_element_type=jnp.float32).astype(jnp.bfloat16),
        "tensor",
        scatter_dimension=0,
        tiled=True,
    ).astype(jnp.float32)
    grad_mixed_a = lax.all_gather(
        attn_grad_share.astype(jnp.bfloat16), "tensor", axis=0, tiled=True
    ).astype(attn_grad_share.dtype)
    token_sums = jnp.sum(grad_qkv, axis=0, dtype=jnp.float32)
    grad_qtime = token_sums[:head_cols, None] * token_wide[None, :]
    grad_vtime = token_sums[2 * head_cols :, None] * token_wide[None, :]
    grad_shift_a = jnp.sum(grad_mixed_a, axis=0)
    grad_scale_a = jnp.sum(grad_mixed_a * normed_a, axis=0)
    grad_in = grad_resid + norm_back(normed_a, inverse_a, grad_mixed_a * (1.0 + scale_a))
    grad_mod = jnp.concatenate(
        [grad_shift_a, grad_scale_a, grad_gate_a, grad_shift_m, grad_scale_m, grad_gate_m]
    )
    grad_mod_piece = lax.dynamic_slice_in_dim(grad_mod, tensor_rank * 6 * head_cols, 6 * head_cols)
    grad_wmod = grad_mod_piece[:, None] * token_wide[None, :]
    grads = jnp.concatenate(
        [grad_wmod, grad_wqkv, grad_qtime, grad_vtime, grad_proj, grad_up, grad_down], axis=0
    )
    grad_blocks = grads.reshape(block_count, block_rows, D)
    owned_blocks = jnp.full((dp_count * own_slots,), -1, jnp.int32).at[slot_of].set(block_ids)
    mine = lax.dynamic_slice_in_dim(owned_blocks, dp_rank * own_slots, own_slots)
    filled = (mine >= 0)[:, None, None]
    placed = (
        jnp.zeros((dp_count * own_slots, block_rows, D), jnp.float32).at[slot_of].set(grad_blocks)
    )
    reduced = lax.psum_scatter(
        placed.astype(jnp.bfloat16), "dp", scatter_dimension=0, tiled=True
    ).astype(jnp.float32)
    new_first = beta_one * first_moment + (1.0 - beta_one) * reduced
    new_second = beta_two * second_moment + (1.0 - beta_two) * reduced * reduced
    fix_one = 1.0 - beta_one**STEP
    fix_two = 1.0 - beta_two**STEP
    change = (
        new_first / fix_one / (jnp.sqrt(new_second / fix_two) + eps_adam)
        + decay_rate * master_weight
    )
    new_master = master_weight - learn_rate * change
    return (
        block_output,
        grad_in.reshape(inputs.shape),
        jnp.where(filled, new_first, 0.0),
        jnp.where(filled, new_second, 0.0),
        jnp.where(filled, new_master, 0.0),
    )


BF = jnp.bfloat16
F32 = jnp.float32
MESH = pl.DeviceIdType.MESH
axes = ("dp", "tensor")
TILE = 64
LAG = 2
PAIR = 48
GELU_C = math.sqrt(2.0 / math.pi)
GELU_K = 0.044715


def rows_at(start, size):
    return pl.ds(pl.multiple_of(start, 16), size)


def remote(src, dst, send_sem, recv_sem, device):
    return pltpu.make_async_remote_copy(
        src_ref=src,
        dst_ref=dst,
        send_sem=send_sem,
        recv_sem=recv_sem,
        device_id=device,
        device_id_type=MESH,
    )


def times(left, right):
    return jnp.dot(left, right, preferred_element_type=F32)


class Sizes:
    def __init__(self, dp_count, tensor_count, slots, block_rows, images, seq):
        self.dp_count, self.tensor_count = dp_count, tensor_count
        self.slots, self.block_rows = slots, block_rows
        self.images, self.seq = images, seq
        self.parts = 2
        self.part_rows = seq // self.parts
        self.shard = self.part_rows // 4
        self.head_cols = D // tensor_count
        self.ffn_cols = FF // tensor_count
        self.heads = HEADS // tensor_count
        self.mod_rows = 6 * self.head_cols
        self.local_rows = 12 * self.head_cols + 2 * self.ffn_cols
        self.blocks = self.local_rows // block_rows
        self.wide = 4 * self.head_cols + 2 * self.ffn_cols
        self.thin = self.mod_rows + 2 * self.head_cols

    def fits(self):
        return (
            self.dp_count == 4
            and self.tensor_count == 8
            and self.images == 2
            and 2 * self.block_rows == PAIR
            and self.slots % 3 == 0
            and self.seq % 128 == 0
            and self.head_cols % PAIR == 0
            and self.ffn_cols % PAIR == 0
            and self.wide % (6 * PAIR) == 0
            and self.thin == D
            and self.thin == 2 * self.ffn_cols
            and self.mod_rows <= 1024
        )


def flatten(plan):
    if isinstance(plan, SimpleNamespace):
        return flatten(list(vars(plan).values()))
    if isinstance(plan, list):
        return [leaf for member in plan for leaf in flatten(member)]
    return [plan]


def rebuild(plan, leaves):
    if isinstance(plan, SimpleNamespace):
        return SimpleNamespace(**{key: rebuild(value, leaves) for key, value in vars(plan).items()})
    if isinstance(plan, list):
        return [rebuild(member, leaves) for member in plan]
    return next(leaves)


def scratch_plan(z):
    dma = pltpu.SemaphoreType.DMA
    vm = pltpu.VMEM
    half = z.wide // PAIR // 2

    def pairs():
        return vm((half, PAIR, D), BF)

    def attention():
        names = 7
        q, k, v, o, dq, dk, dv = (vm((z.seq, z.head_cols), BF) for _ in range(names))
        return SimpleNamespace(q=q, k=k, v=v, o=o, dq=dq, dk=dk, dv=dv)

    def hidden():
        return SimpleNamespace(
            slope=vm((z.seq, z.ffn_cols), F32),
            gact=vm((z.seq, z.ffn_cols), BF),
            dz=vm((z.seq, z.ffn_cols), BF),
        )

    def scatter():
        return SimpleNamespace(
            part=vm((z.part_rows, D), BF),
            zout=vm((z.shard, D), BF),
            zin=vm((3, z.shard, D), BF),
            zs=dma((3,)),
            zr=dma((3,)),
        )

    def gather():
        return SimpleNamespace(buf=vm((z.part_rows, D), BF), zs=dma((3,)), zr=dma((3,)))

    def each(make):
        return [make() for _ in range(z.parts)]

    return SimpleNamespace(
        slot_table=pltpu.SMEM((z.blocks,), jnp.int32),
        master=vm((z.slots, z.block_rows, D), F32),
        master_sem=dma((3,)),
        x=vm((z.seq, D), BF),
        grad=vm((z.seq, D), BF),
        in_sem=dma((2,)),
        placed=vm((z.wide, D), BF),
        thin=vm((z.thin, D), BF),
        extra=vm((4 * z.head_cols, D), BF),
        tok_all=vm((16 * z.dp_count, D), BF),
        tok_s=dma((3,)),
        tok_r=dma((3,)),
        mod_prod=vm((16 * z.dp_count, D), F32),
        mod_pack=vm((z.dp_count, 16, 128), F32),
        mod_recv=vm((3, 16, 128), F32),
        mod_s=dma((3,)),
        mod_r=dma((3,)),
        mod_all=vm((z.tensor_count, 16, 128), F32),
        moda_s=dma((z.tensor_count - 1,)),
        moda_r=dma((z.tensor_count - 1,)),
        modv=vm((8, D), F32),
        time_qv=vm((8, 4 * 256), F32),
        u=vm((z.seq, D), BF),
        dmlp=vm((z.seq, D), BF),
        heads=[attention(), attention()],
        soft=vm((2 * z.heads, z.seq, z.seq), F32),
        hid=[hidden(), hidden()],
        h1=vm((z.parts, z.shard, D), F32),
        attn=vm((z.parts, z.shard, D), F32),
        dh1=vm((z.parts, z.shard, D), F32),
        dmod=vm((8, D), F32),
        dmod_pack=vm((z.tensor_count, 8, 128), F32),
        dmod_recv=vm((z.tensor_count - 1, 8, 128), F32),
        dmod_s=dma((z.tensor_count - 1,)),
        dmod_r=dma((z.tensor_count - 1,)),
        dsum=vm((8, 256), F32),
        dsum_in=vm((8, 256), F32),
        dsum_s=dma((1,)),
        dsum_r=dma((1,)),
        vec=vm((z.dp_count, 16, 256), F32),
        vec_s=dma((3,)),
        vec_r=dma((3,)),
        out_sem=dma((3 + 2 * z.parts,)),
        sib=pairs(),
        mrg=pairs(),
        w=SimpleNamespace(
            far=pairs(),
            fin=vm((z.wide, D), BF),
            oth=vm((z.wide, D), BF),
            s1=dma((half,)),
            r1=dma((half,)),
            s2=dma((half,)),
            r2=dma((half,)),
            s3=dma((half,)),
            r3=dma((half,)),
            s4=dma((half,)),
            r4=dma((half,)),
            s5=dma((half,)),
            r5=dma((half,)),
        ),
        g=SimpleNamespace(
            far=pairs(),
            fin=vm((z.wide, D), BF),
            sib1=pairs(),
            mrg1=pairs(),
            xin=pairs(),
            s0=dma((half,)),
            r0=dma((half,)),
            s1=dma((half,)),
            r1=dma((half,)),
            s2=dma((half,)),
            r2=dma((half,)),
            s3=dma((half,)),
            r3=dma((half,)),
            s4=dma((half,)),
            r4=dma((half,)),
        ),
        rs1=each(scatter),
        rs2=each(scatter),
        rs3=each(scatter),
        rs4=each(scatter),
        ag1=each(gather),
        ag2=each(gather),
        ag3=each(gather),
        ag4=each(gather),
    )


def layer_kernel(z, plan, *refs):
    owners, counts, held, tok, x_hbm, grad_hbm, master_hbm = refs[:7]
    out_own, out_g, out_vec, out_tok = refs[7:11]
    s = rebuild(plan, iter(refs[11:]))
    nt_dims = (((1,), (1,)), ((), ()))
    tn_dims = (((0,), (0,)), ((), ()))

    def nt(left, right):
        return lax.dot_general(left, right, nt_dims, preferred_element_type=F32)

    def tn(left, right):
        return lax.dot_general(left, right, tn_dims, preferred_element_type=F32)

    hc, fc = z.head_cols, z.ffn_cols
    n_dp, n_t = z.dp_count, z.tensor_count
    dp, t = lax.axis_index("dp"), lax.axis_index("tensor")
    core = lax.rem(dp, 2)
    za, xb = t // 2, lax.rem(t, 2)
    near_z = za + 1 - 2 * lax.rem(za, 2)
    far_z = lax.rem(za + 2, 4)
    cross_z = 3 - za
    sib = (dp + 1 - 2 * core, t)
    far = (lax.rem(dp + 2, 4), t)
    xp = (dp, t + 1 - 2 * xb)
    near, across = (dp, 2 * near_z + xb), (dp, 2 * far_z + xb)
    half = z.wide // PAIR // 2
    head_part = (4 * hc) // PAIR // 2
    pending = []

    def go(copy):
        copy.start()
        pending.append(copy)

    third = z.slots // 3
    loads = [
        pltpu.make_async_copy(
            master_hbm.at[pl.ds(i * third, third)],
            s.master.at[pl.ds(i * third, third)],
            s.master_sem.at[i],
        )
        for i in range(3)
    ]
    image_loads = [
        pltpu.make_async_copy(x_hbm.at[xb], s.x, s.in_sem.at[0]),
        pltpu.make_async_copy(grad_hbm.at[xb], s.grad, s.in_sem.at[1]),
    ]
    for load in loads + image_loads:
        load.start()

    barrier = pltpu.get_barrier_semaphore()
    for i in range(1, n_dp):
        pl.semaphore_signal(
            barrier, inc=1, device_id=(lax.rem(dp + i, n_dp), t), device_id_type=MESH
        )
    for i in range(1, n_t):
        pl.semaphore_signal(
            barrier, inc=1, device_id=(dp, lax.rem(t + i, n_t)), device_id_type=MESH
        )
    pl.semaphore_wait(barrier, n_dp + n_t - 2)

    s.tok_all[rows_at(dp * 16, 16), :] = tok[...]

    def tok_copy(i, group):
        block = s.tok_all.at[rows_at(group * 16, 16)]
        return remote(
            block,
            block,
            s.tok_s.at[i - 1],
            s.tok_r.at[i - 1],
            (lax.rem(dp + i, n_dp), t),
        )

    for i in range(1, n_dp):
        go(tok_copy(i, dp))

    def note_slot(block, taken):
        mine = owners[block] == dp
        s.slot_table[block] = jnp.where(mine, taken, -1)
        return taken + mine.astype(jnp.int32)

    lax.fori_loop(0, z.blocks, note_slot, jnp.int32(0))
    for load in loads:
        load.wait()

    def place(into, lower, upper, shift):
        def one(pair, carry):
            halves = []
            for side in range(2):
                slot = s.slot_table[2 * (pair + shift) + side]
                block = s.master[jnp.clip(slot, 0, z.slots - 1)]
                halves.append(jnp.where(slot >= 0, block, 0.0))
            into[rows_at(pair * PAIR, PAIR), :] = jnp.concatenate(halves, axis=0).astype(BF)
            return carry

        lax.fori_loop(lower, upper, one, 0)

    qkv_pairs, mod_pairs = 3 * hc // PAIR, z.mod_rows // PAIR
    time_pairs = 2 * hc // PAIR
    wide_pairs = z.wide // PAIR
    shift_qkv = mod_pairs
    shift_rest = mod_pairs + time_pairs

    def loop(lower, upper, body):
        lax.fori_loop(lower, upper, lambda i, carry: (body(i), carry)[1], 0)

    def pair_at(ref, i, side, first=0):
        return ref.at[rows_at(first + (2 * i + side) * PAIR, PAIR)]

    def w_core(i):
        return remote(
            pair_at(s.placed, i, 1 - core), s.sib.at[i], s.w.s1.at[i], s.w.r1.at[i], sib
        )

    def w_far(i):
        return remote(s.mrg.at[i], s.w.far.at[i], s.w.s2.at[i], s.w.r2.at[i], far)

    def w_back(i, side):
        block = pair_at(s.w.fin, i, side)
        return remote(block, block, s.w.s3.at[i], s.w.r3.at[i], sib)

    def w_x(i):
        return remote(
            pair_at(s.w.fin, i, core),
            pair_at(s.w.oth, i, core),
            s.w.s4.at[i],
            s.w.r4.at[i],
            xp,
        )

    def w_pass(i, side):
        block = pair_at(s.w.oth, i, side)
        return remote(block, block, s.w.s5.at[i], s.w.r5.at[i], sib)

    def w_one(lower, upper):
        loop(lower, upper, lambda i: w_core(i).start())

    def w_two(lower, upper):
        def one(i):
            w_core(i).wait()
            mine = s.placed[rows_at((2 * i + core) * PAIR, PAIR), :].astype(F32)
            s.mrg[i] = (mine + s.sib[i].astype(F32)).astype(BF)
            w_far(i).start()

        loop(lower, upper, one)

    def w_three(i):
        w_far(i).wait()
        total = s.mrg[i].astype(F32) + s.w.far[i].astype(F32)
        s.w.fin[rows_at((2 * i + core) * PAIR, PAIR), :] = total.astype(BF)
        w_x(i).start()
        w_back(i, core).start()

    def w_four(i):
        w_x(i).wait()
        w_pass(i, core).start()

    def w_steps(lower, upper):
        for i in range(lower, upper):
            if i < half:
                w_three(i)
            if 0 <= i - LAG < half:
                w_four(i - LAG)

    def w_end_own(lower, upper):
        def one(i):
            w_back(i, core).wait_send()
            w_back(i, 1 - core).wait_recv()

        loop(lower, upper, one)

    def w_end_other(lower, upper):
        def one(i):
            w_pass(i, core).wait_send()
            w_pass(i, 1 - core).wait_recv()

        loop(lower, upper, one)

    def g_core(i, index, src, first):
        into, send, recv = ((s.sib, s.g.s0, s.g.r0), (s.g.sib1, s.g.s1, s.g.r1))[index]
        return remote(
            pair_at(src, i, 1 - core, first), into.at[i], send.at[i], recv.at[i], sib
        )

    def g_x(i):
        return remote(s.g.mrg1.at[i], s.g.xin.at[i], s.g.s2.at[i], s.g.r2.at[i], xp)

    def g_far(i):
        return remote(s.mrg.at[i], s.g.far.at[i], s.g.s3.at[i], s.g.r3.at[i], far)

    def g_back(i, side):
        block = pair_at(s.g.fin, i, side)
        return remote(block, block, s.g.s4.at[i], s.g.r4.at[i], sib)

    def g_one(index, lower, upper, src, first):
        loop(lower, upper, lambda i: g_core(i, index, src, first).start())

    def g_two(lower, upper, src, first):
        def one(i):
            g_core(i, 1, src, first).wait()
            mine = src[rows_at(first + (2 * i + core) * PAIR, PAIR), :].astype(F32)
            s.g.mrg1[i] = (mine + s.g.sib1[i].astype(F32)).astype(BF)

        loop(lower, upper, one)

    def g_two_own(lower, upper):
        loop(lower, upper, lambda i: g_core(i, 0, s.placed, 0).wait())

    def g_three(i):
        g_x(i).wait()
        mine = s.placed[rows_at((2 * i + core) * PAIR, PAIR), :].astype(F32)
        total = mine + s.sib[i].astype(F32) + s.g.xin[i].astype(F32)
        s.mrg[i] = total.astype(BF)
        g_far(i).start()

    def g_four(i):
        g_far(i).wait()
        total = s.mrg[i].astype(F32) + s.g.far[i].astype(F32)
        s.g.fin[rows_at((2 * i + core) * PAIR, PAIR), :] = total.astype(BF)
        g_back(i, core).start()

    thirds = head_part, head_part + (half - head_part) // 2, half
    g_order = list(range(thirds[1], half)) + list(range(head_part, thirds[1]))
    g_order += list(range(head_part))

    def g_steps(lower, upper):
        for k in range(lower, upper):
            if k < half:
                g_three(g_order[k])
            if k + LAG < half:
                g_x(g_order[k + LAG]).start()
            if 0 <= k - LAG < half:
                g_four(g_order[k - LAG])

    def g_end(lower, upper):
        def one(i):
            g_back(i, core).wait_send()
            g_back(i, 1 - core).wait_recv()

        loop(lower, upper, one)

    place(s.placed, 0, qkv_pairs, shift_qkv)
    place(s.placed, qkv_pairs, 2 * head_part, shift_rest)
    w_one(0, head_part)
    place(s.thin, 0, mod_pairs, 0)
    place(s.thin, mod_pairs, mod_pairs + time_pairs, qkv_pairs)


    for i in range(1, n_dp):
        tok_copy(i, lax.rem(dp - i + n_dp, n_dp)).wait_recv()
    for i in range(3):
        cols = D // 3
        s.mod_prod[:, i * cols : (i + 1) * cols] = nt(
            s.tok_all[...], s.thin[i * cols : (i + 1) * cols, :]
        )
    for group in range(n_dp):
        for i in range(D // 128):
            s.mod_pack[group, i : i + 1, :] = s.mod_prod[
                16 * group : 16 * group + 1, 128 * i : 128 * (i + 1)
            ]

    def mod_copy(i):
        group = lax.rem(dp + i, n_dp)
        return remote(
            s.mod_pack.at[group],
            s.mod_recv.at[i - 1],
            s.mod_s.at[i - 1],
            s.mod_r.at[i - 1],
            (group, t),
        )

    for i in range(1, n_dp):
        go(mod_copy(i))
    w_two(0, head_part)
    place(s.placed, 2 * head_part, wide_pairs, shift_rest)
    w_one(head_part, half)
    for i in range(1, n_dp):
        mod_copy(i).wait_recv()
    s.mod_all[t] = s.mod_pack[dp] + s.mod_recv[0] + s.mod_recv[1] + s.mod_recv[2]

    def mod_all_copy(i, member):
        block = s.mod_all.at[member]
        return remote(
            block,
            block,
            s.moda_s.at[i - 1],
            s.moda_r.at[i - 1],
            (dp, lax.rem(t + i, n_t)),
        )

    for i in range(1, n_t):
        go(mod_all_copy(i, t))
    w_two(head_part, half)
    w_steps(0, 1)
    for i in range(1, n_t):
        mod_all_copy(i, lax.rem(t - i + n_t, n_t)).wait_recv()

    lane = lax.broadcasted_iota(jnp.int32, (8, D), 1)

    def spread(vector):
        return jnp.broadcast_to(vector, (8, D))

    def unpack_rows(block):
        return jnp.concatenate([block[i : i + 1, :] for i in range(block.shape[0])], axis=1)

    for index, member in enumerate((t, t + 1 - 2 * xb)):
        line = spread(unpack_rows(s.mod_all[member][0 : D // 128, :]))
        moved = pltpu.roll(line, D - z.mod_rows, 1)
        s.time_qv[:, 512 * index : 512 * index + 256] = moved[:, 0:256]
        moved = pltpu.roll(line, D - z.mod_rows - hc, 1)
        s.time_qv[:, 512 * index + 256 : 512 * index + 512] = moved[:, 0:256]
    lines = [jnp.zeros((8, D), F32) for _ in range(6)]
    for member in range(n_t):
        first = member * z.mod_rows
        line = jnp.concatenate(
            [s.mod_all[member, i : i + 1, :] for i in range(8)]
            + [jnp.zeros((1, D - 1024), F32)],
            axis=1,
        )
        line = spread(line)
        for piece in range(6):
            lower = max(first, piece * D) - piece * D
            upper = min(first + z.mod_rows, (piece + 1) * D) - piece * D
            if lower < upper:
                moved = pltpu.roll(line, (first - piece * D) % D, 1) if (first - piece * D) % D else line
                lines[piece] = jnp.where((lane >= lower) & (lane < upper), moved, lines[piece])
    for piece in range(6):
        s.modv[piece : piece + 1, :] = lines[piece][0:1, :]

    def mod_line(piece):
        return s.modv[piece : piece + 1, :]

    def norm_parts(values):
        centred = values - jnp.mean(values, axis=-1, keepdims=True)
        inverse = lax.rsqrt(jnp.mean(centred * centred, axis=-1, keepdims=True) + eps_norm)
        return centred * inverse, inverse

    count_sum = counts[0]
    for i in range(1, n_dp):
        count_sum = count_sum + counts[i]
    group_scale = jnp.full((1, 1), counts[dp], jnp.int32).astype(F32) * n_dp / jnp.full(
        (1, 1), count_sum, jnp.int32
    ).astype(F32)

    live = (jnp.full((1, 1), xb, jnp.int32) < held[0]).astype(F32)
    for load in image_loads:
        load.wait()

    def mix_tile(i, carry):
        at = rows_at(i * TILE, TILE)
        normed, _ = norm_parts(s.x[at, :].astype(F32))
        s.u[at, :] = (normed * (1.0 + mod_line(1)) + mod_line(0)).astype(BF)
        dy = s.grad[at, :].astype(F32) * (group_scale * live)
        s.dmlp[at, :] = (mod_line(5) * dy).astype(BF)
        return carry

    w_steps(1, 2)
    lax.fori_loop(0, z.seq // TILE, mix_tile, 0)

    sets = range(2)
    weights = []
    for ref in (s.w.fin, s.w.oth):
        q, k, v, p = (ref.at[i * hc : (i + 1) * hc] for i in range(4))
        up = ref.at[4 * hc : 4 * hc + fc]
        down = ref.at[4 * hc + fc : 4 * hc + 2 * fc]
        weights.append(SimpleNamespace(q=q, k=k, v=v, p=p, up=up, down=down))

    head_of = lax.broadcasted_iota(jnp.int32, (1, hc), 1) // HEAD_DIM

    def only(values, head):
        return jnp.where(head_of == head, values, jnp.zeros_like(values))

    scale = HEAD_DIM ** (-0.5)

    def attend(index):
        own, at = weights[index], s.heads[index]
        mixed = s.u[...]
        q_bias = s.time_qv[0:1, 512 * index : 512 * index + hc]
        v_bias = s.time_qv[0:1, 512 * index + 256 : 512 * index + 256 + hc]
        q = (nt(mixed, own.q[...]) + q_bias).astype(BF)
        k = nt(mixed, own.k[...]).astype(BF)
        v = (nt(mixed, own.v[...]) + v_bias).astype(BF)
        at.q[...] = q
        at.k[...] = k
        at.v[...] = v
        out = jnp.zeros((z.seq, hc), F32)
        for head in range(z.heads):
            scores = nt(only(q, head), k) * scale
            e = jnp.exp(scores - jnp.max(scores, axis=-1, keepdims=True))
            p = e / jnp.sum(e, axis=-1, keepdims=True)
            s.soft[index * z.heads + head] = p
            out = out + times(p.astype(BF), only(v, head))
        at.o[...] = out.astype(BF)

    sh = z.shard

    def shard_of(ref, chip):
        return ref.at[rows_at(chip * sh, sh)]

    def rs_z(ph, k):
        if k == 2:
            return remote(ph.zout, ph.zin.at[2], ph.zs.at[2], ph.zr.at[2], across)
        block = shard_of(ph.part, (cross_z, near_z)[k])
        return remote(block, ph.zin.at[k], ph.zs.at[k], ph.zr.at[k], near)

    def rs_start(ph):
        go(rs_z(ph, 0))
        go(rs_z(ph, 1))

    def rs_middle(ph):
        rs_z(ph, 0).wait_recv()
        to_far = ph.part[rows_at(far_z * sh, sh), :].astype(F32)
        ph.zout[...] = (to_far + ph.zin[0].astype(F32)).astype(BF)
        go(rs_z(ph, 2))

    def rs_end(ph):
        total = ph.part[rows_at(za * sh, sh), :].astype(F32)
        for k in (1, 2):
            rs_z(ph, k).wait_recv()
            total = total + ph.zin[k].astype(F32)
        return total

    def ag_z(ph, chip, k):
        block = shard_of(ph.buf, chip)
        return remote(block, block, ph.zs.at[k], ph.zr.at[k], across if k == 0 else near)

    def ag_start(ph, value):
        ph.buf[rows_at(za * sh, sh), :] = value
        go(ag_z(ph, za, 0))
        go(ag_z(ph, za, 1))

    def ag_middle(ph):
        ag_z(ph, far_z, 0).wait_recv()
        go(ag_z(ph, far_z, 2))

    def ag_end(ph):
        ag_z(ph, near_z, 1).wait_recv()
        ag_z(ph, cross_z, 2).wait_recv()

    parts = range(z.parts)

    def part_at(part):
        return slice(part * z.part_rows, (part + 1) * z.part_rows)

    w_steps(2, head_part)
    w_end_own(0, head_part)
    attend(0)
    w_steps(head_part, head_part + LAG)
    w_end_other(0, head_part)
    attend(1)
    for i in parts:
        total = 0.0
        for index in sets:
            total = total + times(s.heads[index].o[part_at(i), :], weights[index].p[...])
        s.rs1[i].part[...] = total.astype(BF)
        rs_start(s.rs1[i])
    w_steps(head_part + LAG, head_part + LAG + 2)
    for i in parts:
        rs_middle(s.rs1[i])
        w_steps(head_part + LAG + 2 + i, head_part + LAG + 3 + i)

    def mine_at(part):
        return rows_at(part * z.part_rows + za * sh, sh)

    for i in parts:
        attn = rs_end(s.rs1[i])
        if i:
            w_steps(head_part + LAG + 4, head_part + LAG + 5)
        h1 = s.x[mine_at(i), :].astype(F32) + mod_line(2) * attn
        normed_m, _ = norm_parts(h1)
        ag_start(s.ag1[i], (normed_m * (1.0 + mod_line(4)) + mod_line(3)).astype(BF))
        s.attn[i] = attn
        s.h1[i] = h1
    w_steps(head_part + LAG + 5, half - 3)
    for i in parts:
        ag_middle(s.ag1[i])
        w_steps(half - 3 + i, half - 2 + i)
    w_end_own(head_part, thirds[1])
    w_end_other(head_part, thirds[1])

    def mlp_up(part):
        at = part_at(part)
        for index in sets:
            hid = s.hid[index]
            hidden = nt(s.ag1[part].buf[...], weights[index].up[...])
            square = hidden * hidden
            bend = jnp.tanh(GELU_C * hidden * (1.0 + GELU_K * square))
            hid.gact[at, :] = (0.5 * hidden * (1.0 + bend)).astype(BF)
            hid.slope[at, :] = 0.5 * (1.0 + bend) + 0.5 * hidden * (1.0 - bend * bend) * (
                GELU_C * (1.0 + 3.0 * GELU_K * square)
            )

    def mlp_back(part):
        at = part_at(part)
        total = 0.0
        for index in sets:
            hid = s.hid[index]
            dgact = nt(s.dmlp[at, :], weights[index].down[...])
            dz = (dgact * hid.slope[at, :]).astype(BF)
            hid.dz[at, :] = dz
            total = total + times(dz, weights[index].up[...])
        s.rs2[part].part[...] = total.astype(BF)

    def down(part):
        total = 0.0
        for index in sets:
            total = total + times(s.hid[index].gact[part_at(part), :], weights[index].down[...])
        s.rs4[part].part[...] = total.astype(BF)

    cols = 384

    def over_parts(left, gathered, at):
        total = 0.0
        for part in parts:
            total = total + tn(left[part_at(part), :], gathered[part].buf[:, at])
        return total.astype(BF)

    def tiles(body):
        loop(0, D // cols, lambda i: body(pl.ds(pl.multiple_of(i * cols, 128), cols)))

    def up_grad(index, target, first):
        def tile(at):
            target[first : first + fc, at] = over_parts(s.hid[index].dz, s.ag1, at)

        tiles(tile)

    def down_grad(index, target, first):
        def tile(at):
            grad = tn(s.hid[index].gact[...], s.dmlp[:, at])
            target[first + fc : first + 2 * fc, at] = grad.astype(BF)

        tiles(tile)

    first_one = -4 * hc
    for i in parts:
        ag_end(s.ag1[i])
        w_steps(half - 1 + i, half + i)
        mlp_up(i)
    down_grad(1, s.thin, 0)
    g_one(1, thirds[1], half, s.thin, first_one)
    w_steps(half + 1, half + LAG)
    w_end_own(thirds[1], half)
    w_end_other(thirds[1], half)
    g_two(thirds[1], half, s.thin, first_one)
    for i in g_order[:LAG]:
        g_x(i).start()
    for i in parts:
        mlp_back(i)
        rs_start(s.rs2[i])
    up_grad(1, s.thin, 0)
    g_one(1, head_part, thirds[1], s.thin, first_one)
    down_grad(0, s.placed, 4 * hc)
    g_one(0, thirds[1], half, s.placed, 0)
    g_two_own(thirds[1], half)
    for i in parts:
        rs_middle(s.rs2[i])
    g_two(head_part, thirds[1], s.thin, first_one)
    g_steps(0, 2)
    up_grad(0, s.placed, 4 * hc)
    g_one(0, head_part, thirds[1], s.placed, 0)
    for i in parts:
        down(i)
    g_two_own(head_part, thirds[1])

    def norm_back_of(normed, inverse, upstream):
        return inverse * (
            upstream
            - jnp.mean(upstream, axis=-1, keepdims=True)
            - normed * jnp.mean(upstream * normed, axis=-1, keepdims=True)
        )

    def column_sum(values):
        return jnp.sum(values, axis=0, keepdims=True)

    def dy_of(part):
        return s.grad[mine_at(part), :].astype(F32) * (group_scale * live)

    gate_a_sum = shift_m_sum = scale_m_sum = 0.0
    for i in parts:
        dw = rs_end(s.rs2[i])
        g_steps(2 + i, 3 + i)
        normed_m, inverse_m = norm_parts(s.h1[i])
        dh1 = dy_of(i) + norm_back_of(normed_m, inverse_m, dw * (1.0 + mod_line(4)))
        ag_start(s.ag2[i], (mod_line(2) * dh1).astype(BF))
        s.dh1[i] = dh1
        gate_a_sum = gate_a_sum + column_sum(dh1 * s.attn[i])
        shift_m_sum = shift_m_sum + column_sum(dw)
        scale_m_sum = scale_m_sum + column_sum(dw * normed_m)
    s.dmod[2:3, :] = gate_a_sum
    s.dmod[3:4, :] = shift_m_sum
    s.dmod[4:5, :] = scale_m_sum
    g_steps(4, 5)
    for i in parts:
        ag_middle(s.ag2[i])
        g_steps(5 + i, 6 + i)
    for i in parts:
        rs_start(s.rs4[i])

    def attend_back(index):
        own, at = weights[index], s.heads[index]
        do = jnp.concatenate([nt(s.ag2[i].buf[...], own.p[...]) for i in parts], axis=0)
        do = do.astype(BF)
        q, k, v = at.q[...], at.k[...], at.v[...]
        dq = jnp.zeros((z.seq, hc), F32)
        dk = jnp.zeros((z.seq, hc), F32)
        dv = jnp.zeros((z.seq, hc), F32)
        for head in range(z.heads):
            p = s.soft[index * z.heads + head]
            do_head = only(do, head)
            dp_soft = nt(do_head, v)
            inner = jnp.sum(p * dp_soft, axis=-1, keepdims=True)
            ds = (p * (dp_soft - inner)).astype(BF)
            dq = dq + times(ds, only(k, head))
            dk = dk + tn(ds, only(q, head))
            dv = dv + tn(p.astype(BF), do_head)
        at.dq[...] = (dq * scale).astype(BF)
        at.dk[...] = (dk * scale).astype(BF)
        at.dv[...] = dv.astype(BF)

    for i in parts:
        ag_end(s.ag2[i])
        g_steps(7 + i, 8 + i)
    for index in sets:
        attend_back(index)
        g_steps(9 + index, 10)
    for i in parts:
        total = 0.0
        for index in sets:
            own, at = weights[index], s.heads[index]
            rows = part_at(i)
            total = total + times(at.dq[rows, :], own.q[...])
            total = total + times(at.dk[rows, :], own.k[...])
            total = total + times(at.dv[rows, :], own.v[...])
        s.rs3[i].part[...] = total.astype(BF)
        rs_start(s.rs3[i])
    for i in parts:
        rs_middle(s.rs4[i])

    def attn_grad_of(index, target):
        own = s.heads[index]

        def tile(i):
            at = pl.ds(pl.multiple_of(i * cols, 128), cols)
            mixed = s.u[:, at]
            target[0:hc, at] = tn(own.dq[...], mixed).astype(BF)
            target[hc : 2 * hc, at] = tn(own.dk[...], mixed).astype(BF)
            target[2 * hc : 3 * hc, at] = tn(own.dv[...], mixed).astype(BF)
            target[3 * hc : 4 * hc, at] = over_parts(own.o, s.ag2, at)

        loop(0, D // cols, tile)

    attn_grad_of(1, s.extra)
    g_one(1, 0, head_part, s.extra, 0)
    for i in parts:
        rs_middle(s.rs3[i])
    g_two(0, head_part, s.extra, 0)
    g_steps(12 - LAG, 12)
    attn_grad_of(0, s.placed)
    g_one(0, 0, head_part, s.placed, 0)
    g_two_own(0, head_part)

    def dsum_copy():
        return remote(s.dsum, s.dsum_in, s.dsum_s.at[0], s.dsum_r.at[0], xp)

    s.dsum[...] = jnp.zeros((8, 256), F32)
    s.dsum[0:1, 0:hc] = column_sum(s.heads[1].dq[...].astype(F32))
    s.dsum[1:2, 0:hc] = column_sum(s.heads[1].dv[...].astype(F32))
    go(dsum_copy())
    g_steps(12, 13)

    shift_a_sum = scale_a_sum = gate_m_sum = 0.0
    for i in parts:
        du = rs_end(s.rs3[i])
        g_steps(13 + i, 14 + i)
        normed_a, inverse_a = norm_parts(s.x[mine_at(i), :].astype(F32))
        dx = s.dh1[i] + norm_back_of(normed_a, inverse_a, du * (1.0 + mod_line(1)))
        ag_start(s.ag3[i], dx.astype(BF))
        shift_a_sum = shift_a_sum + column_sum(du)
        scale_a_sum = scale_a_sum + column_sum(du * normed_a)
    for i in parts:
        mlp_sum = rs_end(s.rs4[i])
        gate_m_sum = gate_m_sum + column_sum(dy_of(i) * mlp_sum)
        result = (s.h1[i] + mod_line(5) * mlp_sum) * live
        ag_start(s.ag4[i], result.astype(BF))
    s.dmod[0:1, :] = shift_a_sum
    s.dmod[1:2, :] = scale_a_sum
    s.dmod[5:6, :] = gate_m_sum
    s.dmod[6:8, :] = jnp.zeros((2, D), F32)

    dlines = [spread(s.dmod[i : i + 1, :]) for i in range(6)]
    for member in range(n_t):
        first = member * z.mod_rows
        line = jnp.zeros((8, D), F32)
        for piece in range(6):
            lower = max(first, piece * D) - first
            upper = min(first + z.mod_rows, (piece + 1) * D) - first
            if lower < upper:
                back = (piece * D - first) % D
                moved = pltpu.roll(dlines[piece], back, 1) if back else dlines[piece]
                line = jnp.where((lane >= lower) & (lane < upper), moved, line)
        for i in range(8):
            s.dmod_pack[member, i : i + 1, :] = line[0:1, 128 * i : 128 * (i + 1)]

    def dmod_copy(i):
        member = lax.rem(t + i, n_t)
        return remote(
            s.dmod_pack.at[member],
            s.dmod_recv.at[i - 1],
            s.dmod_s.at[i - 1],
            s.dmod_r.at[i - 1],
            (dp, member),
        )

    for i in range(1, n_t):
        go(dmod_copy(i))
    for i in parts:
        ag_middle(s.ag3[i])
    for i in parts:
        ag_middle(s.ag4[i])
    g_steps(15, 16)
    dsum_copy().wait_recv()
    total = s.dmod_pack[t]
    for i in range(1, n_t):
        dmod_copy(i).wait_recv()
        total = total + s.dmod_recv[i - 1]
    s.vec[dp] = jnp.zeros((16, 256), F32)
    s.vec[dp, 0:8, 0:128] = total
    own_sums = (column_sum(s.heads[0].dq[...].astype(F32)), column_sum(s.heads[0].dv[...].astype(F32)))
    s.vec[dp, 8:9, 0:hc] = own_sums[0] + s.dsum_in[0:1, 0:hc]
    s.vec[dp, 9:10, 0:hc] = own_sums[1] + s.dsum_in[1:2, 0:hc]

    def vec_copy(i, group):
        return remote(
            s.vec.at[group],
            s.vec.at[group],
            s.vec_s.at[i - 1],
            s.vec_r.at[i - 1],
            (lax.rem(dp + i, n_dp), t),
        )

    for i in range(1, n_dp):
        go(vec_copy(i, dp))
    g_steps(16, half + LAG)
    for i in parts:
        ag_end(s.ag3[i])
        ag_end(s.ag4[i])
    g_end(0, half)
    for i in range(1, n_dp):
        vec_copy(i, lax.rem(dp - i + n_dp, n_dp)).wait_recv()
    for copy in pending:
        copy.wait_send()

    outs = [(s.g.fin, out_g), (s.vec, out_vec), (s.tok_all, out_tok)]
    for i in parts:
        at = pl.ds(i * z.part_rows, z.part_rows)
        outs.append((s.ag4[i].buf, out_own.at[0, at]))
        outs.append((s.ag3[i].buf, out_own.at[1, at]))
    stores = [
        pltpu.make_async_copy(src, dst, s.out_sem.at[i]) for i, (src, dst) in enumerate(outs)
    ]
    for store in stores:
        store.start()
    for store in stores:
        store.wait()


def update_kernel(z, group_slots, owners, grads, table, tokens, master, first, second, new_first, new_second, new_master, bos):
    step = pl.program_id(0)
    dp = lax.axis_index("dp")

    @pl.when(step == 0)
    def _():
        def clear(slot, carry):
            bos[slot] = -1
            return carry

        lax.fori_loop(0, z.slots, clear, 0)

        def note(block, taken):
            mine = owners[block] == dp

            @pl.when(mine & (taken < z.slots))
            def _():
                bos[taken] = block

            return taken + mine.astype(jnp.int32)

        lax.fori_loop(0, z.blocks, note, jnp.int32(0))

    rows = z.block_rows
    mod_blocks = z.mod_rows // rows
    head_blocks = z.head_cols // rows
    fix_one = 1.0 - beta_one**STEP
    fix_two = 1.0 - beta_two**STEP

    def put(i, grad):
        weight = master[i]
        one = beta_one * first[i] + (1.0 - beta_one) * grad
        two = beta_two * second[i] + (1.0 - beta_two) * grad * grad
        new_first[i] = one
        new_second[i] = two
        spread = two * (1.0 / fix_two)
        root = spread * lax.rsqrt(spread)
        change = one * (1.0 / fix_one) * pltpu.reciprocal(root + eps_adam) + decay_rate * weight
        new_master[i] = weight - learn_rate * change

    def slot(i, carry):
        block = bos[step * group_slots + i]
        is_mod = block < mod_blocks
        is_time = (block >= mod_blocks + 3 * head_blocks) & (block < mod_blocks + 5 * head_blocks)

        @pl.when(block < 0)
        def _():
            new_first[i] = jnp.zeros((rows, D), F32)
            new_second[i] = jnp.zeros((rows, D), F32)
            new_master[i] = jnp.zeros((rows, D), F32)

        @pl.when((block >= 0) & (is_mod | is_time))
        def _():
            index = jnp.where(is_mod, block, block - 3 * head_blocks)
            columns = table[index]
            grad = columns[:, 0:1] * tokens[0:1, :].astype(F32)
            for group in range(1, z.dp_count):
                grad = grad + columns[:, group : group + 1] * tokens[
                    16 * group : 16 * group + 1, :
                ].astype(F32)
            put(i, grad)

        @pl.when((block >= 0) & jnp.logical_not(is_mod | is_time))
        def _():
            index = jnp.where(
                block < mod_blocks + 3 * head_blocks,
                block - mod_blocks,
                block - mod_blocks - 2 * head_blocks,
            )
            both = grads[rows_at(index // 2 * PAIR, PAIR), :].astype(F32)
            put(i, jnp.where(lax.rem(index, 2) == 0, both[:rows], both[rows:]))

        return carry

    lax.fori_loop(0, group_slots, slot, 0)


def per_device_fast(
    z,
    inputs,
    out_grad,
    bucket,
    counts,
    images_held,
    owners,
    master_weight,
    first_moment,
    second_moment,
):
    token = jnp.broadcast_to(time_token(bucket[0]).astype(BF)[None, :], (16, D))
    plan = scratch_plan(z)
    smem = pl.BlockSpec(memory_space=pltpu.SMEM)
    vmem = pl.BlockSpec(memory_space=pltpu.VMEM)
    hbm = pl.BlockSpec(memory_space=pl.ANY)
    flops = 12 * z.seq * D * z.wide
    own, grads, vectors, tokens = pl.pallas_call(
        partial(layer_kernel, z, plan),
        out_shape=(
            jax.ShapeDtypeStruct((2, z.seq, D), BF),
            jax.ShapeDtypeStruct((z.wide, D), BF),
            jax.ShapeDtypeStruct((z.dp_count, 16, 256), F32),
            jax.ShapeDtypeStruct((16 * z.dp_count, D), BF),
        ),
        in_specs=[smem, smem, smem, vmem, hbm, hbm, hbm],
        out_specs=(hbm,) * 4,
        scratch_shapes=flatten(plan),
        compiler_params=pltpu.CompilerParams(
            collective_id=0, has_side_effects=True, vmem_limit_bytes=62 * 2**20
        ),
        cost_estimate=pl.CostEstimate(
            flops=flops, bytes_accessed=20 * 2**20, transcendentals=2 * z.seq * z.ffn_cols
        ),
        name="layer",
    )(
        owners,
        counts,
        images_held,
        token,
        inputs,
        out_grad,
        master_weight,
    )
    swap = [(member, member ^ 1) for member in range(z.tensor_count)]
    other = lax.ppermute(own, axes[1], swap)
    columns = jnp.concatenate(
        [
            vectors[:, :8, :128].reshape(z.dp_count, 1024)[:, : z.mod_rows],
            vectors[:, 8, : z.head_cols],
            vectors[:, 9, : z.head_cols],
        ],
        axis=1,
    ).T.reshape(z.thin // z.block_rows, z.block_rows, z.dp_count)
    group_slots = next(size for size in (15, 12, 10, 8, 6, 5, 4, 3, 2, 1) if z.slots % size == 0)
    block = pl.BlockSpec((group_slots, z.block_rows, D), lambda i: (i, 0, 0))
    state = jax.ShapeDtypeStruct(master_weight.shape, F32)
    new_first, new_second, new_master = pl.pallas_call(
        partial(update_kernel, z, group_slots),
        grid=(z.slots // group_slots,),
        out_shape=(state,) * 3,
        in_specs=[smem, vmem, vmem, vmem, block, block, block],
        out_specs=(block,) * 3,
        scratch_shapes=[pltpu.SMEM((z.slots,), jnp.int32)],
        compiler_params=pltpu.CompilerParams(vmem_limit_bytes=48 * 2**20),
        cost_estimate=pl.CostEstimate(
            flops=20 * master_weight.size,
            bytes_accessed=24 * master_weight.size,
            transcendentals=2 * master_weight.size,
        ),
        name="update",
    )(owners, grads, columns, tokens, master_weight, first_moment, second_moment)
    even = lax.rem(lax.axis_index(axes[1]), 2) == 0
    images = jnp.stack([jnp.where(even, own, other), jnp.where(even, other, own)], axis=1)
    return (
        images[0],
        images[1].astype(F32),
        new_first,
        new_second,
        new_master,
    )


def per_device(inputs, out_grad, bucket, counts, images_held, owners, master, first, second):
    sizes = Sizes(
        lax.axis_size("dp"),
        lax.axis_size("tensor"),
        master.shape[0],
        master.shape[1],
        inputs.shape[0],
        inputs.shape[1],
    )
    run = partial(per_device_fast, sizes) if sizes.fits() else per_device_plain
    return run(inputs, out_grad, bucket, counts, images_held, owners, master, first, second)


def solution(mesh):
    return jax.shard_map(
        per_device,
        mesh=mesh,
        in_specs=(
            P("dp", None, None),
            P("dp", None, None),
            P("dp"),
            P(),
            P("dp"),
            P(),
            P("dp", "tensor", None),
            P("dp", "tensor", None),
            P("dp", "tensor", None),
        ),
        out_specs=(
            P("dp", None, None),
            P("dp", None, None),
            P("dp", "tensor", None),
            P("dp", "tensor", None),
            P("dp", "tensor", None),
        ),
        check_vma=False,
    )
```

```python
from functools import partial
import math
from types import SimpleNamespace

import jax
import jax.numpy as jnp
from jax import lax
from jax.experimental import pallas as pl
from jax.experimental.pallas import tpu as pltpu
from jax.sharding import PartitionSpec as P

D = 1152
HEADS = 16
HEAD_DIM = 72
FF = 4608
NBUCKET = 8
STEP = 10


eps_norm = 1e-06
beta_one = 0.5
beta_two = 0.5
learn_rate = 0.03
decay_rate = 0.01
eps_adam = 1e-08


def time_token(bucket_value):
    half_width = D // 2
    freqs = jnp.exp(-math.log(10000.0) * jnp.arange(half_width, dtype=jnp.float32) / half_width)
    instant = (bucket_value.astype(jnp.float32) + 0.5) * (1000.0 / NBUCKET)
    angles = instant * freqs
    embed = jnp.concatenate([jnp.cos(angles), jnp.sin(angles)])
    return embed * jax.nn.sigmoid(embed)


def norm_stats(values):
    centred = values - jnp.mean(values, axis=-1, keepdims=True)
    inverse = lax.rsqrt(jnp.mean(centred * centred, axis=-1, keepdims=True) + eps_norm)
    return (centred * inverse, inverse)


def norm_back(normed, inverse, upstream):
    return inverse * (
        upstream
        - jnp.mean(upstream, axis=-1, keepdims=True)
        - normed * jnp.mean(upstream * normed, axis=-1, keepdims=True)
    )


def times_transposed(left, right):
    return lax.dot_general(
        left, right, (((1,), (1,)), ((), ())), preferred_element_type=jnp.float32
    )


def transposed_times(left, right):
    return lax.dot_general(
        left, right, (((0,), (0,)), ((), ())), preferred_element_type=jnp.float32
    )


def attend_forward(block):
    queries, key_rows, values = block
    scores = jnp.einsum(
        "bqhd,bkhd->bhqk", queries, key_rows, preferred_element_type=jnp.float32
    ) * HEAD_DIM ** (-0.5)
    row_peak = jnp.max(scores, axis=-1, keepdims=True)
    exp_scores = jnp.exp(scores - row_peak)
    row_total = jnp.sum(exp_scores, axis=-1, keepdims=True)
    soft = (exp_scores / row_total).astype(jnp.bfloat16)
    attended = jnp.einsum("bhqk,bkhd->bqhd", soft, values, preferred_element_type=jnp.float32)
    return (attended, row_peak[..., 0] + jnp.log(row_total[..., 0]))


def attend_backward(block):
    queries, key_rows, values, log_total, upstream = block
    scale_factor = HEAD_DIM ** (-0.5)
    scores = (
        jnp.einsum("bqhd,bkhd->bhqk", queries, key_rows, preferred_element_type=jnp.float32)
        * scale_factor
    )
    soft = jnp.exp(scores - log_total[..., None])
    grad_soft = jnp.einsum("bqhd,bkhd->bhqk", upstream, values, preferred_element_type=jnp.float32)
    inner_sum = jnp.sum(soft * grad_soft, axis=-1, keepdims=True)
    grad_scores = (soft * (grad_soft - inner_sum)).astype(jnp.bfloat16)
    grad_query = (
        jnp.einsum("bhqk,bkhd->bqhd", grad_scores, key_rows, preferred_element_type=jnp.float32)
        * scale_factor
    )
    grad_key = (
        jnp.einsum("bhqk,bqhd->bkhd", grad_scores, queries, preferred_element_type=jnp.float32)
        * scale_factor
    )
    grad_value = jnp.einsum(
        "bhqk,bqhd->bkhd", soft.astype(jnp.bfloat16), upstream, preferred_element_type=jnp.float32
    )
    return (grad_query, grad_key, grad_value)


def per_device_plain(
    inputs,
    out_grad,
    bucket,
    counts,
    images_held,
    owners,
    master_weight,
    first_moment,
    second_moment,
):
    dp_count = lax.axis_size("dp")
    tensor_count = lax.axis_size("tensor")
    dp_rank = lax.axis_index("dp")
    tensor_rank = lax.axis_index("tensor")
    own_slots = master_weight.shape[0]
    block_rows = master_weight.shape[1]
    head_cols = D // tensor_count
    ffn_cols = FF // tensor_count
    local_heads = HEADS // tensor_count
    local_rows = 12 * head_cols + 2 * ffn_cols
    block_count = local_rows // block_rows
    image_count = inputs.shape[0]
    seq_len = inputs.shape[1]
    row_count = image_count * seq_len
    block_ids = jnp.arange(block_count, dtype=jnp.int32)
    earlier = (owners[None, :] == owners[:, None]) & (block_ids[None, :] < block_ids[:, None])
    slot_of = owners * own_slots + jnp.sum(earlier.astype(jnp.int32), axis=1)
    gathered = lax.all_gather(master_weight.astype(jnp.bfloat16), "dp", axis=0, tiled=True)
    weights = gathered[slot_of].reshape(local_rows, D)
    w_mod = weights[: 6 * head_cols]
    w_qkv = weights[6 * head_cols : 9 * head_cols]
    w_qtime = weights[9 * head_cols : 10 * head_cols]
    w_vtime = weights[10 * head_cols : 11 * head_cols]
    w_proj = weights[11 * head_cols : 12 * head_cols]
    w_up = weights[12 * head_cols : 12 * head_cols + ffn_cols]
    w_down = weights[12 * head_cols + ffn_cols :]
    token = time_token(bucket[0]).astype(jnp.bfloat16)
    token_wide = token.astype(jnp.float32)
    mod_piece = jnp.dot(w_mod, token, preferred_element_type=jnp.float32)
    modulation = lax.all_gather(mod_piece, "tensor", axis=0, tiled=True)
    shift_a, scale_a, gate_a, shift_m, scale_m, gate_m = jnp.split(modulation, 6)
    counts_f = counts.astype(jnp.float32)
    group_scale = counts_f[dp_rank] * dp_count / jnp.sum(counts_f)
    flat_rows = inputs.reshape(row_count, D).astype(jnp.float32)
    live = (jnp.arange(row_count, dtype=jnp.int32) // seq_len < images_held[0]).astype(jnp.float32)[
        :, None
    ]
    normed_a, inverse_a = norm_stats(flat_rows)
    mixed_a = (normed_a * (1.0 + scale_a) + shift_a).astype(jnp.bfloat16)
    projected = times_transposed(mixed_a, w_qkv)
    time_query = jnp.dot(w_qtime, token, preferred_element_type=jnp.float32)
    time_value = jnp.dot(w_vtime, token, preferred_element_type=jnp.float32)
    queries = (projected[:, :head_cols] + time_query).astype(jnp.bfloat16)
    key_rows = projected[:, head_cols : 2 * head_cols].astype(jnp.bfloat16)
    values = (projected[:, 2 * head_cols :] + time_value).astype(jnp.bfloat16)
    group_imgs = math.gcd(image_count, max(1, 512 // seq_len))
    block_shape = (image_count // group_imgs, group_imgs, seq_len, local_heads, HEAD_DIM)
    q_blocks = queries.reshape(block_shape)
    k_blocks = key_rows.reshape(block_shape)
    v_blocks = values.reshape(block_shape)
    attended, log_total = lax.map(attend_forward, (q_blocks, k_blocks, v_blocks))
    heads_out = attended.reshape(row_count, head_cols).astype(jnp.bfloat16)
    heads_share = lax.psum_scatter(
        jnp.dot(heads_out, w_proj, preferred_element_type=jnp.float32).astype(jnp.bfloat16),
        "tensor",
        scatter_dimension=0,
        tiled=True,
    ).astype(jnp.float32)
    branch_a = lax.all_gather(
        heads_share.astype(jnp.bfloat16), "tensor", axis=0, tiled=True
    ).astype(heads_share.dtype)
    resid = flat_rows + gate_a * branch_a
    normed_m, inverse_m = norm_stats(resid)
    mixed_m = (normed_m * (1.0 + scale_m) + shift_m).astype(jnp.bfloat16)
    hidden = times_transposed(mixed_m, w_up)
    acted = jax.nn.gelu(hidden, approximate=True).astype(jnp.bfloat16)
    hidden_share = lax.psum_scatter(
        jnp.dot(acted, w_down, preferred_element_type=jnp.float32).astype(jnp.bfloat16),
        "tensor",
        scatter_dimension=0,
        tiled=True,
    ).astype(jnp.float32)
    branch_m = lax.all_gather(
        hidden_share.astype(jnp.bfloat16), "tensor", axis=0, tiled=True
    ).astype(hidden_share.dtype)
    result = resid + gate_m * branch_m
    block_output = (result * live).astype(jnp.bfloat16).reshape(inputs.shape)
    grad_y = out_grad.reshape(row_count, D).astype(jnp.float32) * (group_scale * live)
    grad_branch_m = (gate_m * grad_y).astype(jnp.bfloat16)
    grad_gate_m = jnp.sum(grad_y * branch_m, axis=0)
    grad_acted = times_transposed(grad_branch_m, w_down)
    grad_down = transposed_times(acted, grad_branch_m)
    grad_hidden = jax.vjp(partial(jax.nn.gelu, approximate=True), hidden)[1](grad_acted)[0].astype(
        jnp.bfloat16
    )
    grad_up = transposed_times(grad_hidden, mixed_m)
    mlp_grad_share = lax.psum_scatter(
        jnp.dot(grad_hidden, w_up, preferred_element_type=jnp.float32).astype(jnp.bfloat16),
        "tensor",
        scatter_dimension=0,
        tiled=True,
    ).astype(jnp.float32)
    grad_mixed_m = lax.all_gather(
        mlp_grad_share.astype(jnp.bfloat16), "tensor", axis=0, tiled=True
    ).astype(mlp_grad_share.dtype)
    grad_shift_m = jnp.sum(grad_mixed_m, axis=0)
    grad_scale_m = jnp.sum(grad_mixed_m * normed_m, axis=0)
    grad_resid = grad_y + norm_back(normed_m, inverse_m, grad_mixed_m * (1.0 + scale_m))
    grad_branch_a = (gate_a * grad_resid).astype(jnp.bfloat16)
    grad_gate_a = jnp.sum(grad_resid * branch_a, axis=0)
    grad_heads = times_transposed(grad_branch_a, w_proj).astype(jnp.bfloat16)
    grad_proj = transposed_times(heads_out, grad_branch_a)
    grads_query, grads_key, grads_value = lax.map(
        attend_backward, (q_blocks, k_blocks, v_blocks, log_total, grad_heads.reshape(block_shape))
    )
    grad_qkv = jnp.concatenate(
        [
            grads_query.reshape(row_count, head_cols),
            grads_key.reshape(row_count, head_cols),
            grads_value.reshape(row_count, head_cols),
        ],
        axis=1,
    ).astype(jnp.bfloat16)
    grad_wqkv = transposed_times(grad_qkv, mixed_a)
    attn_grad_share = lax.psum_scatter(
        jnp.dot(grad_qkv, w_qkv, preferred_element_type=jnp.float32).astype(jnp.bfloat16),
        "tensor",
        scatter_dimension=0,
        tiled=True,
    ).astype(jnp.float32)
    grad_mixed_a = lax.all_gather(
        attn_grad_share.astype(jnp.bfloat16), "tensor", axis=0, tiled=True
    ).astype(attn_grad_share.dtype)
    token_sums = jnp.sum(grad_qkv, axis=0, dtype=jnp.float32)
    grad_qtime = token_sums[:head_cols, None] * token_wide[None, :]
    grad_vtime = token_sums[2 * head_cols :, None] * token_wide[None, :]
    grad_shift_a = jnp.sum(grad_mixed_a, axis=0)
    grad_scale_a = jnp.sum(grad_mixed_a * normed_a, axis=0)
    grad_in = grad_resid + norm_back(normed_a, inverse_a, grad_mixed_a * (1.0 + scale_a))
    grad_mod = jnp.concatenate(
        [grad_shift_a, grad_scale_a, grad_gate_a, grad_shift_m, grad_scale_m, grad_gate_m]
    )
    grad_mod_piece = lax.dynamic_slice_in_dim(grad_mod, tensor_rank * 6 * head_cols, 6 * head_cols)
    grad_wmod = grad_mod_piece[:, None] * token_wide[None, :]
    grads = jnp.concatenate(
        [grad_wmod, grad_wqkv, grad_qtime, grad_vtime, grad_proj, grad_up, grad_down], axis=0
    )
    grad_blocks = grads.reshape(block_count, block_rows, D)
    owned_blocks = jnp.full((dp_count * own_slots,), -1, jnp.int32).at[slot_of].set(block_ids)
    mine = lax.dynamic_slice_in_dim(owned_blocks, dp_rank * own_slots, own_slots)
    filled = (mine >= 0)[:, None, None]
    placed = (
        jnp.zeros((dp_count * own_slots, block_rows, D), jnp.float32).at[slot_of].set(grad_blocks)
    )
    reduced = lax.psum_scatter(
        placed.astype(jnp.bfloat16), "dp", scatter_dimension=0, tiled=True
    ).astype(jnp.float32)
    new_first = beta_one * first_moment + (1.0 - beta_one) * reduced
    new_second = beta_two * second_moment + (1.0 - beta_two) * reduced * reduced
    fix_one = 1.0 - beta_one**STEP
    fix_two = 1.0 - beta_two**STEP
    change = (
        new_first / fix_one / (jnp.sqrt(new_second / fix_two) + eps_adam)
        + decay_rate * master_weight
    )
    new_master = master_weight - learn_rate * change
    return (
        block_output,
        grad_in.reshape(inputs.shape),
        jnp.where(filled, new_first, 0.0),
        jnp.where(filled, new_second, 0.0),
        jnp.where(filled, new_master, 0.0),
    )


BF = jnp.bfloat16
F32 = jnp.float32
MESH = pl.DeviceIdType.MESH
axes = ("dp", "tensor")
TILE = 64
LAG = 2
PAIR = 48
GELU_C = math.sqrt(2.0 / math.pi)
GELU_K = 0.044715


def rows_at(start, size):
    return pl.ds(pl.multiple_of(start, 16), size)


def remote(src, dst, send_sem, recv_sem, device):
    return pltpu.make_async_remote_copy(
        src_ref=src,
        dst_ref=dst,
        send_sem=send_sem,
        recv_sem=recv_sem,
        device_id=device,
        device_id_type=MESH,
    )


def times(left, right):
    return jnp.dot(left, right, preferred_element_type=F32)


class Sizes:
    def __init__(self, dp_count, tensor_count, slots, block_rows, images, seq):
        self.dp_count, self.tensor_count = dp_count, tensor_count
        self.slots, self.block_rows = slots, block_rows
        self.images, self.seq = images, seq
        self.parts = 2
        self.part_rows = seq // self.parts
        self.shard = self.part_rows // 4
        self.head_cols = D // tensor_count
        self.ffn_cols = FF // tensor_count
        self.heads = HEADS // tensor_count
        self.mod_rows = 6 * self.head_cols
        self.local_rows = 12 * self.head_cols + 2 * self.ffn_cols
        self.blocks = self.local_rows // block_rows
        self.wide = 4 * self.head_cols + 2 * self.ffn_cols
        self.thin = self.mod_rows + 2 * self.head_cols

    def fits(self):
        return (
            self.dp_count == 4
            and self.tensor_count == 8
            and self.images == 2
            and 2 * self.block_rows == PAIR
            and self.slots % 3 == 0
            and self.seq % 128 == 0
            and self.head_cols % PAIR == 0
            and self.ffn_cols % PAIR == 0
            and self.wide % (6 * PAIR) == 0
            and self.thin == D
            and self.thin == 2 * self.ffn_cols
            and self.mod_rows <= 1024
        )


def flatten(plan):
    if isinstance(plan, SimpleNamespace):
        return flatten(list(vars(plan).values()))
    if isinstance(plan, list):
        return [leaf for member in plan for leaf in flatten(member)]
    return [plan]


def rebuild(plan, leaves):
    if isinstance(plan, SimpleNamespace):
        return SimpleNamespace(**{key: rebuild(value, leaves) for key, value in vars(plan).items()})
    if isinstance(plan, list):
        return [rebuild(member, leaves) for member in plan]
    return next(leaves)


def scratch_plan(z):
    dma = pltpu.SemaphoreType.DMA
    vm = pltpu.VMEM
    half = z.wide // PAIR // 2

    def pairs():
        return vm((half, PAIR, D), BF)

    def attention():
        names = 7
        q, k, v, o, dq, dk, dv = (vm((z.seq, z.head_cols), BF) for _ in range(names))
        return SimpleNamespace(q=q, k=k, v=v, o=o, dq=dq, dk=dk, dv=dv)

    def hidden():
        return SimpleNamespace(
            slope=vm((z.seq, z.ffn_cols), F32),
            gact=vm((z.seq, z.ffn_cols), BF),
            dz=vm((z.seq, z.ffn_cols), BF),
        )

    def scatter():
        return SimpleNamespace(
            part=vm((z.part_rows, D), BF),
            zout=vm((z.shard, D), BF),
            zin=vm((3, z.shard, D), BF),
            zs=dma((3,)),
            zr=dma((3,)),
        )

    def gather():
        return SimpleNamespace(buf=vm((z.part_rows, D), BF), zs=dma((3,)), zr=dma((3,)))

    def each(make):
        return [make() for _ in range(z.parts)]

    return SimpleNamespace(
        slot_table=pltpu.SMEM((z.blocks,), jnp.int32),
        master=vm((z.slots, z.block_rows, D), F32),
        master_sem=dma((3,)),
        x=vm((z.seq, D), BF),
        grad=vm((z.seq, D), BF),
        in_sem=dma((2,)),
        placed=vm((z.wide, D), BF),
        thin=vm((z.thin, D), BF),
        extra=vm((4 * z.head_cols, D), BF),
        tok_all=vm((16 * z.dp_count, D), BF),
        tok_s=dma((3,)),
        tok_r=dma((3,)),
        mod_prod=vm((16 * z.dp_count, D), F32),
        mod_pack=vm((z.dp_count, 16, 128), F32),
        mod_recv=vm((3, 16, 128), F32),
        mod_s=dma((3,)),
        mod_r=dma((3,)),
        mod_all=vm((z.tensor_count, 16, 128), F32),
        moda_s=dma((z.tensor_count - 1,)),
        moda_r=dma((z.tensor_count - 1,)),
        modv=vm((8, D), F32),
        time_qv=vm((8, 4 * 256), F32),
        u=vm((z.seq, D), BF),
        dmlp=vm((z.seq, D), BF),
        heads=[attention(), attention()],
        soft=vm((2 * z.heads, z.seq, z.seq), F32),
        hid=[hidden(), hidden()],
        h1=vm((z.parts, z.shard, D), F32),
        attn=vm((z.parts, z.shard, D), F32),
        dh1=vm((z.parts, z.shard, D), F32),
        dmod=vm((8, D), F32),
        dmod_pack=vm((z.tensor_count, 8, 128), F32),
        dmod_recv=vm((z.tensor_count - 1, 8, 128), F32),
        dmod_s=dma((z.tensor_count - 1,)),
        dmod_r=dma((z.tensor_count - 1,)),
        dsum=vm((8, 256), F32),
        dsum_in=vm((8, 256), F32),
        dsum_s=dma((1,)),
        dsum_r=dma((1,)),
        vec=vm((z.dp_count, 16, 256), F32),
        table=vm((z.thin, 8), F32),
        vec_s=dma((3,)),
        vec_r=dma((3,)),
        out_sem=dma((5 + z.parts,)),
        sib=pairs(),
        mrg=pairs(),
        w=SimpleNamespace(
            far=pairs(),
            fin=vm((z.wide, D), BF),
            oth=vm((z.wide, D), BF),
            s1=dma((half,)),
            r1=dma((half,)),
            s2=dma((half,)),
            r2=dma((half,)),
            s3=dma((half,)),
            r3=dma((half,)),
            s4=dma((half,)),
            r4=dma((half,)),
            s5=dma((half,)),
            r5=dma((half,)),
        ),
        g=SimpleNamespace(
            far=pairs(),
            fin=vm((z.wide, D), BF),
            sib1=pairs(),
            mrg1=pairs(),
            xin=pairs(),
            s0=dma((half,)),
            r0=dma((half,)),
            s1=dma((half,)),
            r1=dma((half,)),
            s2=dma((half,)),
            r2=dma((half,)),
            s3=dma((half,)),
            r3=dma((half,)),
            s4=dma((half,)),
            r4=dma((half,)),
        ),
        rs1=each(scatter),
        rs2=each(scatter),
        rs3=each(scatter),
        rs4=each(scatter),
        ag1=each(gather),
        ag2=each(gather),
        ag3=each(gather),
        bo=vm((z.parts * z.shard, D), BF),
        bo_in=vm((z.parts * z.shard, D), BF),
        bo_s=dma((1,)),
        bo_r=dma((1,)),
    )


def layer_kernel(z, plan, *refs):
    owners, counts, held, tok, x_hbm, grad_hbm, master_hbm = refs[:7]
    out_bo, out_ig, out_g, out_table, out_tok = refs[7:12]
    s = rebuild(plan, iter(refs[12:]))
    nt_dims = (((1,), (1,)), ((), ()))
    tn_dims = (((0,), (0,)), ((), ()))

    def nt(left, right):
        return lax.dot_general(left, right, nt_dims, preferred_element_type=F32)

    def tn(left, right):
        return lax.dot_general(left, right, tn_dims, preferred_element_type=F32)

    hc, fc = z.head_cols, z.ffn_cols
    n_dp, n_t = z.dp_count, z.tensor_count
    dp, t = lax.axis_index("dp"), lax.axis_index("tensor")
    core = lax.rem(dp, 2)
    za, xb = t // 2, lax.rem(t, 2)
    near_z = za + 1 - 2 * lax.rem(za, 2)
    far_z = lax.rem(za + 2, 4)
    cross_z = 3 - za
    sib = (dp + 1 - 2 * core, t)
    far = (lax.rem(dp + 2, 4), t)
    xp = (dp, t + 1 - 2 * xb)
    near, across = (dp, 2 * near_z + xb), (dp, 2 * far_z + xb)
    half = z.wide // PAIR // 2
    head_part = (4 * hc) // PAIR // 2
    pending = []

    def go(copy):
        copy.start()
        pending.append(copy)

    third = z.slots // 3
    loads = [
        pltpu.make_async_copy(
            master_hbm.at[pl.ds(i * third, third)],
            s.master.at[pl.ds(i * third, third)],
            s.master_sem.at[i],
        )
        for i in range(3)
    ]
    image_loads = [
        pltpu.make_async_copy(x_hbm.at[xb], s.x, s.in_sem.at[0]),
        pltpu.make_async_copy(grad_hbm.at[xb], s.grad, s.in_sem.at[1]),
    ]
    for load in loads + image_loads:
        load.start()

    barrier = pltpu.get_barrier_semaphore()
    for i in range(1, n_dp):
        pl.semaphore_signal(
            barrier, inc=1, device_id=(lax.rem(dp + i, n_dp), t), device_id_type=MESH
        )
    for i in range(1, n_t):
        pl.semaphore_signal(
            barrier, inc=1, device_id=(dp, lax.rem(t + i, n_t)), device_id_type=MESH
        )
    pl.semaphore_wait(barrier, n_dp + n_t - 2)

    s.tok_all[rows_at(dp * 16, 16), :] = tok[...]

    def tok_copy(i, group):
        block = s.tok_all.at[rows_at(group * 16, 16)]
        return remote(
            block,
            block,
            s.tok_s.at[i - 1],
            s.tok_r.at[i - 1],
            (lax.rem(dp + i, n_dp), t),
        )

    for i in range(1, n_dp):
        go(tok_copy(i, dp))

    def note_slot(block, taken):
        mine = owners[block] == dp
        s.slot_table[block] = jnp.where(mine, taken, -1)
        return taken + mine.astype(jnp.int32)

    lax.fori_loop(0, z.blocks, note_slot, jnp.int32(0))
    for load in loads:
        load.wait()

    def place(into, lower, upper, shift):
        def one(pair, carry):
            halves = []
            for side in range(2):
                slot = s.slot_table[2 * (pair + shift) + side]
                block = s.master[jnp.clip(slot, 0, z.slots - 1)]
                halves.append(jnp.where(slot >= 0, block, 0.0))
            into[rows_at(pair * PAIR, PAIR), :] = jnp.concatenate(halves, axis=0).astype(BF)
            return carry

        lax.fori_loop(lower, upper, one, 0)

    qkv_pairs, mod_pairs = 3 * hc // PAIR, z.mod_rows // PAIR
    time_pairs = 2 * hc // PAIR
    wide_pairs = z.wide // PAIR
    shift_qkv = mod_pairs
    shift_rest = mod_pairs + time_pairs

    def loop(lower, upper, body):
        lax.fori_loop(lower, upper, lambda i, carry: (body(i), carry)[1], 0)

    def pair_at(ref, i, side, first=0):
        return ref.at[rows_at(first + (2 * i + side) * PAIR, PAIR)]

    def w_core(i):
        return remote(
            pair_at(s.placed, i, 1 - core), s.sib.at[i], s.w.s1.at[i], s.w.r1.at[i], sib
        )

    def w_far(i):
        return remote(s.mrg.at[i], s.w.far.at[i], s.w.s2.at[i], s.w.r2.at[i], far)

    def w_back(i, side):
        block = pair_at(s.w.fin, i, side)
        return remote(block, block, s.w.s3.at[i], s.w.r3.at[i], sib)

    def w_x(i):
        return remote(
            pair_at(s.w.fin, i, core),
            pair_at(s.w.oth, i, core),
            s.w.s4.at[i],
            s.w.r4.at[i],
            xp,
        )

    def w_pass(i, side):
        block = pair_at(s.w.oth, i, side)
        return remote(block, block, s.w.s5.at[i], s.w.r5.at[i], sib)

    def w_one(lower, upper):
        loop(lower, upper, lambda i: w_core(i).start())

    def w_two(lower, upper):
        def one(i):
            w_core(i).wait()
            mine = s.placed[rows_at((2 * i + core) * PAIR, PAIR), :].astype(F32)
            s.mrg[i] = (mine + s.sib[i].astype(F32)).astype(BF)
            w_far(i).start()

        loop(lower, upper, one)

    def w_three(i):
        w_far(i).wait()
        total = s.mrg[i].astype(F32) + s.w.far[i].astype(F32)
        s.w.fin[rows_at((2 * i + core) * PAIR, PAIR), :] = total.astype(BF)
        w_x(i).start()
        w_back(i, core).start()

    def w_four(i):
        w_x(i).wait()
        w_pass(i, core).start()

    def w_steps(lower, upper):
        for i in range(lower, upper):
            if i < half:
                w_three(i)
            if 0 <= i - LAG < half:
                w_four(i - LAG)

    def w_end_own(lower, upper):
        def one(i):
            w_back(i, core).wait_send()
            w_back(i, 1 - core).wait_recv()

        loop(lower, upper, one)

    def w_end_other(lower, upper):
        def one(i):
            w_pass(i, core).wait_send()
            w_pass(i, 1 - core).wait_recv()

        loop(lower, upper, one)

    def g_core(i, index, src, first):
        into, send, recv = ((s.sib, s.g.s0, s.g.r0), (s.g.sib1, s.g.s1, s.g.r1))[index]
        return remote(
            pair_at(src, i, 1 - core, first), into.at[i], send.at[i], recv.at[i], sib
        )

    def g_x(i):
        return remote(s.g.mrg1.at[i], s.g.xin.at[i], s.g.s2.at[i], s.g.r2.at[i], xp)

    def g_far(i):
        return remote(s.mrg.at[i], s.g.far.at[i], s.g.s3.at[i], s.g.r3.at[i], far)

    def g_back(i, side):
        block = pair_at(s.g.fin, i, side)
        return remote(block, block, s.g.s4.at[i], s.g.r4.at[i], sib)

    def g_one(index, lower, upper, src, first):
        loop(lower, upper, lambda i: g_core(i, index, src, first).start())

    def g_two(lower, upper, src, first):
        def one(i):
            g_core(i, 1, src, first).wait()
            mine = src[rows_at(first + (2 * i + core) * PAIR, PAIR), :].astype(F32)
            s.g.mrg1[i] = (mine + s.g.sib1[i].astype(F32)).astype(BF)
            g_x(i).start()

        loop(lower, upper, one)

    def g_two_own(lower, upper):
        loop(lower, upper, lambda i: g_core(i, 0, s.placed, 0).wait())

    def g_three(i):
        g_x(i).wait()
        mine = s.placed[rows_at((2 * i + core) * PAIR, PAIR), :].astype(F32)
        total = mine + s.sib[i].astype(F32) + s.g.xin[i].astype(F32)
        s.mrg[i] = total.astype(BF)
        g_far(i).start()

    def g_four(i):
        g_far(i).wait()
        total = s.mrg[i].astype(F32) + s.g.far[i].astype(F32)
        s.g.fin[rows_at((2 * i + core) * PAIR, PAIR), :] = total.astype(BF)
        g_back(i, core).start()

    thirds = head_part, head_part + (half - head_part) // 2, half
    g_order = list(range(thirds[1], half)) + list(range(head_part, thirds[1]))
    g_order += list(range(head_part))

    def g_steps(lower, upper):
        for k in range(lower, upper):
            if k < half:
                g_three(g_order[k])
            if 0 <= k - LAG < half:
                g_four(g_order[k - LAG])

    def g_end(lower, upper):
        def one(i):
            g_back(i, core).wait_send()
            g_back(i, 1 - core).wait_recv()

        loop(lower, upper, one)

    place(s.placed, 0, qkv_pairs, shift_qkv)
    place(s.placed, qkv_pairs, 2 * head_part, shift_rest)
    w_one(0, head_part)
    place(s.thin, 0, mod_pairs, 0)
    place(s.thin, mod_pairs, mod_pairs + time_pairs, qkv_pairs)


    for i in range(1, n_dp):
        tok_copy(i, lax.rem(dp - i + n_dp, n_dp)).wait_recv()
    for i in range(3):
        cols = D // 3
        s.mod_prod[:, i * cols : (i + 1) * cols] = nt(
            s.tok_all[...], s.thin[i * cols : (i + 1) * cols, :]
        )
    for group in range(n_dp):
        for i in range(D // 128):
            s.mod_pack[group, i : i + 1, :] = s.mod_prod[
                16 * group : 16 * group + 1, 128 * i : 128 * (i + 1)
            ]

    def mod_copy(i):
        group = lax.rem(dp + i, n_dp)
        return remote(
            s.mod_pack.at[group],
            s.mod_recv.at[i - 1],
            s.mod_s.at[i - 1],
            s.mod_r.at[i - 1],
            (group, t),
        )

    for i in range(1, n_dp):
        go(mod_copy(i))
    w_two(0, head_part)
    place(s.placed, 2 * head_part, wide_pairs, shift_rest)
    w_one(head_part, half)
    for i in range(1, n_dp):
        mod_copy(i).wait_recv()
    s.mod_all[t] = s.mod_pack[dp] + s.mod_recv[0] + s.mod_recv[1] + s.mod_recv[2]

    def mod_all_copy(i, member):
        block = s.mod_all.at[member]
        return remote(
            block,
            block,
            s.moda_s.at[i - 1],
            s.moda_r.at[i - 1],
            (dp, lax.rem(t + i, n_t)),
        )

    for i in range(1, n_t):
        go(mod_all_copy(i, t))
    w_two(head_part, half)
    w_steps(0, 1)
    for i in range(1, n_t):
        mod_all_copy(i, lax.rem(t - i + n_t, n_t)).wait_recv()

    lane = lax.broadcasted_iota(jnp.int32, (8, D), 1)

    def spread(vector):
        return jnp.broadcast_to(vector, (8, D))

    def unpack_rows(block):
        return jnp.concatenate([block[i : i + 1, :] for i in range(block.shape[0])], axis=1)

    for index, member in enumerate((t, t + 1 - 2 * xb)):
        line = spread(unpack_rows(s.mod_all[member][0 : D // 128, :]))
        moved = pltpu.roll(line, D - z.mod_rows, 1)
        s.time_qv[:, 512 * index : 512 * index + 256] = moved[:, 0:256]
        moved = pltpu.roll(line, D - z.mod_rows - hc, 1)
        s.time_qv[:, 512 * index + 256 : 512 * index + 512] = moved[:, 0:256]
    lines = [jnp.zeros((8, D), F32) for _ in range(6)]
    for member in range(n_t):
        first = member * z.mod_rows
        line = jnp.concatenate(
            [s.mod_all[member, i : i + 1, :] for i in range(8)]
            + [jnp.zeros((1, D - 1024), F32)],
            axis=1,
        )
        line = spread(line)
        for piece in range(6):
            lower = max(first, piece * D) - piece * D
            upper = min(first + z.mod_rows, (piece + 1) * D) - piece * D
            if lower < upper:
                moved = pltpu.roll(line, (first - piece * D) % D, 1) if (first - piece * D) % D else line
                lines[piece] = jnp.where((lane >= lower) & (lane < upper), moved, lines[piece])
    for piece in range(6):
        s.modv[piece : piece + 1, :] = lines[piece][0:1, :]

    def mod_line(piece):
        return s.modv[piece : piece + 1, :]

    def norm_parts(values):
        centred = values - jnp.mean(values, axis=-1, keepdims=True)
        inverse = lax.rsqrt(jnp.mean(centred * centred, axis=-1, keepdims=True) + eps_norm)
        return centred * inverse, inverse

    count_sum = counts[0]
    for i in range(1, n_dp):
        count_sum = count_sum + counts[i]
    group_scale = jnp.full((1, 1), counts[dp], jnp.int32).astype(F32) * n_dp / jnp.full(
        (1, 1), count_sum, jnp.int32
    ).astype(F32)

    live = (jnp.full((1, 1), xb, jnp.int32) < held[0]).astype(F32)
    for load in image_loads:
        load.wait()

    def mix_tile(i, carry):
        at = rows_at(i * TILE, TILE)
        normed, _ = norm_parts(s.x[at, :].astype(F32))
        s.u[at, :] = (normed * (1.0 + mod_line(1)) + mod_line(0)).astype(BF)
        dy = s.grad[at, :].astype(F32) * (group_scale * live)
        s.dmlp[at, :] = (mod_line(5) * dy).astype(BF)
        return carry

    w_steps(1, 2)
    lax.fori_loop(0, z.seq // TILE, mix_tile, 0)

    sets = range(2)
    weights = []
    for ref in (s.w.fin, s.w.oth):
        q, k, v, p = (ref.at[i * hc : (i + 1) * hc] for i in range(4))
        up = ref.at[4 * hc : 4 * hc + fc]
        down = ref.at[4 * hc + fc : 4 * hc + 2 * fc]
        weights.append(SimpleNamespace(q=q, k=k, v=v, p=p, up=up, down=down))

    head_of = lax.broadcasted_iota(jnp.int32, (1, hc), 1) // HEAD_DIM

    def only(values, head):
        return jnp.where(head_of == head, values, jnp.zeros_like(values))

    scale = HEAD_DIM ** (-0.5)

    def attend(index):
        own, at = weights[index], s.heads[index]
        mixed = s.u[...]
        q_bias = s.time_qv[0:1, 512 * index : 512 * index + hc]
        v_bias = s.time_qv[0:1, 512 * index + 256 : 512 * index + 256 + hc]
        q = (nt(mixed, own.q[...]) + q_bias).astype(BF)
        k = nt(mixed, own.k[...]).astype(BF)
        v = (nt(mixed, own.v[...]) + v_bias).astype(BF)
        at.q[...] = q
        at.k[...] = k
        at.v[...] = v
        out = jnp.zeros((z.seq, hc), F32)
        for head in range(z.heads):
            scores = nt(only(q, head), k) * scale
            e = jnp.exp(scores - jnp.max(scores, axis=-1, keepdims=True))
            p = e / jnp.sum(e, axis=-1, keepdims=True)
            s.soft[index * z.heads + head] = p
            out = out + times(p.astype(BF), only(v, head))
        at.o[...] = out.astype(BF)

    sh = z.shard

    def shard_of(ref, chip):
        return ref.at[rows_at(chip * sh, sh)]

    def rs_z(ph, k):
        if k == 2:
            return remote(ph.zout, ph.zin.at[2], ph.zs.at[2], ph.zr.at[2], across)
        block = shard_of(ph.part, (cross_z, near_z)[k])
        return remote(block, ph.zin.at[k], ph.zs.at[k], ph.zr.at[k], near)

    def rs_start(ph):
        go(rs_z(ph, 0))
        go(rs_z(ph, 1))

    def rs_middle(ph):
        rs_z(ph, 0).wait_recv()
        to_far = ph.part[rows_at(far_z * sh, sh), :].astype(F32)
        ph.zout[...] = (to_far + ph.zin[0].astype(F32)).astype(BF)
        go(rs_z(ph, 2))

    def rs_end(ph):
        total = ph.part[rows_at(za * sh, sh), :].astype(F32)
        for k in (1, 2):
            rs_z(ph, k).wait_recv()
            total = total + ph.zin[k].astype(F32)
        return total

    def ag_z(ph, chip, k):
        block = shard_of(ph.buf, chip)
        return remote(block, block, ph.zs.at[k], ph.zr.at[k], across if k == 0 else near)

    def ag_send(ph):
        go(ag_z(ph, za, 0))
        go(ag_z(ph, za, 1))

    def ag_start(ph, value):
        ph.buf[rows_at(za * sh, sh), :] = value
        ag_send(ph)

    def ag_middle(ph):
        ag_z(ph, far_z, 0).wait_recv()
        go(ag_z(ph, far_z, 2))

    def ag_end(ph):
        ag_z(ph, near_z, 1).wait_recv()
        ag_z(ph, cross_z, 2).wait_recv()

    parts = range(z.parts)

    def part_at(part):
        return slice(part * z.part_rows, (part + 1) * z.part_rows)

    w_steps(2, head_part)
    w_end_own(0, head_part)
    attend(0)
    w_steps(head_part, head_part + LAG)
    w_end_other(0, head_part)
    attend(1)
    for i in parts:
        total = 0.0
        for index in sets:
            total = total + times(s.heads[index].o[part_at(i), :], weights[index].p[...])
        s.rs1[i].part[...] = total.astype(BF)
        rs_start(s.rs1[i])
    w_steps(head_part + LAG, head_part + LAG + 2)
    for i in parts:
        rs_middle(s.rs1[i])
        w_steps(head_part + LAG + 2 + i, head_part + LAG + 3 + i)

    def mine_at(part):
        return rows_at(part * z.part_rows + za * sh, sh)

    for i in parts:
        attn = rs_end(s.rs1[i])
        if i:
            w_steps(head_part + LAG + 4, head_part + LAG + 5)
        h1 = s.x[mine_at(i), :].astype(F32) + mod_line(2) * attn
        normed_m, _ = norm_parts(h1)
        ag_start(s.ag1[i], (normed_m * (1.0 + mod_line(4)) + mod_line(3)).astype(BF))
        s.attn[i] = attn
        s.h1[i] = h1
    w_steps(head_part + LAG + 5, half - 3)
    for i in parts:
        ag_middle(s.ag1[i])
        w_steps(half - 3 + i, half - 2 + i)
    w_end_own(head_part, thirds[1])
    w_end_other(head_part, thirds[1])

    def mlp_up(part):
        at = part_at(part)
        for index in sets:
            hid = s.hid[index]
            hidden = nt(s.ag1[part].buf[...], weights[index].up[...])
            square = hidden * hidden
            bend = jnp.tanh(GELU_C * hidden * (1.0 + GELU_K * square))
            hid.gact[at, :] = (0.5 * hidden * (1.0 + bend)).astype(BF)
            hid.slope[at, :] = 0.5 * (1.0 + bend) + 0.5 * hidden * (1.0 - bend * bend) * (
                GELU_C * (1.0 + 3.0 * GELU_K * square)
            )

    def mlp_back(part):
        at = part_at(part)
        total = 0.0
        for index in sets:
            hid = s.hid[index]
            dgact = nt(s.dmlp[at, :], weights[index].down[...])
            dz = (dgact * hid.slope[at, :]).astype(BF)
            hid.dz[at, :] = dz
            total = total + times(dz, weights[index].up[...])
        s.rs2[part].part[...] = total.astype(BF)

    def down(part):
        total = 0.0
        for index in sets:
            total = total + times(s.hid[index].gact[part_at(part), :], weights[index].down[...])
        s.rs4[part].part[...] = total.astype(BF)

    cols = 384

    def over_parts(left, gathered, at):
        total = 0.0
        for part in parts:
            total = total + tn(left[part_at(part), :], gathered[part].buf[:, at])
        return total.astype(BF)

    def tiles(body):
        loop(0, D // cols, lambda i: body(pl.ds(pl.multiple_of(i * cols, 128), cols)))

    def up_grad(index, target, first):
        def tile(at):
            target[first : first + fc, at] = over_parts(s.hid[index].dz, s.ag1, at)

        tiles(tile)

    def down_grad(index, target, first):
        def tile(at):
            grad = tn(s.hid[index].gact[...], s.dmlp[:, at])
            target[first + fc : first + 2 * fc, at] = grad.astype(BF)

        tiles(tile)

    first_one = -4 * hc
    for i in parts:
        ag_end(s.ag1[i])
        w_steps(half - 1 + i, half + i)
        mlp_up(i)
    down_grad(1, s.thin, 0)
    g_one(1, thirds[1], half, s.thin, first_one)
    w_steps(half + 1, half + LAG)
    w_end_own(thirds[1], half)
    w_end_other(thirds[1], half)
    g_two(thirds[1], half, s.thin, first_one)
    for i in parts:
        mlp_back(i)
        rs_start(s.rs2[i])
    up_grad(1, s.thin, 0)
    g_one(1, head_part, thirds[1], s.thin, first_one)
    down_grad(0, s.placed, 4 * hc)
    g_one(0, thirds[1], half, s.placed, 0)
    g_two_own(thirds[1], half)
    for i in parts:
        rs_middle(s.rs2[i])
    g_two(head_part, thirds[1], s.thin, first_one)
    g_steps(0, 2)
    up_grad(0, s.placed, 4 * hc)
    g_one(0, head_part, thirds[1], s.placed, 0)
    for i in parts:
        down(i)
    g_two_own(head_part, thirds[1])

    def norm_back_of(normed, inverse, upstream):
        return inverse * (
            upstream
            - jnp.mean(upstream, axis=-1, keepdims=True)
            - normed * jnp.mean(upstream * normed, axis=-1, keepdims=True)
        )

    def column_sum(values):
        return jnp.sum(values, axis=0, keepdims=True)

    def dy_of(part):
        return s.grad[mine_at(part), :].astype(F32) * (group_scale * live)

    g_steps(2, 4)
    gate_a_sum = shift_m_sum = scale_m_sum = 0.0
    for i in parts:
        dw = rs_end(s.rs2[i])
        normed_m, inverse_m = norm_parts(s.h1[i])
        dh1 = dy_of(i) + norm_back_of(normed_m, inverse_m, dw * (1.0 + mod_line(4)))
        ag_start(s.ag2[i], (mod_line(2) * dh1).astype(BF))
        s.dh1[i] = dh1
        gate_a_sum = gate_a_sum + column_sum(dh1 * s.attn[i])
        shift_m_sum = shift_m_sum + column_sum(dw)
        scale_m_sum = scale_m_sum + column_sum(dw * normed_m)
    s.dmod[2:3, :] = gate_a_sum
    s.dmod[3:4, :] = shift_m_sum
    s.dmod[4:5, :] = scale_m_sum
    g_steps(4, 6)
    for i in parts:
        ag_middle(s.ag2[i])
        g_steps(6 + i, 7 + i)
    for i in parts:
        rs_start(s.rs4[i])

    def attend_back(index):
        own, at = weights[index], s.heads[index]
        do = jnp.concatenate([nt(s.ag2[i].buf[...], own.p[...]) for i in parts], axis=0)
        do = do.astype(BF)
        q, k, v = at.q[...], at.k[...], at.v[...]
        dq = jnp.zeros((z.seq, hc), F32)
        dk = jnp.zeros((z.seq, hc), F32)
        dv = jnp.zeros((z.seq, hc), F32)
        for head in range(z.heads):
            p = s.soft[index * z.heads + head]
            do_head = only(do, head)
            dp_soft = nt(do_head, v)
            inner = jnp.sum(p * dp_soft, axis=-1, keepdims=True)
            ds = (p * (dp_soft - inner)).astype(BF)
            dq = dq + times(ds, only(k, head))
            dk = dk + tn(ds, only(q, head))
            dv = dv + tn(p.astype(BF), do_head)
        at.dq[...] = (dq * scale).astype(BF)
        at.dk[...] = (dk * scale).astype(BF)
        at.dv[...] = dv.astype(BF)

    def proj_grad(index, target):
        def tile(at):
            target[3 * hc : 4 * hc, at] = over_parts(s.heads[index].o, s.ag2, at)

        tiles(tile)

    def attn_grad(index, target):
        own = s.heads[index]

        def tile(at):
            mixed = s.u[:, at]
            target[0:hc, at] = tn(own.dq[...], mixed).astype(BF)
            target[hc : 2 * hc, at] = tn(own.dk[...], mixed).astype(BF)
            target[2 * hc : 3 * hc, at] = tn(own.dv[...], mixed).astype(BF)

        tiles(tile)

    for i in parts:
        ag_end(s.ag2[i])
        g_steps(8 + i, 9 + i)
    attend_back(1)
    proj_grad(1, s.extra)
    attn_grad(1, s.extra)
    g_one(1, 0, head_part, s.extra, 0)
    g_steps(10, 11)
    attend_back(0)
    g_two(0, head_part, s.extra, 0)
    for i in parts:
        total = 0.0
        for index in sets:
            own, at = weights[index], s.heads[index]
            rows = part_at(i)
            total = total + times(at.dq[rows, :], own.q[...])
            total = total + times(at.dk[rows, :], own.k[...])
            total = total + times(at.dv[rows, :], own.v[...])
        s.rs3[i].part[...] = total.astype(BF)
        rs_start(s.rs3[i])
    g_steps(11, 12)
    proj_grad(0, s.placed)
    attn_grad(0, s.placed)
    g_one(0, 0, head_part, s.placed, 0)
    for i in parts:
        rs_middle(s.rs4[i])
    g_two_own(0, head_part)
    g_steps(12, 14)
    for i in parts:
        rs_middle(s.rs3[i])
    g_steps(14, 15)

    def dsum_copy():
        return remote(s.dsum, s.dsum_in, s.dsum_s.at[0], s.dsum_r.at[0], xp)

    s.dsum[...] = jnp.zeros((8, 256), F32)
    s.dsum[0:1, 0:hc] = column_sum(s.heads[1].dq[...].astype(F32))
    s.dsum[1:2, 0:hc] = column_sum(s.heads[1].dv[...].astype(F32))
    go(dsum_copy())

    gate_m_sum = 0.0
    for i in parts:
        mlp_sum = rs_end(s.rs4[i])
        gate_m_sum = gate_m_sum + column_sum(dy_of(i) * mlp_sum)
        result = (s.h1[i] + mod_line(5) * mlp_sum) * live
        s.bo[i * sh : (i + 1) * sh, :] = result.astype(BF)
    s.dmod[5:6, :] = gate_m_sum

    def bo_copy():
        return remote(s.bo, s.bo_in, s.bo_s.at[0], s.bo_r.at[0], xp)

    go(bo_copy())
    g_steps(15, 16)
    shift_a_sum = scale_a_sum = 0.0
    for i in parts:
        du = rs_end(s.rs3[i])
        g_steps(16 + i, 17 + i)
        normed_a, inverse_a = norm_parts(s.x[mine_at(i), :].astype(F32))
        dx = s.dh1[i] + norm_back_of(normed_a, inverse_a, du * (1.0 + mod_line(1)))
        s.ag3[i].buf[rows_at(za * sh, sh), :] = dx.astype(BF)
        shift_a_sum = shift_a_sum + column_sum(du)
        scale_a_sum = scale_a_sum + column_sum(du * normed_a)
    s.dmod[0:1, :] = shift_a_sum
    s.dmod[1:2, :] = scale_a_sum
    s.dmod[6:8, :] = jnp.zeros((2, D), F32)

    dlines = [spread(s.dmod[i : i + 1, :]) for i in range(6)]
    for member in range(n_t):
        first = member * z.mod_rows
        line = jnp.zeros((8, D), F32)
        for piece in range(6):
            lower = max(first, piece * D) - first
            upper = min(first + z.mod_rows, (piece + 1) * D) - first
            if lower < upper:
                back = (piece * D - first) % D
                moved = pltpu.roll(dlines[piece], back, 1) if back else dlines[piece]
                line = jnp.where((lane >= lower) & (lane < upper), moved, line)
        for i in range(8):
            s.dmod_pack[member, i : i + 1, :] = line[0:1, 128 * i : 128 * (i + 1)]

    def dmod_copy(i):
        member = lax.rem(t + i, n_t)
        return remote(
            s.dmod_pack.at[member],
            s.dmod_recv.at[i - 1],
            s.dmod_s.at[i - 1],
            s.dmod_r.at[i - 1],
            (dp, member),
        )

    for i in range(1, n_t):
        go(dmod_copy(i))
    for i in parts:
        ag_send(s.ag3[i])
    for i in parts:
        ag_middle(s.ag3[i])
    dsum_copy().wait_recv()
    total = s.dmod_pack[t]
    for i in range(1, n_t):
        dmod_copy(i).wait_recv()
        total = total + s.dmod_recv[i - 1]
    s.vec[dp] = jnp.zeros((16, 256), F32)
    s.vec[dp, 0:8, 0:128] = total
    own_sums = (column_sum(s.heads[0].dq[...].astype(F32)), column_sum(s.heads[0].dv[...].astype(F32)))
    s.vec[dp, 8:9, 0:hc] = own_sums[0] + s.dsum_in[0:1, 0:hc]
    s.vec[dp, 9:10, 0:hc] = own_sums[1] + s.dsum_in[1:2, 0:hc]

    def vec_copy(i, group):
        return remote(
            s.vec.at[group],
            s.vec.at[group],
            s.vec_s.at[i - 1],
            s.vec_r.at[i - 1],
            (lax.rem(dp + i, n_dp), t),
        )

    for i in range(1, n_dp):
        go(vec_copy(i, dp))
    g_steps(half, half + LAG)
    for i in parts:
        ag_end(s.ag3[i])
    g_end(0, half)
    for i in range(1, n_dp):
        vec_copy(i, lax.rem(dp - i + n_dp, n_dp)).wait_recv()
    group_lines = []
    for group in range(n_dp):
        line = [unpack_rows(s.vec[group, 0:8, 0:128]), jnp.zeros((1, D - 1024), F32)]
        line = spread(jnp.concatenate(line, axis=1))
        for index in range(2):
            ends = [s.vec[group, 8 + index : 9 + index, :], jnp.zeros((1, D - 256), F32)]
            ends = spread(jnp.concatenate(ends, axis=1))
            line = line + pltpu.roll(ends, z.mod_rows + index * hc, 1)
        group_lines.append(line[0:1, :])
    group_lines.append(jnp.zeros((8 - n_dp, D), F32))
    s.table[...] = jnp.transpose(jnp.concatenate(group_lines, axis=0))
    bo_copy().wait_recv()
    for copy in pending:
        copy.wait_send()

    outs = [(s.g.fin, out_g), (s.table, out_table), (s.tok_all, out_tok)]
    outs += [(s.bo, out_bo.at[xb]), (s.bo_in, out_bo.at[1 - xb])]
    for i in parts:
        outs.append((s.ag3[i].buf, out_ig.at[pl.ds(i * z.part_rows, z.part_rows)]))
    stores = [
        pltpu.make_async_copy(src, dst, s.out_sem.at[i]) for i, (src, dst) in enumerate(outs)
    ]
    for store in stores:
        store.start()
    for store in stores:
        store.wait()


def update_kernel(
    z,
    group_slots,
    owners,
    grads_hbm,
    table,
    tokens,
    master,
    first,
    second,
    new_first,
    new_second,
    new_master,
    bos,
    grads,
    sem,
):
    step = pl.program_id(0)
    dp = lax.axis_index("dp")

    @pl.when(step == 0)
    def _():
        load = pltpu.make_async_copy(grads_hbm, grads, sem)
        load.start()

        def clear(slot, carry):
            bos[slot] = -1
            return carry

        lax.fori_loop(0, z.slots, clear, 0)

        def note(block, taken):
            mine = owners[block] == dp

            @pl.when(mine & (taken < z.slots))
            def _():
                bos[taken] = block

            return taken + mine.astype(jnp.int32)

        lax.fori_loop(0, z.blocks, note, jnp.int32(0))
        load.wait()

    rows = z.block_rows
    mod_blocks = z.mod_rows // rows
    head_blocks = z.head_cols // rows
    fix_one = 1.0 - beta_one**STEP
    fix_two = 1.0 - beta_two**STEP

    def put(i, grad):
        weight = master[i]
        one = beta_one * first[i] + (1.0 - beta_one) * grad
        two = beta_two * second[i] + (1.0 - beta_two) * grad * grad
        new_first[i] = one
        new_second[i] = two
        spread = two * (1.0 / fix_two)
        root = spread * lax.rsqrt(spread)
        move = one * (learn_rate / fix_one) * pltpu.reciprocal(root + eps_adam)
        new_master[i] = weight * (1.0 - learn_rate * decay_rate) - move

    def slot(i, carry):
        block = bos[step * group_slots + i]
        is_mod = block < mod_blocks
        is_time = (block >= mod_blocks + 3 * head_blocks) & (block < mod_blocks + 5 * head_blocks)

        @pl.when(block < 0)
        def _():
            new_first[i] = jnp.zeros((rows, D), F32)
            new_second[i] = jnp.zeros((rows, D), F32)
            new_master[i] = jnp.zeros((rows, D), F32)

        @pl.when((block >= 0) & (is_mod | is_time))
        def _():
            index = jnp.where(is_mod, block, block - 3 * head_blocks)
            columns = table[pl.ds(pl.multiple_of(index * rows, 8), rows), :]
            grad = columns[:, 0:1] * tokens[0:1, :].astype(F32)
            for group in range(1, z.dp_count):
                grad = grad + columns[:, group : group + 1] * tokens[
                    16 * group : 16 * group + 1, :
                ].astype(F32)
            put(i, grad)

        is_wide = (block >= 0) & jnp.logical_not(is_mod | is_time)
        index = jnp.where(
            block < mod_blocks + 3 * head_blocks,
            block - mod_blocks,
            block - mod_blocks - 2 * head_blocks,
        )
        pair = jnp.clip(index, 0, z.wide // rows - 1) // 2 * PAIR

        @pl.when(is_wide & (lax.rem(index, 2) == 0))
        def _():
            put(i, grads[rows_at(pair, 32), :].astype(F32)[:rows])

        @pl.when(is_wide & (lax.rem(index, 2) == 1))
        def _():
            put(i, grads[rows_at(pair + 16, 32), :].astype(F32)[8:])

        return carry

    lax.fori_loop(0, group_slots, slot, 0)


def per_device_fast(
    z,
    inputs,
    out_grad,
    bucket,
    counts,
    images_held,
    owners,
    master_weight,
    first_moment,
    second_moment,
):
    token = jnp.broadcast_to(time_token(bucket[0]).astype(BF)[None, :], (16, D))
    plan = scratch_plan(z)
    smem = pl.BlockSpec(memory_space=pltpu.SMEM)
    vmem = pl.BlockSpec(memory_space=pltpu.VMEM)
    hbm = pl.BlockSpec(memory_space=pl.ANY)
    flops = 12 * z.seq * D * z.wide
    bo, own, grads, table, tokens = pl.pallas_call(
        partial(layer_kernel, z, plan),
        out_shape=(
            jax.ShapeDtypeStruct((2, z.parts * z.shard, D), BF),
            jax.ShapeDtypeStruct((z.seq, D), BF),
            jax.ShapeDtypeStruct((z.wide, D), BF),
            jax.ShapeDtypeStruct((z.thin, 8), F32),
            jax.ShapeDtypeStruct((16 * z.dp_count, D), BF),
        ),
        in_specs=[smem, smem, smem, vmem, hbm, hbm, hbm],
        out_specs=(hbm,) * 5,
        scratch_shapes=flatten(plan),
        compiler_params=pltpu.CompilerParams(
            collective_id=0, has_side_effects=True, vmem_limit_bytes=62 * 2**20
        ),
        cost_estimate=pl.CostEstimate(
            flops=flops, bytes_accessed=20 * 2**20, transcendentals=2 * z.seq * z.ffn_cols
        ),
        name="layer",
    )(
        owners,
        counts,
        images_held,
        token,
        inputs,
        out_grad,
        master_weight,
    )
    def partner(value, bits):
        swap = [(member, member ^ bits) for member in range(z.tensor_count)]
        return lax.ppermute(value, axes[1], swap)

    shards = [bo] + [partner(bo, 2 * step) for step in range(1, 4)]
    other = partner(own, 1)
    group_slots = next(size for size in (15, 12, 10, 8, 6, 5, 4, 3, 2, 1) if z.slots % size == 0)
    block = pl.BlockSpec((group_slots, z.block_rows, D), lambda i: (i, 0, 0))
    state = jax.ShapeDtypeStruct(master_weight.shape, F32)
    new_first, new_second, new_master = pl.pallas_call(
        partial(update_kernel, z, group_slots),
        grid=(z.slots // group_slots,),
        out_shape=(state,) * 3,
        in_specs=[smem, hbm, vmem, vmem, block, block, block],
        out_specs=(block,) * 3,
        scratch_shapes=[
            pltpu.SMEM((z.slots,), jnp.int32),
            pltpu.VMEM((z.wide, D), BF),
            pltpu.SemaphoreType.DMA,
        ],
        compiler_params=pltpu.CompilerParams(vmem_limit_bytes=60 * 2**20),
        cost_estimate=pl.CostEstimate(
            flops=20 * master_weight.size,
            bytes_accessed=24 * master_weight.size,
            transcendentals=2 * master_weight.size,
        ),
        name="update",
    )(owners, grads, table, tokens, master_weight, first_moment, second_moment)
    place = lax.axis_index(axes[1])
    even = lax.rem(place, 2) == 0
    for bit in (1, 2):
        swapped = lax.rem(place // (2 * bit), 2) == 1
        shards = [jnp.where(swapped, shards[step ^ bit], shards[step]) for step in range(4)]
    split = (z.images, z.parts, 1, z.shard, D)
    block_output = jnp.concatenate([shard.reshape(split) for shard in shards], axis=2)
    input_grad = jnp.stack([jnp.where(even, own, other), jnp.where(even, other, own)])
    return (
        block_output.reshape(inputs.shape),
        input_grad.astype(F32),
        new_first,
        new_second,
        new_master,
    )


def per_device(inputs, out_grad, bucket, counts, images_held, owners, master, first, second):
    sizes = Sizes(
        lax.axis_size("dp"),
        lax.axis_size("tensor"),
        master.shape[0],
        master.shape[1],
        inputs.shape[0],
        inputs.shape[1],
    )
    run = partial(per_device_fast, sizes) if sizes.fits() else per_device_plain
    return run(inputs, out_grad, bucket, counts, images_held, owners, master, first, second)


def solution(mesh):
    return jax.shard_map(
        per_device,
        mesh=mesh,
        in_specs=(
            P("dp", None, None),
            P("dp", None, None),
            P("dp"),
            P(),
            P("dp"),
            P(),
            P("dp", "tensor", None),
            P("dp", "tensor", None),
            P("dp", "tensor", None),
        ),
        out_specs=(
            P("dp", None, None),
            P("dp", None, None),
            P("dp", "tensor", None),
            P("dp", "tensor", None),
            P("dp", "tensor", None),
        ),
        check_vma=False,
    )
```

```python
from functools import partial
import math
from types import SimpleNamespace

import jax
import jax.numpy as jnp
from jax import lax
from jax.experimental import pallas as pl
from jax.experimental.pallas import tpu as pltpu
from jax.sharding import PartitionSpec as P

D = 1152
HEADS = 16
HEAD_DIM = 72
FF = 4608
NBUCKET = 8
STEP = 10


eps_norm = 1e-06
beta_one = 0.5
beta_two = 0.5
learn_rate = 0.03
decay_rate = 0.01
eps_adam = 1e-08


def time_token(bucket_value):
    half_width = D // 2
    freqs = jnp.exp(-math.log(10000.0) * jnp.arange(half_width, dtype=jnp.float32) / half_width)
    instant = (bucket_value.astype(jnp.float32) + 0.5) * (1000.0 / NBUCKET)
    angles = instant * freqs
    embed = jnp.concatenate([jnp.cos(angles), jnp.sin(angles)])
    return embed * jax.nn.sigmoid(embed)


def norm_stats(values):
    centred = values - jnp.mean(values, axis=-1, keepdims=True)
    inverse = lax.rsqrt(jnp.mean(centred * centred, axis=-1, keepdims=True) + eps_norm)
    return (centred * inverse, inverse)


def norm_back(normed, inverse, upstream):
    return inverse * (
        upstream
        - jnp.mean(upstream, axis=-1, keepdims=True)
        - normed * jnp.mean(upstream * normed, axis=-1, keepdims=True)
    )


def times_transposed(left, right):
    return lax.dot_general(
        left, right, (((1,), (1,)), ((), ())), preferred_element_type=jnp.float32
    )


def transposed_times(left, right):
    return lax.dot_general(
        left, right, (((0,), (0,)), ((), ())), preferred_element_type=jnp.float32
    )


def attend_forward(block):
    queries, key_rows, values = block
    scores = jnp.einsum(
        "bqhd,bkhd->bhqk", queries, key_rows, preferred_element_type=jnp.float32
    ) * HEAD_DIM ** (-0.5)
    row_peak = jnp.max(scores, axis=-1, keepdims=True)
    exp_scores = jnp.exp(scores - row_peak)
    row_total = jnp.sum(exp_scores, axis=-1, keepdims=True)
    soft = (exp_scores / row_total).astype(jnp.bfloat16)
    attended = jnp.einsum("bhqk,bkhd->bqhd", soft, values, preferred_element_type=jnp.float32)
    return (attended, row_peak[..., 0] + jnp.log(row_total[..., 0]))


def attend_backward(block):
    queries, key_rows, values, log_total, upstream = block
    scale_factor = HEAD_DIM ** (-0.5)
    scores = (
        jnp.einsum("bqhd,bkhd->bhqk", queries, key_rows, preferred_element_type=jnp.float32)
        * scale_factor
    )
    soft = jnp.exp(scores - log_total[..., None])
    grad_soft = jnp.einsum("bqhd,bkhd->bhqk", upstream, values, preferred_element_type=jnp.float32)
    inner_sum = jnp.sum(soft * grad_soft, axis=-1, keepdims=True)
    grad_scores = (soft * (grad_soft - inner_sum)).astype(jnp.bfloat16)
    grad_query = (
        jnp.einsum("bhqk,bkhd->bqhd", grad_scores, key_rows, preferred_element_type=jnp.float32)
        * scale_factor
    )
    grad_key = (
        jnp.einsum("bhqk,bqhd->bkhd", grad_scores, queries, preferred_element_type=jnp.float32)
        * scale_factor
    )
    grad_value = jnp.einsum(
        "bhqk,bqhd->bkhd", soft.astype(jnp.bfloat16), upstream, preferred_element_type=jnp.float32
    )
    return (grad_query, grad_key, grad_value)


def per_device_plain(
    inputs,
    out_grad,
    bucket,
    counts,
    images_held,
    owners,
    master_weight,
    first_moment,
    second_moment,
):
    dp_count = lax.axis_size("dp")
    tensor_count = lax.axis_size("tensor")
    dp_rank = lax.axis_index("dp")
    tensor_rank = lax.axis_index("tensor")
    own_slots = master_weight.shape[0]
    block_rows = master_weight.shape[1]
    head_cols = D // tensor_count
    ffn_cols = FF // tensor_count
    local_heads = HEADS // tensor_count
    local_rows = 12 * head_cols + 2 * ffn_cols
    block_count = local_rows // block_rows
    image_count = inputs.shape[0]
    seq_len = inputs.shape[1]
    row_count = image_count * seq_len
    block_ids = jnp.arange(block_count, dtype=jnp.int32)
    earlier = (owners[None, :] == owners[:, None]) & (block_ids[None, :] < block_ids[:, None])
    slot_of = owners * own_slots + jnp.sum(earlier.astype(jnp.int32), axis=1)
    gathered = lax.all_gather(master_weight.astype(jnp.bfloat16), "dp", axis=0, tiled=True)
    weights = gathered[slot_of].reshape(local_rows, D)
    w_mod = weights[: 6 * head_cols]
    w_qkv = weights[6 * head_cols : 9 * head_cols]
    w_qtime = weights[9 * head_cols : 10 * head_cols]
    w_vtime = weights[10 * head_cols : 11 * head_cols]
    w_proj = weights[11 * head_cols : 12 * head_cols]
    w_up = weights[12 * head_cols : 12 * head_cols + ffn_cols]
    w_down = weights[12 * head_cols + ffn_cols :]
    token = time_token(bucket[0]).astype(jnp.bfloat16)
    token_wide = token.astype(jnp.float32)
    mod_piece = jnp.dot(w_mod, token, preferred_element_type=jnp.float32)
    modulation = lax.all_gather(mod_piece, "tensor", axis=0, tiled=True)
    shift_a, scale_a, gate_a, shift_m, scale_m, gate_m = jnp.split(modulation, 6)
    counts_f = counts.astype(jnp.float32)
    group_scale = counts_f[dp_rank] * dp_count / jnp.sum(counts_f)
    flat_rows = inputs.reshape(row_count, D).astype(jnp.float32)
    live = (jnp.arange(row_count, dtype=jnp.int32) // seq_len < images_held[0]).astype(jnp.float32)[
        :, None
    ]
    normed_a, inverse_a = norm_stats(flat_rows)
    mixed_a = (normed_a * (1.0 + scale_a) + shift_a).astype(jnp.bfloat16)
    projected = times_transposed(mixed_a, w_qkv)
    time_query = jnp.dot(w_qtime, token, preferred_element_type=jnp.float32)
    time_value = jnp.dot(w_vtime, token, preferred_element_type=jnp.float32)
    queries = (projected[:, :head_cols] + time_query).astype(jnp.bfloat16)
    key_rows = projected[:, head_cols : 2 * head_cols].astype(jnp.bfloat16)
    values = (projected[:, 2 * head_cols :] + time_value).astype(jnp.bfloat16)
    group_imgs = math.gcd(image_count, max(1, 512 // seq_len))
    block_shape = (image_count // group_imgs, group_imgs, seq_len, local_heads, HEAD_DIM)
    q_blocks = queries.reshape(block_shape)
    k_blocks = key_rows.reshape(block_shape)
    v_blocks = values.reshape(block_shape)
    attended, log_total = lax.map(attend_forward, (q_blocks, k_blocks, v_blocks))
    heads_out = attended.reshape(row_count, head_cols).astype(jnp.bfloat16)
    heads_share = lax.psum_scatter(
        jnp.dot(heads_out, w_proj, preferred_element_type=jnp.float32).astype(jnp.bfloat16),
        "tensor",
        scatter_dimension=0,
        tiled=True,
    ).astype(jnp.float32)
    branch_a = lax.all_gather(
        heads_share.astype(jnp.bfloat16), "tensor", axis=0, tiled=True
    ).astype(heads_share.dtype)
    resid = flat_rows + gate_a * branch_a
    normed_m, inverse_m = norm_stats(resid)
    mixed_m = (normed_m * (1.0 + scale_m) + shift_m).astype(jnp.bfloat16)
    hidden = times_transposed(mixed_m, w_up)
    acted = jax.nn.gelu(hidden, approximate=True).astype(jnp.bfloat16)
    hidden_share = lax.psum_scatter(
        jnp.dot(acted, w_down, preferred_element_type=jnp.float32).astype(jnp.bfloat16),
        "tensor",
        scatter_dimension=0,
        tiled=True,
    ).astype(jnp.float32)
    branch_m = lax.all_gather(
        hidden_share.astype(jnp.bfloat16), "tensor", axis=0, tiled=True
    ).astype(hidden_share.dtype)
    result = resid + gate_m * branch_m
    block_output = (result * live).astype(jnp.bfloat16).reshape(inputs.shape)
    grad_y = out_grad.reshape(row_count, D).astype(jnp.float32) * (group_scale * live)
    grad_branch_m = (gate_m * grad_y).astype(jnp.bfloat16)
    grad_gate_m = jnp.sum(grad_y * branch_m, axis=0)
    grad_acted = times_transposed(grad_branch_m, w_down)
    grad_down = transposed_times(acted, grad_branch_m)
    grad_hidden = jax.vjp(partial(jax.nn.gelu, approximate=True), hidden)[1](grad_acted)[0].astype(
        jnp.bfloat16
    )
    grad_up = transposed_times(grad_hidden, mixed_m)
    mlp_grad_share = lax.psum_scatter(
        jnp.dot(grad_hidden, w_up, preferred_element_type=jnp.float32).astype(jnp.bfloat16),
        "tensor",
        scatter_dimension=0,
        tiled=True,
    ).astype(jnp.float32)
    grad_mixed_m = lax.all_gather(
        mlp_grad_share.astype(jnp.bfloat16), "tensor", axis=0, tiled=True
    ).astype(mlp_grad_share.dtype)
    grad_shift_m = jnp.sum(grad_mixed_m, axis=0)
    grad_scale_m = jnp.sum(grad_mixed_m * normed_m, axis=0)
    grad_resid = grad_y + norm_back(normed_m, inverse_m, grad_mixed_m * (1.0 + scale_m))
    grad_branch_a = (gate_a * grad_resid).astype(jnp.bfloat16)
    grad_gate_a = jnp.sum(grad_resid * branch_a, axis=0)
    grad_heads = times_transposed(grad_branch_a, w_proj).astype(jnp.bfloat16)
    grad_proj = transposed_times(heads_out, grad_branch_a)
    grads_query, grads_key, grads_value = lax.map(
        attend_backward, (q_blocks, k_blocks, v_blocks, log_total, grad_heads.reshape(block_shape))
    )
    grad_qkv = jnp.concatenate(
        [
            grads_query.reshape(row_count, head_cols),
            grads_key.reshape(row_count, head_cols),
            grads_value.reshape(row_count, head_cols),
        ],
        axis=1,
    ).astype(jnp.bfloat16)
    grad_wqkv = transposed_times(grad_qkv, mixed_a)
    attn_grad_share = lax.psum_scatter(
        jnp.dot(grad_qkv, w_qkv, preferred_element_type=jnp.float32).astype(jnp.bfloat16),
        "tensor",
        scatter_dimension=0,
        tiled=True,
    ).astype(jnp.float32)
    grad_mixed_a = lax.all_gather(
        attn_grad_share.astype(jnp.bfloat16), "tensor", axis=0, tiled=True
    ).astype(attn_grad_share.dtype)
    token_sums = jnp.sum(grad_qkv, axis=0, dtype=jnp.float32)
    grad_qtime = token_sums[:head_cols, None] * token_wide[None, :]
    grad_vtime = token_sums[2 * head_cols :, None] * token_wide[None, :]
    grad_shift_a = jnp.sum(grad_mixed_a, axis=0)
    grad_scale_a = jnp.sum(grad_mixed_a * normed_a, axis=0)
    grad_in = grad_resid + norm_back(normed_a, inverse_a, grad_mixed_a * (1.0 + scale_a))
    grad_mod = jnp.concatenate(
        [grad_shift_a, grad_scale_a, grad_gate_a, grad_shift_m, grad_scale_m, grad_gate_m]
    )
    grad_mod_piece = lax.dynamic_slice_in_dim(grad_mod, tensor_rank * 6 * head_cols, 6 * head_cols)
    grad_wmod = grad_mod_piece[:, None] * token_wide[None, :]
    grads = jnp.concatenate(
        [grad_wmod, grad_wqkv, grad_qtime, grad_vtime, grad_proj, grad_up, grad_down], axis=0
    )
    grad_blocks = grads.reshape(block_count, block_rows, D)
    owned_blocks = jnp.full((dp_count * own_slots,), -1, jnp.int32).at[slot_of].set(block_ids)
    mine = lax.dynamic_slice_in_dim(owned_blocks, dp_rank * own_slots, own_slots)
    filled = (mine >= 0)[:, None, None]
    placed = (
        jnp.zeros((dp_count * own_slots, block_rows, D), jnp.float32).at[slot_of].set(grad_blocks)
    )
    reduced = lax.psum_scatter(
        placed.astype(jnp.bfloat16), "dp", scatter_dimension=0, tiled=True
    ).astype(jnp.float32)
    new_first = beta_one * first_moment + (1.0 - beta_one) * reduced
    new_second = beta_two * second_moment + (1.0 - beta_two) * reduced * reduced
    fix_one = 1.0 - beta_one**STEP
    fix_two = 1.0 - beta_two**STEP
    change = (
        new_first / fix_one / (jnp.sqrt(new_second / fix_two) + eps_adam)
        + decay_rate * master_weight
    )
    new_master = master_weight - learn_rate * change
    return (
        block_output,
        grad_in.reshape(inputs.shape),
        jnp.where(filled, new_first, 0.0),
        jnp.where(filled, new_second, 0.0),
        jnp.where(filled, new_master, 0.0),
    )


BF = jnp.bfloat16
F32 = jnp.float32
MESH = pl.DeviceIdType.MESH
axes = ("dp", "tensor")
TILE = 64
LAG = 2
PAIR = 48
GELU_C = math.sqrt(2.0 / math.pi)
GELU_K = 0.044715


def rows_at(start, size):
    return pl.ds(pl.multiple_of(start, 16), size)


def remote(src, dst, send_sem, recv_sem, device):
    return pltpu.make_async_remote_copy(
        src_ref=src,
        dst_ref=dst,
        send_sem=send_sem,
        recv_sem=recv_sem,
        device_id=device,
        device_id_type=MESH,
    )


def times(left, right):
    return jnp.dot(left, right, preferred_element_type=F32)


class Sizes:
    def __init__(self, dp_count, tensor_count, slots, block_rows, images, seq):
        self.dp_count, self.tensor_count = dp_count, tensor_count
        self.slots, self.block_rows = slots, block_rows
        self.images, self.seq = images, seq
        self.parts = 2
        self.part_rows = seq // self.parts
        self.shard = self.part_rows // 4
        self.head_cols = D // tensor_count
        self.ffn_cols = FF // tensor_count
        self.heads = HEADS // tensor_count
        self.mod_rows = 6 * self.head_cols
        self.local_rows = 12 * self.head_cols + 2 * self.ffn_cols
        self.blocks = self.local_rows // block_rows
        self.wide = 4 * self.head_cols + 2 * self.ffn_cols
        self.thin = self.mod_rows + 2 * self.head_cols

    def fits(self):
        return (
            self.dp_count == 4
            and self.tensor_count == 8
            and self.images == 2
            and 2 * self.block_rows == PAIR
            and self.slots % 3 == 0
            and self.seq % 128 == 0
            and self.head_cols % PAIR == 0
            and self.ffn_cols % PAIR == 0
            and self.wide % (6 * PAIR) == 0
            and self.thin == D
            and self.thin == 2 * self.ffn_cols
            and self.mod_rows <= 1024
        )


def flatten(plan):
    if isinstance(plan, SimpleNamespace):
        return flatten(list(vars(plan).values()))
    if isinstance(plan, list):
        return [leaf for member in plan for leaf in flatten(member)]
    return [plan]


def rebuild(plan, leaves):
    if isinstance(plan, SimpleNamespace):
        return SimpleNamespace(**{key: rebuild(value, leaves) for key, value in vars(plan).items()})
    if isinstance(plan, list):
        return [rebuild(member, leaves) for member in plan]
    return next(leaves)


def scratch_plan(z):
    dma = pltpu.SemaphoreType.DMA
    vm = pltpu.VMEM
    half = z.wide // PAIR // 2

    def pairs():
        return vm((half, PAIR, D), BF)

    def attention():
        names = 7
        q, k, v, o, dq, dk, dv = (vm((z.seq, z.head_cols), BF) for _ in range(names))
        return SimpleNamespace(q=q, k=k, v=v, o=o, dq=dq, dk=dk, dv=dv)

    def hidden():
        return SimpleNamespace(
            slope=vm((z.seq, z.ffn_cols), F32),
            gact=vm((z.seq, z.ffn_cols), BF),
            dz=vm((z.seq, z.ffn_cols), BF),
        )

    def scatter():
        return SimpleNamespace(
            part=vm((z.part_rows, D), BF),
            zout=vm((z.shard, D), BF),
            zin=vm((3, z.shard, D), BF),
            zs=dma((3,)),
            zr=dma((3,)),
        )

    def gather():
        return SimpleNamespace(buf=vm((z.part_rows, D), BF), zs=dma((3,)), zr=dma((3,)))

    def each(make):
        return [make() for _ in range(z.parts)]

    return SimpleNamespace(
        slot_table=pltpu.SMEM((z.blocks,), jnp.int32),
        master=vm((z.slots, z.block_rows, D), F32),
        master_sem=dma((3,)),
        x=vm((z.seq, D), BF),
        grad=vm((z.seq, D), BF),
        in_sem=dma((2,)),
        placed=vm((z.wide, D), BF),
        thin=vm((z.thin, D), BF),
        extra=vm((4 * z.head_cols, D), BF),
        tok_all=vm((16 * z.dp_count, D), BF),
        tok_s=dma((3,)),
        tok_r=dma((3,)),
        mod_prod=vm((16 * z.dp_count, D), F32),
        mod_pack=vm((z.dp_count, 16, 128), F32),
        mod_recv=vm((3, 16, 128), F32),
        mod_s=dma((3,)),
        mod_r=dma((3,)),
        mod_all=vm((z.tensor_count, 16, 128), F32),
        moda_s=dma((z.tensor_count - 1,)),
        moda_r=dma((z.tensor_count - 1,)),
        modv=vm((8, D), F32),
        time_qv=vm((8, 4 * 256), F32),
        u=vm((z.seq, D), BF),
        dmlp=vm((z.seq, D), BF),
        heads=[attention(), attention()],
        soft=vm((2 * z.heads, z.seq, z.seq), F32),
        hid=[hidden(), hidden()],
        h1=vm((z.parts, z.shard, D), F32),
        attn=vm((z.parts, z.shard, D), F32),
        dh1=vm((z.parts, z.shard, D), F32),
        dmod=vm((8, D), F32),
        dmod_pack=vm((z.tensor_count, 8, 128), F32),
        dmod_recv=vm((z.tensor_count - 1, 8, 128), F32),
        dmod_s=dma((z.tensor_count - 1,)),
        dmod_r=dma((z.tensor_count - 1,)),
        dsum=vm((8, 256), F32),
        dsum_in=vm((8, 256), F32),
        dsum_s=dma((1,)),
        dsum_r=dma((1,)),
        vec=vm((z.dp_count, 16, 256), F32),
        table=vm((z.thin, 8), F32),
        vec_s=dma((3,)),
        vec_r=dma((3,)),
        out_sem=dma((5 + z.parts,)),
        sib=pairs(),
        mrg=pairs(),
        w=SimpleNamespace(
            far=pairs(),
            fin=vm((z.wide, D), BF),
            oth=vm((z.wide, D), BF),
            s1=dma((half,)),
            r1=dma((half,)),
            s2=dma((half,)),
            r2=dma((half,)),
            s3=dma((half,)),
            r3=dma((half,)),
            s4=dma((half,)),
            r4=dma((half,)),
            s5=dma((half,)),
            r5=dma((half,)),
        ),
        g=SimpleNamespace(
            far=pairs(),
            fin=vm((z.wide, D), BF),
            sib1=pairs(),
            mrg1=pairs(),
            xin=pairs(),
            s0=dma((half,)),
            r0=dma((half,)),
            s1=dma((half,)),
            r1=dma((half,)),
            s2=dma((half,)),
            r2=dma((half,)),
            s3=dma((half,)),
            r3=dma((half,)),
            s4=dma((half,)),
            r4=dma((half,)),
        ),
        rs1=each(scatter),
        rs2=each(scatter),
        rs3=each(scatter),
        rs4=each(scatter),
        ag1=each(gather),
        ag2=each(gather),
        ag3=each(gather),
        bo=vm((z.parts * z.shard, D), BF),
        bo_in=vm((z.parts * z.shard, D), BF),
        bo_s=dma((1,)),
        bo_r=dma((1,)),
    )


def layer_kernel(z, plan, *refs):
    owners, counts, held, tok, x_hbm, grad_hbm, master_hbm = refs[:7]
    out_bo, out_ig, out_g, out_table, out_tok = refs[7:12]
    s = rebuild(plan, iter(refs[12:]))
    nt_dims = (((1,), (1,)), ((), ()))
    tn_dims = (((0,), (0,)), ((), ()))

    def nt(left, right):
        return lax.dot_general(left, right, nt_dims, preferred_element_type=F32)

    def tn(left, right):
        return lax.dot_general(left, right, tn_dims, preferred_element_type=F32)

    hc, fc = z.head_cols, z.ffn_cols
    n_dp, n_t = z.dp_count, z.tensor_count
    dp, t = lax.axis_index("dp"), lax.axis_index("tensor")
    core = lax.rem(dp, 2)
    za, xb = t // 2, lax.rem(t, 2)
    near_z = za + 1 - 2 * lax.rem(za, 2)
    far_z = lax.rem(za + 2, 4)
    cross_z = 3 - za
    sib = (dp + 1 - 2 * core, t)
    far = (lax.rem(dp + 2, 4), t)
    xp = (dp, t + 1 - 2 * xb)
    near, across = (dp, 2 * near_z + xb), (dp, 2 * far_z + xb)
    half = z.wide // PAIR // 2
    head_part = (4 * hc) // PAIR // 2
    pending = []

    def go(copy):
        copy.start()
        pending.append(copy)

    third = z.slots // 3
    loads = [
        pltpu.make_async_copy(
            master_hbm.at[pl.ds(i * third, third)],
            s.master.at[pl.ds(i * third, third)],
            s.master_sem.at[i],
        )
        for i in range(3)
    ]
    image_loads = [
        pltpu.make_async_copy(x_hbm.at[xb], s.x, s.in_sem.at[0]),
        pltpu.make_async_copy(grad_hbm.at[xb], s.grad, s.in_sem.at[1]),
    ]
    for load in loads + image_loads:
        load.start()

    barrier = pltpu.get_barrier_semaphore()
    for i in range(1, n_dp):
        pl.semaphore_signal(
            barrier, inc=1, device_id=(lax.rem(dp + i, n_dp), t), device_id_type=MESH
        )
    for i in range(1, n_t):
        pl.semaphore_signal(
            barrier, inc=1, device_id=(dp, lax.rem(t + i, n_t)), device_id_type=MESH
        )
    pl.semaphore_wait(barrier, n_dp + n_t - 2)

    s.tok_all[rows_at(dp * 16, 16), :] = tok[...]

    def tok_copy(i, group):
        block = s.tok_all.at[rows_at(group * 16, 16)]
        return remote(
            block,
            block,
            s.tok_s.at[i - 1],
            s.tok_r.at[i - 1],
            (lax.rem(dp + i, n_dp), t),
        )

    for i in range(1, n_dp):
        go(tok_copy(i, dp))

    def note_slot(block, taken):
        mine = owners[block] == dp
        s.slot_table[block] = jnp.where(mine, taken, -1)
        return taken + mine.astype(jnp.int32)

    lax.fori_loop(0, z.blocks, note_slot, jnp.int32(0))
    for load in loads:
        load.wait()

    def place(into, lower, upper, shift):
        def one(pair, carry):
            halves = []
            for side in range(2):
                slot = s.slot_table[2 * (pair + shift) + side]
                block = s.master[jnp.clip(slot, 0, z.slots - 1)]
                halves.append(jnp.where(slot >= 0, block, 0.0))
            into[rows_at(pair * PAIR, PAIR), :] = jnp.concatenate(halves, axis=0).astype(BF)
            return carry

        lax.fori_loop(lower, upper, one, 0)

    qkv_pairs, mod_pairs = 3 * hc // PAIR, z.mod_rows // PAIR
    time_pairs = 2 * hc // PAIR
    wide_pairs = z.wide // PAIR
    shift_qkv = mod_pairs
    shift_rest = mod_pairs + time_pairs

    def loop(lower, upper, body):
        lax.fori_loop(lower, upper, lambda i, carry: (body(i), carry)[1], 0)

    def pair_at(ref, i, side, first=0):
        return ref.at[rows_at(first + (2 * i + side) * PAIR, PAIR)]

    def w_core(i):
        return remote(
            pair_at(s.placed, i, 1 - core), s.sib.at[i], s.w.s1.at[i], s.w.r1.at[i], sib
        )

    def w_far(i):
        return remote(s.mrg.at[i], s.w.far.at[i], s.w.s2.at[i], s.w.r2.at[i], far)

    def w_back(i, side):
        block = pair_at(s.w.fin, i, side)
        return remote(block, block, s.w.s3.at[i], s.w.r3.at[i], sib)

    def w_x(i):
        return remote(
            pair_at(s.w.fin, i, core),
            pair_at(s.w.oth, i, core),
            s.w.s4.at[i],
            s.w.r4.at[i],
            xp,
        )

    def w_pass(i, side):
        block = pair_at(s.w.oth, i, side)
        return remote(block, block, s.w.s5.at[i], s.w.r5.at[i], sib)

    def w_one(lower, upper):
        loop(lower, upper, lambda i: w_core(i).start())

    def w_two(lower, upper):
        def one(i):
            w_core(i).wait()
            mine = s.placed[rows_at((2 * i + core) * PAIR, PAIR), :].astype(F32)
            s.mrg[i] = (mine + s.sib[i].astype(F32)).astype(BF)
            w_far(i).start()

        loop(lower, upper, one)

    def w_three(i):
        w_far(i).wait()
        total = s.mrg[i].astype(F32) + s.w.far[i].astype(F32)
        s.w.fin[rows_at((2 * i + core) * PAIR, PAIR), :] = total.astype(BF)
        w_x(i).start()
        w_back(i, core).start()

    def w_four(i):
        w_x(i).wait()
        w_pass(i, core).start()

    def w_steps(lower, upper):
        for i in range(lower, upper):
            if i < half:
                w_three(i)
            if 0 <= i - LAG < half:
                w_four(i - LAG)

    def w_end_own(lower, upper):
        def one(i):
            w_back(i, core).wait_send()
            w_back(i, 1 - core).wait_recv()

        loop(lower, upper, one)

    def w_end_other(lower, upper):
        def one(i):
            w_pass(i, core).wait_send()
            w_pass(i, 1 - core).wait_recv()

        loop(lower, upper, one)

    def g_core(i, index, src, first):
        into, send, recv = ((s.sib, s.g.s0, s.g.r0), (s.g.sib1, s.g.s1, s.g.r1))[index]
        return remote(
            pair_at(src, i, 1 - core, first), into.at[i], send.at[i], recv.at[i], sib
        )

    def g_x(i):
        return remote(s.g.mrg1.at[i], s.g.xin.at[i], s.g.s2.at[i], s.g.r2.at[i], xp)

    def g_far(i):
        return remote(s.mrg.at[i], s.g.far.at[i], s.g.s3.at[i], s.g.r3.at[i], far)

    def g_back(i, side):
        block = pair_at(s.g.fin, i, side)
        return remote(block, block, s.g.s4.at[i], s.g.r4.at[i], sib)

    def g_one(index, lower, upper, src, first):
        loop(lower, upper, lambda i: g_core(i, index, src, first).start())

    def g_two(lower, upper, src, first):
        def one(i):
            g_core(i, 1, src, first).wait()
            mine = src[rows_at(first + (2 * i + core) * PAIR, PAIR), :].astype(F32)
            s.g.mrg1[i] = (mine + s.g.sib1[i].astype(F32)).astype(BF)
            g_x(i).start()

        loop(lower, upper, one)

    def g_two_own(lower, upper):
        loop(lower, upper, lambda i: g_core(i, 0, s.placed, 0).wait())

    def g_three(i):
        g_x(i).wait()
        mine = s.placed[rows_at((2 * i + core) * PAIR, PAIR), :].astype(F32)
        total = mine + s.sib[i].astype(F32) + s.g.xin[i].astype(F32)
        s.mrg[i] = total.astype(BF)
        g_far(i).start()

    def g_four(i):
        g_far(i).wait()
        total = s.mrg[i].astype(F32) + s.g.far[i].astype(F32)
        s.g.fin[rows_at((2 * i + core) * PAIR, PAIR), :] = total.astype(BF)
        g_back(i, core).start()

    thirds = head_part, head_part + (half - head_part) // 2, half
    g_order = list(range(thirds[1], half)) + list(range(head_part, thirds[1]))
    g_order += list(range(head_part))

    def g_steps(lower, upper):
        for k in range(lower, upper):
            if k < half:
                g_three(g_order[k])
            if 0 <= k - LAG < half:
                g_four(g_order[k - LAG])

    def g_end(lower, upper):
        def one(i):
            g_back(i, core).wait_send()
            g_back(i, 1 - core).wait_recv()

        loop(lower, upper, one)

    place(s.placed, 0, qkv_pairs, shift_qkv)
    place(s.placed, qkv_pairs, 2 * head_part, shift_rest)
    w_one(0, head_part)
    place(s.thin, 0, mod_pairs, 0)
    place(s.thin, mod_pairs, mod_pairs + time_pairs, qkv_pairs)


    for i in range(1, n_dp):
        tok_copy(i, lax.rem(dp - i + n_dp, n_dp)).wait_recv()
    for i in range(3):
        cols = D // 3
        s.mod_prod[:, i * cols : (i + 1) * cols] = nt(
            s.tok_all[...], s.thin[i * cols : (i + 1) * cols, :]
        )
    for group in range(n_dp):
        for i in range(D // 128):
            s.mod_pack[group, i : i + 1, :] = s.mod_prod[
                16 * group : 16 * group + 1, 128 * i : 128 * (i + 1)
            ]

    def mod_copy(i):
        group = lax.rem(dp + i, n_dp)
        return remote(
            s.mod_pack.at[group],
            s.mod_recv.at[i - 1],
            s.mod_s.at[i - 1],
            s.mod_r.at[i - 1],
            (group, t),
        )

    for i in range(1, n_dp):
        go(mod_copy(i))
    w_two(0, head_part)
    place(s.placed, 2 * head_part, wide_pairs, shift_rest)
    w_one(head_part, half)
    for i in range(1, n_dp):
        mod_copy(i).wait_recv()
    s.mod_all[t] = s.mod_pack[dp] + s.mod_recv[0] + s.mod_recv[1] + s.mod_recv[2]

    def mod_all_copy(i, member):
        block = s.mod_all.at[member]
        return remote(
            block,
            block,
            s.moda_s.at[i - 1],
            s.moda_r.at[i - 1],
            (dp, lax.rem(t + i, n_t)),
        )

    for i in range(1, n_t):
        go(mod_all_copy(i, t))
    w_two(head_part, half)
    w_steps(0, 1)
    for i in range(1, n_t):
        mod_all_copy(i, lax.rem(t - i + n_t, n_t)).wait_recv()

    lane = lax.broadcasted_iota(jnp.int32, (8, D), 1)

    def spread(vector):
        return jnp.broadcast_to(vector, (8, D))

    def unpack_rows(block):
        return jnp.concatenate([block[i : i + 1, :] for i in range(block.shape[0])], axis=1)

    for index, member in enumerate((t, t + 1 - 2 * xb)):
        line = spread(unpack_rows(s.mod_all[member][0 : D // 128, :]))
        moved = pltpu.roll(line, D - z.mod_rows, 1)
        s.time_qv[:, 512 * index : 512 * index + 256] = moved[:, 0:256]
        moved = pltpu.roll(line, D - z.mod_rows - hc, 1)
        s.time_qv[:, 512 * index + 256 : 512 * index + 512] = moved[:, 0:256]
    lines = [jnp.zeros((8, D), F32) for _ in range(6)]
    for member in range(n_t):
        first = member * z.mod_rows
        line = jnp.concatenate(
            [s.mod_all[member, i : i + 1, :] for i in range(8)]
            + [jnp.zeros((1, D - 1024), F32)],
            axis=1,
        )
        line = spread(line)
        for piece in range(6):
            lower = max(first, piece * D) - piece * D
            upper = min(first + z.mod_rows, (piece + 1) * D) - piece * D
            if lower < upper:
                moved = pltpu.roll(line, (first - piece * D) % D, 1) if (first - piece * D) % D else line
                lines[piece] = jnp.where((lane >= lower) & (lane < upper), moved, lines[piece])
    for piece in range(6):
        s.modv[piece : piece + 1, :] = lines[piece][0:1, :]

    def mod_line(piece):
        return s.modv[piece : piece + 1, :]

    def norm_parts(values):
        centred = values - jnp.mean(values, axis=-1, keepdims=True)
        inverse = lax.rsqrt(jnp.mean(centred * centred, axis=-1, keepdims=True) + eps_norm)
        return centred * inverse, inverse

    count_sum = counts[0]
    for i in range(1, n_dp):
        count_sum = count_sum + counts[i]
    group_scale = jnp.full((1, 1), counts[dp], jnp.int32).astype(F32) * n_dp / jnp.full(
        (1, 1), count_sum, jnp.int32
    ).astype(F32)

    live = (jnp.full((1, 1), xb, jnp.int32) < held[0]).astype(F32)
    for load in image_loads:
        load.wait()

    def mix_tile(i, carry):
        at = rows_at(i * TILE, TILE)
        normed, _ = norm_parts(s.x[at, :].astype(F32))
        s.u[at, :] = (normed * (1.0 + mod_line(1)) + mod_line(0)).astype(BF)
        dy = s.grad[at, :].astype(F32) * (group_scale * live)
        s.dmlp[at, :] = (mod_line(5) * dy).astype(BF)
        return carry

    w_steps(1, 2)
    lax.fori_loop(0, z.seq // TILE, mix_tile, 0)

    sets = range(2)
    weights = []
    for ref in (s.w.fin, s.w.oth):
        q, k, v, p = (ref.at[i * hc : (i + 1) * hc] for i in range(4))
        up = ref.at[4 * hc : 4 * hc + fc]
        down = ref.at[4 * hc + fc : 4 * hc + 2 * fc]
        weights.append(SimpleNamespace(q=q, k=k, v=v, p=p, up=up, down=down))

    head_of = lax.broadcasted_iota(jnp.int32, (1, hc), 1) // HEAD_DIM

    def only(values, head):
        return jnp.where(head_of == head, values, jnp.zeros_like(values))

    scale = HEAD_DIM ** (-0.5)

    def attend(index):
        own, at = weights[index], s.heads[index]
        mixed = s.u[...]
        q_bias = s.time_qv[0:1, 512 * index : 512 * index + hc]
        v_bias = s.time_qv[0:1, 512 * index + 256 : 512 * index + 256 + hc]
        q = (nt(mixed, own.q[...]) + q_bias).astype(BF)
        k = nt(mixed, own.k[...]).astype(BF)
        v = (nt(mixed, own.v[...]) + v_bias).astype(BF)
        at.q[...] = q
        at.k[...] = k
        at.v[...] = v
        out = jnp.zeros((z.seq, hc), F32)
        for head in range(z.heads):
            scores = nt(only(q, head), k) * scale
            e = jnp.exp(scores - jnp.max(scores, axis=-1, keepdims=True))
            p = e / jnp.sum(e, axis=-1, keepdims=True)
            s.soft[index * z.heads + head] = p
            out = out + times(p.astype(BF), only(v, head))
        at.o[...] = out.astype(BF)

    sh = z.shard

    def shard_of(ref, chip):
        return ref.at[rows_at(chip * sh, sh)]

    def rs_z(ph, k):
        if k == 2:
            return remote(ph.zout, ph.zin.at[2], ph.zs.at[2], ph.zr.at[2], across)
        block = shard_of(ph.part, (cross_z, near_z)[k])
        return remote(block, ph.zin.at[k], ph.zs.at[k], ph.zr.at[k], near)

    def rs_start(ph):
        go(rs_z(ph, 0))
        go(rs_z(ph, 1))

    def rs_middle(ph):
        rs_z(ph, 0).wait_recv()
        to_far = ph.part[rows_at(far_z * sh, sh), :].astype(F32)
        ph.zout[...] = (to_far + ph.zin[0].astype(F32)).astype(BF)
        go(rs_z(ph, 2))

    def rs_end(ph):
        total = ph.part[rows_at(za * sh, sh), :].astype(F32)
        for k in (1, 2):
            rs_z(ph, k).wait_recv()
            total = total + ph.zin[k].astype(F32)
        return total

    def ag_z(ph, chip, k):
        block = shard_of(ph.buf, chip)
        return remote(block, block, ph.zs.at[k], ph.zr.at[k], across if k == 0 else near)

    def ag_send(ph):
        go(ag_z(ph, za, 0))
        go(ag_z(ph, za, 1))

    def ag_start(ph, value):
        ph.buf[rows_at(za * sh, sh), :] = value
        ag_send(ph)

    def ag_middle(ph):
        ag_z(ph, far_z, 0).wait_recv()
        go(ag_z(ph, far_z, 2))

    def ag_end(ph):
        ag_z(ph, near_z, 1).wait_recv()
        ag_z(ph, cross_z, 2).wait_recv()

    parts = range(z.parts)

    def part_at(part):
        return slice(part * z.part_rows, (part + 1) * z.part_rows)

    w_steps(2, head_part)
    w_end_own(0, head_part)
    attend(0)
    w_steps(head_part, head_part + LAG)
    w_end_other(0, head_part)
    attend(1)
    for i in parts:
        total = 0.0
        for index in sets:
            total = total + times(s.heads[index].o[part_at(i), :], weights[index].p[...])
        s.rs1[i].part[...] = total.astype(BF)
        rs_start(s.rs1[i])
    w_steps(head_part + LAG, head_part + LAG + 2)
    for i in parts:
        rs_middle(s.rs1[i])
        w_steps(head_part + LAG + 2 + i, head_part + LAG + 3 + i)

    def mine_at(part):
        return rows_at(part * z.part_rows + za * sh, sh)

    for i in parts:
        attn = rs_end(s.rs1[i])
        if i:
            w_steps(head_part + LAG + 4, head_part + LAG + 5)
        h1 = s.x[mine_at(i), :].astype(F32) + mod_line(2) * attn
        normed_m, _ = norm_parts(h1)
        ag_start(s.ag1[i], (normed_m * (1.0 + mod_line(4)) + mod_line(3)).astype(BF))
        s.attn[i] = attn
        s.h1[i] = h1
    w_steps(head_part + LAG + 5, half - 3)
    for i in parts:
        ag_middle(s.ag1[i])
        w_steps(half - 3 + i, half - 2 + i)
    w_end_own(head_part, thirds[1])
    w_end_other(head_part, thirds[1])

    def mlp_up(part):
        at = part_at(part)
        for index in sets:
            hid = s.hid[index]
            hidden = nt(s.ag1[part].buf[...], weights[index].up[...])
            square = hidden * hidden
            bend = jnp.tanh(GELU_C * hidden * (1.0 + GELU_K * square))
            hid.gact[at, :] = (0.5 * hidden * (1.0 + bend)).astype(BF)
            hid.slope[at, :] = 0.5 * (1.0 + bend) + 0.5 * hidden * (1.0 - bend * bend) * (
                GELU_C * (1.0 + 3.0 * GELU_K * square)
            )

    def mlp_back(part):
        at = part_at(part)
        total = 0.0
        for index in sets:
            hid = s.hid[index]
            dgact = nt(s.dmlp[at, :], weights[index].down[...])
            dz = (dgact * hid.slope[at, :]).astype(BF)
            hid.dz[at, :] = dz
            total = total + times(dz, weights[index].up[...])
        s.rs2[part].part[...] = total.astype(BF)

    def down(part):
        total = 0.0
        for index in sets:
            total = total + times(s.hid[index].gact[part_at(part), :], weights[index].down[...])
        s.rs4[part].part[...] = total.astype(BF)

    cols = 384

    def over_parts(left, gathered, at):
        total = 0.0
        for part in parts:
            total = total + tn(left[part_at(part), :], gathered[part].buf[:, at])
        return total.astype(BF)

    def tiles(body):
        loop(0, D // cols, lambda i: body(pl.ds(pl.multiple_of(i * cols, 128), cols)))

    def up_grad(index, target, first):
        def tile(at):
            target[first : first + fc, at] = over_parts(s.hid[index].dz, s.ag1, at)

        tiles(tile)

    def down_grad(index, target, first):
        def tile(at):
            grad = tn(s.hid[index].gact[...], s.dmlp[:, at])
            target[first + fc : first + 2 * fc, at] = grad.astype(BF)

        tiles(tile)

    first_one = -4 * hc
    for i in parts:
        ag_end(s.ag1[i])
        w_steps(half - 1 + i, half + i)
        mlp_up(i)
    down_grad(1, s.thin, 0)
    g_one(1, thirds[1], half, s.thin, first_one)
    w_steps(half + 1, half + LAG)
    w_end_own(thirds[1], half)
    w_end_other(thirds[1], half)
    g_two(thirds[1], half, s.thin, first_one)
    for i in parts:
        mlp_back(i)
        rs_start(s.rs2[i])
    up_grad(1, s.thin, 0)
    g_one(1, head_part, thirds[1], s.thin, first_one)
    down_grad(0, s.placed, 4 * hc)
    g_one(0, thirds[1], half, s.placed, 0)
    g_two_own(thirds[1], half)
    for i in parts:
        rs_middle(s.rs2[i])
    g_two(head_part, thirds[1], s.thin, first_one)
    g_steps(0, 2)
    up_grad(0, s.placed, 4 * hc)
    g_one(0, head_part, thirds[1], s.placed, 0)
    for i in parts:
        down(i)
    g_two_own(head_part, thirds[1])

    def norm_back_of(normed, inverse, upstream):
        return inverse * (
            upstream
            - jnp.mean(upstream, axis=-1, keepdims=True)
            - normed * jnp.mean(upstream * normed, axis=-1, keepdims=True)
        )

    def column_sum(values):
        return jnp.sum(values, axis=0, keepdims=True)

    def dy_of(part):
        return s.grad[mine_at(part), :].astype(F32) * (group_scale * live)

    for i in parts:
        rs_start(s.rs4[i])
    g_steps(2, 4)
    gate_a_sum = shift_m_sum = scale_m_sum = 0.0
    for i in parts:
        dw = rs_end(s.rs2[i])
        normed_m, inverse_m = norm_parts(s.h1[i])
        dh1 = dy_of(i) + norm_back_of(normed_m, inverse_m, dw * (1.0 + mod_line(4)))
        ag_start(s.ag2[i], (mod_line(2) * dh1).astype(BF))
        s.dh1[i] = dh1
        gate_a_sum = gate_a_sum + column_sum(dh1 * s.attn[i])
        shift_m_sum = shift_m_sum + column_sum(dw)
        scale_m_sum = scale_m_sum + column_sum(dw * normed_m)
    s.dmod[2:3, :] = gate_a_sum
    s.dmod[3:4, :] = shift_m_sum
    s.dmod[4:5, :] = scale_m_sum
    g_steps(4, 6)
    for i in parts:
        ag_middle(s.ag2[i])
        g_steps(6 + i, 7 + i)

    def attend_back(index):
        own, at = weights[index], s.heads[index]
        do = jnp.concatenate([nt(s.ag2[i].buf[...], own.p[...]) for i in parts], axis=0)
        do = do.astype(BF)
        q, k, v = at.q[...], at.k[...], at.v[...]
        dq = jnp.zeros((z.seq, hc), F32)
        dk = jnp.zeros((z.seq, hc), F32)
        dv = jnp.zeros((z.seq, hc), F32)
        for head in range(z.heads):
            p = s.soft[index * z.heads + head]
            do_head = only(do, head)
            dp_soft = nt(do_head, v)
            inner = jnp.sum(p * dp_soft, axis=-1, keepdims=True)
            ds = (p * (dp_soft - inner)).astype(BF)
            dq = dq + times(ds, only(k, head))
            dk = dk + tn(ds, only(q, head))
            dv = dv + tn(p.astype(BF), do_head)
        at.dq[...] = (dq * scale).astype(BF)
        at.dk[...] = (dk * scale).astype(BF)
        at.dv[...] = dv.astype(BF)

    def proj_grad(index, target):
        def tile(at):
            target[3 * hc : 4 * hc, at] = over_parts(s.heads[index].o, s.ag2, at)

        tiles(tile)

    def attn_grad(index, target):
        own = s.heads[index]

        def tile(at):
            mixed = s.u[:, at]
            target[0:hc, at] = tn(own.dq[...], mixed).astype(BF)
            target[hc : 2 * hc, at] = tn(own.dk[...], mixed).astype(BF)
            target[2 * hc : 3 * hc, at] = tn(own.dv[...], mixed).astype(BF)

        tiles(tile)

    for i in parts:
        ag_end(s.ag2[i])
        g_steps(8 + i, 9 + i)
    attend_back(1)
    proj_grad(1, s.extra)
    attn_grad(1, s.extra)
    g_one(1, 0, head_part, s.extra, 0)
    g_steps(10, 11)
    attend_back(0)
    g_two(0, head_part, s.extra, 0)
    for i in parts:
        total = 0.0
        for index in sets:
            own, at = weights[index], s.heads[index]
            rows = part_at(i)
            total = total + times(at.dq[rows, :], own.q[...])
            total = total + times(at.dk[rows, :], own.k[...])
            total = total + times(at.dv[rows, :], own.v[...])
        s.rs3[i].part[...] = total.astype(BF)
        rs_start(s.rs3[i])
    g_steps(11, 12)
    proj_grad(0, s.placed)
    attn_grad(0, s.placed)
    g_one(0, 0, head_part, s.placed, 0)
    for i in parts:
        rs_middle(s.rs4[i])
    g_two_own(0, head_part)
    g_steps(12, 14)
    for i in parts:
        rs_middle(s.rs3[i])
    g_steps(14, 15)

    def dsum_copy():
        return remote(s.dsum, s.dsum_in, s.dsum_s.at[0], s.dsum_r.at[0], xp)

    s.dsum[...] = jnp.zeros((8, 256), F32)
    s.dsum[0:1, 0:hc] = column_sum(s.heads[1].dq[...].astype(F32))
    s.dsum[1:2, 0:hc] = column_sum(s.heads[1].dv[...].astype(F32))
    go(dsum_copy())

    gate_m_sum = 0.0
    for i in parts:
        mlp_sum = rs_end(s.rs4[i])
        gate_m_sum = gate_m_sum + column_sum(dy_of(i) * mlp_sum)
        result = (s.h1[i] + mod_line(5) * mlp_sum) * live
        s.bo[i * sh : (i + 1) * sh, :] = result.astype(BF)
    s.dmod[5:6, :] = gate_m_sum

    def bo_copy():
        return remote(s.bo, s.bo_in, s.bo_s.at[0], s.bo_r.at[0], xp)

    go(bo_copy())
    g_steps(15, 16)
    shift_a_sum = scale_a_sum = 0.0
    for i in parts:
        du = rs_end(s.rs3[i])
        g_steps(16 + i, 17 + i)
        normed_a, inverse_a = norm_parts(s.x[mine_at(i), :].astype(F32))
        dx = s.dh1[i] + norm_back_of(normed_a, inverse_a, du * (1.0 + mod_line(1)))
        s.ag3[i].buf[rows_at(za * sh, sh), :] = dx.astype(BF)
        shift_a_sum = shift_a_sum + column_sum(du)
        scale_a_sum = scale_a_sum + column_sum(du * normed_a)
    s.dmod[0:1, :] = shift_a_sum
    s.dmod[1:2, :] = scale_a_sum
    s.dmod[6:8, :] = jnp.zeros((2, D), F32)

    dlines = [spread(s.dmod[i : i + 1, :]) for i in range(6)]
    for member in range(n_t):
        first = member * z.mod_rows
        line = jnp.zeros((8, D), F32)
        for piece in range(6):
            lower = max(first, piece * D) - first
            upper = min(first + z.mod_rows, (piece + 1) * D) - first
            if lower < upper:
                back = (piece * D - first) % D
                moved = pltpu.roll(dlines[piece], back, 1) if back else dlines[piece]
                line = jnp.where((lane >= lower) & (lane < upper), moved, line)
        for i in range(8):
            s.dmod_pack[member, i : i + 1, :] = line[0:1, 128 * i : 128 * (i + 1)]

    def dmod_copy(i):
        member = lax.rem(t + i, n_t)
        return remote(
            s.dmod_pack.at[member],
            s.dmod_recv.at[i - 1],
            s.dmod_s.at[i - 1],
            s.dmod_r.at[i - 1],
            (dp, member),
        )

    for i in range(1, n_t):
        go(dmod_copy(i))
    for i in parts:
        ag_send(s.ag3[i])
    for i in parts:
        ag_middle(s.ag3[i])
    dsum_copy().wait_recv()
    total = s.dmod_pack[t]
    for i in range(1, n_t):
        dmod_copy(i).wait_recv()
        total = total + s.dmod_recv[i - 1]
    s.vec[dp] = jnp.zeros((16, 256), F32)
    s.vec[dp, 0:8, 0:128] = total
    own_sums = (column_sum(s.heads[0].dq[...].astype(F32)), column_sum(s.heads[0].dv[...].astype(F32)))
    s.vec[dp, 8:9, 0:hc] = own_sums[0] + s.dsum_in[0:1, 0:hc]
    s.vec[dp, 9:10, 0:hc] = own_sums[1] + s.dsum_in[1:2, 0:hc]

    def vec_copy(i, group):
        return remote(
            s.vec.at[group],
            s.vec.at[group],
            s.vec_s.at[i - 1],
            s.vec_r.at[i - 1],
            (lax.rem(dp + i, n_dp), t),
        )

    for i in range(1, n_dp):
        go(vec_copy(i, dp))
    g_steps(half, half + LAG)
    for i in parts:
        ag_end(s.ag3[i])
    g_end(0, half)
    for i in range(1, n_dp):
        vec_copy(i, lax.rem(dp - i + n_dp, n_dp)).wait_recv()
    group_lines = []
    for group in range(n_dp):
        line = [unpack_rows(s.vec[group, 0:8, 0:128]), jnp.zeros((1, D - 1024), F32)]
        line = spread(jnp.concatenate(line, axis=1))
        for index in range(2):
            ends = [s.vec[group, 8 + index : 9 + index, :], jnp.zeros((1, D - 256), F32)]
            ends = spread(jnp.concatenate(ends, axis=1))
            line = line + pltpu.roll(ends, z.mod_rows + index * hc, 1)
        group_lines.append(line[0:1, :])
    group_lines.append(jnp.zeros((8 - n_dp, D), F32))
    s.table[...] = jnp.transpose(jnp.concatenate(group_lines, axis=0))
    bo_copy().wait_recv()
    for copy in pending:
        copy.wait_send()

    outs = [(s.g.fin, out_g), (s.table, out_table), (s.tok_all, out_tok)]
    outs += [(s.bo, out_bo.at[xb]), (s.bo_in, out_bo.at[1 - xb])]
    for i in parts:
        outs.append((s.ag3[i].buf, out_ig.at[pl.ds(i * z.part_rows, z.part_rows)]))
    stores = [
        pltpu.make_async_copy(src, dst, s.out_sem.at[i]) for i, (src, dst) in enumerate(outs)
    ]
    for store in stores:
        store.start()
    for store in stores:
        store.wait()


def update_kernel(
    z,
    group_slots,
    owners,
    grads_hbm,
    table,
    tokens,
    master,
    first,
    second,
    new_first,
    new_second,
    new_master,
    bos,
    grads,
    sem,
):
    step = pl.program_id(0)
    dp = lax.axis_index("dp")

    @pl.when(step == 0)
    def _():
        load = pltpu.make_async_copy(grads_hbm, grads, sem)
        load.start()

        def clear(slot, carry):
            bos[slot] = -1
            return carry

        lax.fori_loop(0, z.slots, clear, 0)

        def note(block, taken):
            mine = owners[block] == dp

            @pl.when(mine & (taken < z.slots))
            def _():
                bos[taken] = block

            return taken + mine.astype(jnp.int32)

        lax.fori_loop(0, z.blocks, note, jnp.int32(0))
        load.wait()

    rows = z.block_rows
    mod_blocks = z.mod_rows // rows
    head_blocks = z.head_cols // rows
    fix_one = 1.0 - beta_one**STEP
    fix_two = 1.0 - beta_two**STEP

    def put(i, grad):
        weight = master[i]
        one = beta_one * first[i] + (1.0 - beta_one) * grad
        two = beta_two * second[i] + (1.0 - beta_two) * grad * grad
        new_first[i] = one
        new_second[i] = two
        spread = two * (1.0 / fix_two)
        root = spread * lax.rsqrt(spread)
        move = one * (learn_rate / fix_one) * pltpu.reciprocal(root + eps_adam)
        new_master[i] = weight * (1.0 - learn_rate * decay_rate) - move

    def slot(i, carry):
        block = bos[step * group_slots + i]
        is_mod = block < mod_blocks
        is_time = (block >= mod_blocks + 3 * head_blocks) & (block < mod_blocks + 5 * head_blocks)

        @pl.when(block < 0)
        def _():
            new_first[i] = jnp.zeros((rows, D), F32)
            new_second[i] = jnp.zeros((rows, D), F32)
            new_master[i] = jnp.zeros((rows, D), F32)

        @pl.when((block >= 0) & (is_mod | is_time))
        def _():
            index = jnp.where(is_mod, block, block - 3 * head_blocks)
            columns = table[pl.ds(pl.multiple_of(index * rows, 8), rows), :]
            grad = columns[:, 0:1] * tokens[0:1, :].astype(F32)
            for group in range(1, z.dp_count):
                grad = grad + columns[:, group : group + 1] * tokens[
                    16 * group : 16 * group + 1, :
                ].astype(F32)
            put(i, grad)

        is_wide = (block >= 0) & jnp.logical_not(is_mod | is_time)
        index = jnp.where(
            block < mod_blocks + 3 * head_blocks,
            block - mod_blocks,
            block - mod_blocks - 2 * head_blocks,
        )
        pair = jnp.clip(index, 0, z.wide // rows - 1) // 2 * PAIR

        @pl.when(is_wide & (lax.rem(index, 2) == 0))
        def _():
            put(i, grads[rows_at(pair, 32), :].astype(F32)[:rows])

        @pl.when(is_wide & (lax.rem(index, 2) == 1))
        def _():
            put(i, grads[rows_at(pair + 16, 32), :].astype(F32)[8:])

        return carry

    lax.fori_loop(0, group_slots, slot, 0)


def per_device_fast(
    z,
    inputs,
    out_grad,
    bucket,
    counts,
    images_held,
    owners,
    master_weight,
    first_moment,
    second_moment,
):
    token = jnp.broadcast_to(time_token(bucket[0]).astype(BF)[None, :], (16, D))
    plan = scratch_plan(z)
    smem = pl.BlockSpec(memory_space=pltpu.SMEM)
    vmem = pl.BlockSpec(memory_space=pltpu.VMEM)
    hbm = pl.BlockSpec(memory_space=pl.ANY)
    flops = 12 * z.seq * D * z.wide
    bo, own, grads, table, tokens = pl.pallas_call(
        partial(layer_kernel, z, plan),
        out_shape=(
            jax.ShapeDtypeStruct((2, z.parts * z.shard, D), BF),
            jax.ShapeDtypeStruct((z.seq, D), BF),
            jax.ShapeDtypeStruct((z.wide, D), BF),
            jax.ShapeDtypeStruct((z.thin, 8), F32),
            jax.ShapeDtypeStruct((16 * z.dp_count, D), BF),
        ),
        in_specs=[smem, smem, smem, vmem, hbm, hbm, hbm],
        out_specs=(hbm,) * 5,
        scratch_shapes=flatten(plan),
        compiler_params=pltpu.CompilerParams(
            collective_id=0, has_side_effects=True, vmem_limit_bytes=62 * 2**20
        ),
        cost_estimate=pl.CostEstimate(
            flops=flops, bytes_accessed=20 * 2**20, transcendentals=2 * z.seq * z.ffn_cols
        ),
        name="layer",
    )(
        owners,
        counts,
        images_held,
        token,
        inputs,
        out_grad,
        master_weight,
    )
    def partner(value, bits):
        swap = [(member, member ^ bits) for member in range(z.tensor_count)]
        return lax.ppermute(value, axes[1], swap)

    shards = [bo] + [partner(bo, 2 * step) for step in range(1, 4)]
    other = partner(own, 1)
    group_slots = next(size for size in (15, 12, 10, 8, 6, 5, 4, 3, 2, 1) if z.slots % size == 0)
    block = pl.BlockSpec((group_slots, z.block_rows, D), lambda i: (i, 0, 0))
    state = jax.ShapeDtypeStruct(master_weight.shape, F32)
    new_first, new_second, new_master = pl.pallas_call(
        partial(update_kernel, z, group_slots),
        grid=(z.slots // group_slots,),
        out_shape=(state,) * 3,
        in_specs=[smem, hbm, vmem, vmem, block, block, block],
        out_specs=(block,) * 3,
        scratch_shapes=[
            pltpu.SMEM((z.slots,), jnp.int32),
            pltpu.VMEM((z.wide, D), BF),
            pltpu.SemaphoreType.DMA,
        ],
        compiler_params=pltpu.CompilerParams(vmem_limit_bytes=60 * 2**20),
        cost_estimate=pl.CostEstimate(
            flops=20 * master_weight.size,
            bytes_accessed=24 * master_weight.size,
            transcendentals=2 * master_weight.size,
        ),
        name="update",
    )(owners, grads, table, tokens, master_weight, first_moment, second_moment)
    place = lax.axis_index(axes[1])
    even = lax.rem(place, 2) == 0
    for bit in (1, 2):
        swapped = lax.rem(place // (2 * bit), 2) == 1
        shards = [jnp.where(swapped, shards[step ^ bit], shards[step]) for step in range(4)]
    split = (z.images, z.parts, 1, z.shard, D)
    block_output = jnp.concatenate([shard.reshape(split) for shard in shards], axis=2)
    input_grad = jnp.stack([jnp.where(even, own, other), jnp.where(even, other, own)])
    return (
        block_output.reshape(inputs.shape),
        input_grad.astype(F32),
        new_first,
        new_second,
        new_master,
    )


def per_device(inputs, out_grad, bucket, counts, images_held, owners, master, first, second):
    sizes = Sizes(
        lax.axis_size("dp"),
        lax.axis_size("tensor"),
        master.shape[0],
        master.shape[1],
        inputs.shape[0],
        inputs.shape[1],
    )
    run = partial(per_device_fast, sizes) if sizes.fits() else per_device_plain
    return run(inputs, out_grad, bucket, counts, images_held, owners, master, first, second)


def solution(mesh):
    return jax.shard_map(
        per_device,
        mesh=mesh,
        in_specs=(
            P("dp", None, None),
            P("dp", None, None),
            P("dp"),
            P(),
            P("dp"),
            P(),
            P("dp", "tensor", None),
            P("dp", "tensor", None),
            P("dp", "tensor", None),
        ),
        out_specs=(
            P("dp", None, None),
            P("dp", None, None),
            P("dp", "tensor", None),
            P("dp", "tensor", None),
            P("dp", "tensor", None),
        ),
        check_vma=False,
    )
```
